32 devices in a mesh: depth: 16 (over z, y, core), freq: 2 (over x).
Axes of the slice: x: 2, y: 2, z: 4, core: 2. Of those that a mesh axis runs over, the one named last changes fastest.
Arguments:
- extrapolation_operator: float32 [2, 16, 2, 512, 512], P('freq', 'depth'), may hold values from -0.1875 to 0.1875
- impedance_contrast: float32 [16, 512], P('depth'), may hold values from -3 to 3
- ascending_residual: float32 [2, 16, 5, 2, 96, 512], P('freq', 'depth'), may hold values from -6 to 6
- arriving_downward_matrices: float32 [2, 16, 2, 96, 512], P('freq', 'depth'), may hold values from -6 to 6
- shot_node_indices: int32 [4, 96], replicated, may hold values from 0 to 511
- emitted_pulse: float32 [2, 4, 2], P('freq'), may hold values from -4 to 4
Outputs:
- departing_downward_matrices: float32 [2, 16, 2, 96, 512], P('freq', 'depth')
- gradient: float32 [16, 512], P('depth', 'freq')
The draws below stay inside these ranges and needn't reach their ends.
All inputs are finite; a program needn't handle non-finite values.
Results may differ from the reference program's by a relative error of at most 0.00013.
Values sent between devices are 32-bit elements; how exact they have to be, the bound alone decides.
No kernel may reach another device: no remote copies, remote signals or barrier semaphores. Data moves between devices by JAX's collectives and lax.ppermute only.
A program may use at most 64 MiB of HBM per device.

```python
import math
import jax
import jax.numpy as jnp
from jax import lax

HORIZONTAL_NODES = 512
SHOT_NUMBER = 96
TICKS = 5
STRATUM_NUMBER = 16
TEMPORAL_RATES = 2


def plant(drawn, stream_key, smallest, largest):
    longest = drawn.shape.index(max(drawn.shape))
    spots = []
    for shift in (0, 1):
        where = [jax.random.randint(jax.random.fold_in(stream_key, axis), (), 0, length) for axis, length in enumerate(drawn.shape)]
        where[longest] = (where[longest] + shift) % drawn.shape[longest]
        spots.append(tuple(where))
    return drawn.at[spots[0]].set(smallest).at[spots[1]].set(largest)


def steps_of(key, extent, split, smallest, high):
    factor_of = 1.0
    for position, shards_of in split:
        draws = jax.random.uniform(jax.random.fold_in(jax.random.fold_in(key, 6), position), (shards_of,), jnp.float32, smallest / len(split), high / len(split))
        factor_of = factor_of * jnp.repeat(jnp.exp(draws), extent[position] // shards_of).reshape((-1,) + (1,) * (len(extent) - 1 - position))
    return factor_of


def bell_draw(stream_key, dims, scale, limit, shards=(), kind=jnp.bfloat16):
    array = scale * jax.random.normal(stream_key, dims, jnp.float32)
    if shards:
        array = array * steps_of(stream_key, dims, shards, -0.22, 0.18)
    return jnp.clip(array, -limit, limit).astype(kind)


def setup_inputs(seed: int = 0) -> dict:
    key_of = jax.random.split(jax.random.key(seed), 7)
    return {
        "extrapolation_operator": bell_draw(key_of[0], (TEMPORAL_RATES, STRATUM_NUMBER, 2, HORIZONTAL_NODES, HORIZONTAL_NODES), (2 * HORIZONTAL_NODES) ** -0.5, 0.1875, ((0, 2), (1, 16)), jnp.float32),
        "impedance_contrast": bell_draw(key_of[1], (STRATUM_NUMBER, HORIZONTAL_NODES), 0.5, 3.0, ((0, 16),), jnp.float32),
        "ascending_residual": bell_draw(key_of[2], (TEMPORAL_RATES, STRATUM_NUMBER, TICKS, 2, SHOT_NUMBER, HORIZONTAL_NODES), 1.0, 6.0, ((0, 2), (1, 16)), jnp.float32),
        "arriving_downward_matrices": bell_draw(key_of[3], (TEMPORAL_RATES, STRATUM_NUMBER, 2, SHOT_NUMBER, HORIZONTAL_NODES), 1.0, 6.0, ((0, 2), (1, 16)), jnp.float32),
        "shot_node_indices": plant(jax.random.randint(key_of[4], (TICKS - 1, SHOT_NUMBER), 0, HORIZONTAL_NODES), jax.random.fold_in(key_of[4], 1), 0, HORIZONTAL_NODES - 1).astype(jnp.int32),
        "emitted_pulse": bell_draw(key_of[5], (TEMPORAL_RATES, TICKS - 1, 2), 1.0, 4.0, ((0, 2),), jnp.float32),
    }


def complex_step(mixed, prop_parts):
    highest = lax.Precision.HIGHEST

    def product(left, right):
        return jnp.einsum('zsy,zyx->zsx', left, right, precision=highest)
    real_out = product(mixed[:, 0], prop_parts[:, 0]) - product(mixed[:, 1], prop_parts[:, 1])
    imag_out = product(mixed[:, 0], prop_parts[:, 1]) + product(mixed[:, 1], prop_parts[:, 0])
    return jnp.stack([real_out, imag_out], 1)

def inject_panel(wave_pair, source_sites):
    columns = jnp.arange(HORIZONTAL_NODES, dtype=jnp.int32)
    hits = (columns[None, :] == source_sites[:, None].astype(jnp.int32)).astype(jnp.float32)
    return wave_pair[:, None, None] * hits[None]

def reference(extrapolation_operator, impedance_contrast, ascending_residual, arriving_downward_matrices, shot_node_indices, emitted_pulse):

    def chosen_temporal_rate(operand_list):
        propagator_field, upgoing_field, transit_field, wavelet_spectrum = operand_list
        present_shot_matrix = transit_field
        gradient_sum = jnp.zeros((STRATUM_NUMBER, HORIZONTAL_NODES), jnp.float32)
        outgoing = present_shot_matrix
        for moment in range(TICKS):
            wave_now = upgoing_field[:, moment]
            gradient_sum = gradient_sum + lax.optimization_barrier(jnp.sum(present_shot_matrix * wave_now, axis=(1, 2)))
            mixed = present_shot_matrix + impedance_contrast[:, None, None, :] * wave_now
            outgoing = complex_step(mixed, propagator_field)
            if moment < TICKS - 1:
                top_panel = inject_panel(wavelet_spectrum[moment], shot_node_indices[moment])
                present_shot_matrix = jnp.concatenate([top_panel[None], outgoing[:-1]], 0)
        return (outgoing, gradient_sum / math.sqrt(SHOT_NUMBER * TICKS))
    departing_downward_matrices, reflector_sensitivity_shares = lax.map(chosen_temporal_rate, (extrapolation_operator, ascending_residual, arriving_downward_matrices, emitted_pulse))
    return (departing_downward_matrices, lax.optimization_barrier(jnp.sum(reflector_sensitivity_shares, 0)))
```

```python
import math

import jax
import jax.numpy as jnp
from jax import lax
from jax.sharding import PartitionSpec as P

TICKS = 5


def product(left, right):
    return jnp.dot(left, right, precision=lax.Precision.HIGH, preferred_element_type=jnp.float32)


def after(value, *earlier):
    return lax.optimization_barrier((value,) + earlier)[0]


def sum_over(vector, axis):
    count = lax.axis_size(axis)
    me = lax.axis_index(axis)
    chunks = vector.reshape(count, -1)
    total = lax.dynamic_index_in_dim(chunks, me, 0, keepdims=True)
    for distance in range(1, count):
        chunk = lax.dynamic_index_in_dim(chunks, (me + distance) % count, 0, keepdims=True)
        route = [(i, (i + distance) % count) for i in range(count)]
        total = total + lax.ppermute(chunk, axis, route)
    return total


def local(
    extrapolation_operator,
    impedance_contrast,
    ascending_residual,
    arriving_downward_matrices,
    shot_node_indices,
    emitted_pulse,
):
    prop_real = extrapolation_operator[0, 0, 0]
    prop_imag = extrapolation_operator[0, 0, 1]
    prop_both = prop_real + prop_imag
    reflect = impedance_contrast[0]
    shots, breadth = arriving_downward_matrices.shape[3:]
    residual = ascending_residual[0, 0]
    levels = lax.axis_size("depth")
    at_surface = lax.axis_index("depth") == 0
    columns = jnp.arange(breadth, dtype=jnp.int32)
    fast_route = [(i, i + 1) for i in range(0, levels - 1, 2)]
    slow_route = [(i, i + 1) for i in range(1, levels - 1, 2)]
    terms = []

    def injected(tick):
        hits = (columns[None, :] == shot_node_indices[tick - 1][:, None]).astype(jnp.float32)
        return emitted_pulse[0, tick - 1][:, None, None] * hits[None]

    def work(arriving, tick):
        wave = residual[tick]
        terms.append(jnp.sum(arriving * wave, axis=(0, 1)))
        mixed = arriving + reflect[None, None, :] * wave
        first = product(mixed[0], prop_real)
        second = product(mixed[1], prop_imag)
        third = product(mixed[0] + mixed[1], prop_both)
        return jnp.stack([first - second, third - first - second], 0)

    def fast(panel):
        return lax.ppermute(panel, "depth", fast_route)

    def slow(panel, tick):
        got = lax.ppermute(panel, "depth", slow_route)
        return jnp.where(at_surface, injected(tick), got)

    out0 = work(arriving_downward_matrices[0, 0], 0)
    f0 = fast(out0)
    s0 = slow(out0, 1)
    odd1 = work(f0, 1)
    s1 = slow(odd1, 2)
    even1 = work(after(s0, odd1), 1)
    f1 = fast(even1)
    odd2 = work(f1, 2)
    s2 = slow(odd2, 3)
    even2 = work(after(s1, odd2), 2)
    f2 = fast(even2)
    odd3 = work(f2, 3)
    s3 = slow(odd3, 4)
    even3 = work(after(s2, odd3), 3)
    f3 = fast(even3)
    out4 = work(s3 + f3, 4)

    scale = 1.0 / math.sqrt(shots * TICKS)
    gradient = sum(terms[1:], terms[0]) * scale
    return (out4[None, None], sum_over(gradient, "freq"))


def solution(mesh):
    placed = (
        P("freq", "depth", None, None, None),
        P("depth", None),
        P("freq", "depth", None, None, None, None),
        P("freq", "depth", None, None, None),
        P(),
        P("freq", None, None),
    )
    return jax.shard_map(
        local,
        mesh=mesh,
        in_specs=placed,
        out_specs=(P("freq", "depth", None, None, None), P("depth", "freq")),
        check_vma=False,
    )
```

```python
import math

import jax
import jax.numpy as jnp
from jax import lax
from jax.sharding import PartitionSpec as P

TICKS = 5


def product(left, right):
    return jnp.dot(left, right, precision=lax.Precision.HIGH, preferred_element_type=jnp.float32)


def after(value, *earlier):
    return lax.optimization_barrier((value,) + earlier)[0]


def sum_over(vector, axis):
    count = lax.axis_size(axis)
    me = lax.axis_index(axis)
    chunks = vector.reshape(count, -1)
    total = lax.dynamic_index_in_dim(chunks, me, 0, keepdims=True)
    for distance in range(1, count):
        chunk = lax.dynamic_index_in_dim(chunks, (me + distance) % count, 0, keepdims=True)
        route = [(i, (i + distance) % count) for i in range(count)]
        total = total + lax.ppermute(chunk, axis, route)
    return total


def local(
    extrapolation_operator,
    impedance_contrast,
    ascending_residual,
    arriving_downward_matrices,
    shot_node_indices,
    emitted_pulse,
):
    prop_real = extrapolation_operator[0, 0, 0]
    prop_imag = extrapolation_operator[0, 0, 1]
    prop_both = prop_real + prop_imag
    reflect = impedance_contrast[0]
    shots, breadth = arriving_downward_matrices.shape[3:]
    residual = ascending_residual[0, 0]
    levels = lax.axis_size("depth")
    at_surface = lax.axis_index("depth") == 0
    columns = jnp.arange(breadth, dtype=jnp.int32)
    odd = lax.axis_index("depth") % 2 == 1
    fast_route = [(i, i ^ 1) for i in range(levels)]
    slow_route = [(i, (i + 1) % levels) for i in range(levels)]
    terms = []

    def injected(tick):
        hits = (columns[None, :] == shot_node_indices[tick - 1][:, None]).astype(jnp.float32)
        return emitted_pulse[0, tick - 1][:, None, None] * hits[None]

    def work(arriving, tick):
        wave = residual[tick]
        terms.append(jnp.sum(arriving * wave, axis=(0, 1)))
        mixed = arriving + reflect[None, None, :] * wave
        first = product(mixed[0], prop_real)
        second = product(mixed[1], prop_imag)
        third = product(mixed[0] + mixed[1], prop_both)
        return jnp.stack([first - second, third - first - second], 0)

    def fast(panel):
        got = lax.ppermute(panel, "depth", fast_route)
        return jnp.where(odd, got, 0.0)

    def slow(panel, tick):
        got = lax.ppermute(panel, "depth", slow_route)
        return jnp.where(odd, 0.0, jnp.where(at_surface, injected(tick), got))

    out0 = work(arriving_downward_matrices[0, 0], 0)
    f0 = fast(out0)
    s0 = slow(out0, 1)
    odd1 = work(f0, 1)
    s1 = slow(odd1, 2)
    even1 = work(after(s0, odd1), 1)
    f1 = fast(even1)
    odd2 = work(f1, 2)
    s2 = slow(odd2, 3)
    even2 = work(after(s1, odd2), 2)
    f2 = fast(even2)
    odd3 = work(f2, 3)
    s3 = slow(odd3, 4)
    even3 = work(after(s2, odd3), 3)
    f3 = fast(even3)
    out4 = work(s3 + f3, 4)

    scale = 1.0 / math.sqrt(shots * TICKS)
    gradient = sum(terms[1:], terms[0]) * scale
    return (out4[None, None], sum_over(gradient, "freq"))


def solution(mesh):
    placed = (
        P("freq", "depth", None, None, None),
        P("depth", None),
        P("freq", "depth", None, None, None, None),
        P("freq", "depth", None, None, None),
        P(),
        P("freq", None, None),
    )
    return jax.shard_map(
        local,
        mesh=mesh,
        in_specs=placed,
        out_specs=(P("freq", "depth", None, None, None), P("depth", "freq")),
        check_vma=False,
    )
```

```python
import functools
import math

import jax
import jax.numpy as jnp
from jax import lax
from jax.experimental import pallas as pl
from jax.experimental.pallas import tpu as pltpu
from jax.sharding import PartitionSpec as P

TICKS = 5
VMEM_LIMIT = 24 * 1024 * 1024
QUICK = pl.CostEstimate(flops=1, bytes_accessed=1, transcendentals=0)


def pinned(value):
    return pltpu.with_memory_space_constraint(value, pltpu.VMEM)


def in_vmem():
    return pl.BlockSpec(memory_space=pltpu.VMEM)


def is_odd():
    return lax.axis_index("depth") % 2 == 1


def split(value):
    high = value.astype(jnp.bfloat16)
    low = (value - high.astype(jnp.float32)).astype(jnp.bfloat16)
    return high, low


def fold(product):
    rows = product.shape[0] * product.shape[1]
    return jnp.sum(product.reshape(rows // 8, 8, product.shape[2]), axis=0)


def load_left(mixed, left):
    shots = mixed.shape[1]
    for part in range(2):
        high, low = split(mixed[part])
        left[pl.ds(part * shots, shots), :] = high
        left[pl.ds((2 + part) * shots, shots), :] = low


def multiply(left, high, low, out):
    shots = out.shape[1]
    dot = functools.partial(jnp.dot, preferred_element_type=jnp.float32)

    def by(part):
        big = dot(left[...], high[part])
        small = dot(left[pl.ds(0, 2 * shots), :], low[part])
        real = big[:shots] + (big[2 * shots : 3 * shots] + small[:shots])
        imag = big[shots : 2 * shots] + (big[3 * shots :] + small[shots:])
        return real, imag

    real_real, imag_real = by(0)
    real_imag, imag_imag = by(1)
    out[0] = real_real - imag_imag
    out[1] = real_imag + imag_real


def injected(tick, sites, pulse, shape):
    shots, breadth = shape
    row = lax.broadcasted_iota(jnp.int32, (shots, shots), 0)
    column = lax.broadcasted_iota(jnp.int32, (shots, shots), 1)
    spread = jnp.broadcast_to(sites[pl.ds(tick - 1, 1), :], (shots, shots)).astype(jnp.float32)
    site = jnp.sum(jnp.where(row == column, spread, 0.0), axis=1, keepdims=True)
    lanes = lax.broadcasted_iota(jnp.int32, (shots, breadth), 1).astype(jnp.float32)
    hit = lanes == site
    return [jnp.where(hit, pulse[part, tick - 1], 0.0) for part in range(2)]


def first_kernel(parity, chained, *refs):
    if chained:
        refs = refs[:4] + refs[8:]
    operator, contrast, residual, panel = refs[:4]
    out, high, low, grad = refs[4:8]
    whole, wave, arrived, left, sems = refs[8:]

    @pl.when(is_odd() if parity else jnp.logical_not(is_odd()))
    def _():
        copies = [
            pltpu.make_async_copy(residual.at[0, 0, 0], wave, sems.at[0]),
            pltpu.make_async_copy(panel.at[0, 0], arrived, sems.at[1]),
            pltpu.make_async_copy(operator.at[0, 0, 0], whole.at[0], sems.at[2]),
            pltpu.make_async_copy(operator.at[0, 0, 1], whole.at[1], sems.at[3]),
        ]
        for copy in copies:
            copy.start()
        copies[0].wait()
        copies[1].wait()
        grad[...] = fold(arrived[...] * wave[...])
        load_left(arrived[...] + contrast[...][None] * wave[...], left)
        for part in range(2):
            copies[2 + part].wait()
            high[part], low[part] = split(whole[part])
        multiply(left, high, low, out)


def first(parity, operator, contrast, residual, panel, carried):
    shots, breadth = panel.shape[3:]
    any_ref = pl.BlockSpec(memory_space=pl.ANY)
    half = pltpu.VMEM((2, breadth, breadth), jnp.bfloat16)
    carried = [pinned(value) for value in carried]
    out = pl.pallas_call(
        functools.partial(first_kernel, parity, bool(carried)),
        out_shape=(
            pltpu.VMEM((2, shots, breadth), jnp.float32),
            half,
            half,
            pltpu.VMEM((8, breadth), jnp.float32),
        ),
        in_specs=[any_ref, in_vmem(), any_ref, any_ref] + [in_vmem()] * len(carried),
        out_specs=(in_vmem(),) * 4,
        scratch_shapes=[
            pltpu.VMEM((2, breadth, breadth), jnp.float32),
            pltpu.VMEM((2, shots, breadth), jnp.float32),
            pltpu.VMEM((2, shots, breadth), jnp.float32),
            pltpu.VMEM((4 * shots, breadth), jnp.bfloat16),
            pltpu.SemaphoreType.DMA((4,)),
        ],
        input_output_aliases={4 + i: i for i in range(len(carried))},
        compiler_params=pltpu.CompilerParams(vmem_limit_bytes=VMEM_LIMIT),
        cost_estimate=QUICK,
    )(operator, contrast, residual, panel, *carried)
    return out


def arrive(tick, arrived, residual, contrast, sites, pulse, grad_in, grad, left, odd_side):
    def take(panel):
        wave = residual[0, 0, tick]
        if grad is not None:
            grad[...] = grad_in[...] + fold(panel * wave)
        if left is not None:
            load_left(panel + contrast[...][None] * wave, left)

    if odd_side:
        take(arrived[...])
        return
    surface = lax.axis_index("depth") == 0

    @pl.when(surface)
    def _():
        take(jnp.stack(injected(tick, sites, pulse, arrived.shape[1:]), 0))

    @pl.when(jnp.logical_not(surface))
    def _():
        take(arrived[...])


def step_kernel(tick, parity, arrived, residual, contrast, sites, pulse, high, low, grad_in, out, grad, left):
    @pl.when(is_odd() if parity else jnp.logical_not(is_odd()))
    def _():
        arrive(tick, arrived, residual, contrast, sites, pulse, grad_in, grad, left, parity)
        multiply(left, high, low, out)


def step(tick, parity, arrived, shared, high, low, grad):
    shots, breadth = arrived.shape[1:]
    residual, contrast, sites, pulse = shared
    return pl.pallas_call(
        functools.partial(step_kernel, tick, parity),
        out_shape=(
            pltpu.VMEM((2, shots, breadth), jnp.float32),
            pltpu.VMEM(grad.shape, jnp.float32),
        ),
        in_specs=[in_vmem()] * 4 + [pl.BlockSpec(memory_space=pltpu.SMEM)] + [in_vmem()] * 3,
        out_specs=(in_vmem(),) * 2,
        scratch_shapes=[pltpu.VMEM((4 * shots, breadth), jnp.bfloat16)],
        input_output_aliases={7: 1},
        compiler_params=pltpu.CompilerParams(vmem_limit_bytes=VMEM_LIMIT),
        cost_estimate=QUICK,
    )(pinned(arrived), residual, contrast, sites, pulse, pinned(high), pinned(low), pinned(grad))


def gradient_kernel(count, scale, from_above, from_mate, residual, contrast, sites, pulse, grad_in, chunks, total):
    tick = TICKS - 1
    rest = (residual, contrast, sites, pulse, grad_in, total, None)

    @pl.when(is_odd())
    def _():
        arrive(tick, from_mate, *rest, True)

    @pl.when(jnp.logical_not(is_odd()))
    def _():
        arrive(tick, from_above, *rest, False)

    gradient = jnp.sum(total[...], axis=0, keepdims=True) * scale
    width = gradient.shape[1] // count
    me = lax.axis_index("freq")
    for distance in range(count):
        owner = lax.rem(me + distance, count)
        chunk = jnp.zeros((1, width), jnp.float32)
        for place in range(count):
            piece = gradient[:, place * width : (place + 1) * width]
            chunk = jnp.where(owner == place, piece, chunk)
        chunks[distance][...] = chunk


def gradient_chunks(from_above, from_mate, shared, grad):
    shots, breadth = from_above.shape[1:]
    residual, contrast, sites, pulse = shared
    count = lax.axis_size("freq")

    def body(*refs):
        gradient_kernel(count, 1.0 / math.sqrt(shots * TICKS), *refs[:7], refs[7 : 7 + count], refs[7 + count])

    return pl.pallas_call(
        body,
        out_shape=(pltpu.VMEM((1, breadth // count), jnp.float32),) * count,
        in_specs=[in_vmem()] * 5 + [pl.BlockSpec(memory_space=pltpu.SMEM)] + [in_vmem()],
        out_specs=(in_vmem(),) * count,
        scratch_shapes=[pltpu.VMEM(grad.shape, jnp.float32)],
        compiler_params=pltpu.CompilerParams(vmem_limit_bytes=VMEM_LIMIT),
        cost_estimate=QUICK,
    )(pinned(from_above), pinned(from_mate), residual, contrast, sites, pulse, pinned(grad))


def last_kernel(from_above, from_mate, residual, contrast, sites, pulse, high, low, out, left):
    tick = TICKS - 1
    rest = (residual, contrast, sites, pulse, None, None, left)

    @pl.when(is_odd())
    def _():
        arrive(tick, from_mate, *rest, True)

    @pl.when(jnp.logical_not(is_odd()))
    def _():
        arrive(tick, from_above, *rest, False)

    multiply(left, high, low, out)


def last(from_above, from_mate, shared, high, low):
    shots, breadth = from_above.shape[1:]
    residual, contrast, sites, pulse = shared
    return pl.pallas_call(
        last_kernel,
        out_shape=jax.ShapeDtypeStruct((2, shots, breadth), jnp.float32),
        in_specs=[in_vmem()] * 5 + [pl.BlockSpec(memory_space=pltpu.SMEM)] + [in_vmem()] * 2,
        out_specs=in_vmem(),
        scratch_shapes=[pltpu.VMEM((4 * shots, breadth), jnp.bfloat16)],
        compiler_params=pltpu.CompilerParams(vmem_limit_bytes=VMEM_LIMIT),
        cost_estimate=QUICK,
    )(pinned(from_above), pinned(from_mate), residual, contrast, sites, pulse, pinned(high), pinned(low))


def cross_route(levels):
    route = {level: level + 1 for level in range(levels - 1)}
    chips = levels // 2
    route[levels - 1] = 0
    if chips % 2 == 0 and chips > 2:
        route[levels - 1] = levels - 3
        for chip in range(chips - 2, 2, -2):
            route[2 * chip] = 2 * (chip - 2) + 1
        route[4] = 0
    return sorted(route.items())


def local(
    extrapolation_operator,
    impedance_contrast,
    ascending_residual,
    arriving_downward_matrices,
    shot_node_indices,
    emitted_pulse,
):
    levels = lax.axis_size("depth")
    mate_route = [(level, level ^ 1) for level in range(levels)]
    down_route = cross_route(levels)
    freqs = lax.axis_size("freq")
    shared = (
        pinned(ascending_residual),
        impedance_contrast,
        shot_node_indices,
        emitted_pulse[0].T,
    )

    def mate(panel):
        return lax.ppermute(panel, "depth", mate_route)

    def down(panel):
        return lax.ppermute(panel, "depth", down_route)

    start = (extrapolation_operator, impedance_contrast, ascending_residual, arriving_downward_matrices)
    odd, *carried = first(1, *start, ())
    from_above = down(odd)
    even, high, low, grad = first(0, *start, (odd, *carried))
    from_mate = mate(even)
    for tick in range(1, TICKS):
        if tick == TICKS - 1:
            chunks = gradient_chunks(from_above, from_mate, shared, grad)
            out = last(from_above, from_mate, shared, high, low)
            break
        odd, grad = step(tick, 1, from_mate, shared, high, low, grad)
        later = down(odd)
        even, grad = step(tick, 0, from_above, shared, high, low, grad)
        from_mate = mate(even)
        from_above = later

    gradient = chunks[0]
    for distance in range(1, freqs):
        route = [(i, (i + distance) % freqs) for i in range(freqs)]
        gradient = gradient + lax.ppermute(chunks[distance], "freq", route)
    return (out[None, None], gradient)


def solution(mesh):
    placed = (
        P("freq", "depth", None, None, None),
        P("depth", None),
        P("freq", "depth", None, None, None, None),
        P("freq", "depth", None, None, None),
        P(),
        P("freq", None, None),
    )
    return jax.shard_map(
        local,
        mesh=mesh,
        in_specs=placed,
        out_specs=(P("freq", "depth", None, None, None), P("depth", "freq")),
        check_vma=False,
    )
```

```python
import functools
import math

import jax
import jax.numpy as jnp
from jax import lax
from jax.experimental import pallas as pl
from jax.experimental.pallas import tpu as pltpu
from jax.sharding import PartitionSpec as P

TICKS = 5
VMEM_LIMIT = 24 * 1024 * 1024
QUICK = pl.CostEstimate(flops=1, bytes_accessed=1, transcendentals=0)
LONGER = pl.CostEstimate(flops=500000000, bytes_accessed=1, transcendentals=0)
PARAMS = pltpu.CompilerParams(vmem_limit_bytes=VMEM_LIMIT)


def pinned(value):
    return pltpu.with_memory_space_constraint(value, pltpu.VMEM)


def kept(value):
    return pltpu.with_memory_space_constraint(value, pltpu.HBM)


IN_VMEM = pl.BlockSpec(memory_space=pltpu.VMEM)
IN_HBM = pl.BlockSpec(memory_space=pltpu.HBM)


def is_odd():
    return lax.axis_index("depth") % 2 == 1


def split(value):
    high = value.astype(jnp.bfloat16)
    low = (value - high.astype(jnp.float32)).astype(jnp.bfloat16)
    return high, low


def fold(product):
    return jnp.sum(product.reshape(-1, 8, product.shape[1]), axis=0)


def take(pair, waves, contrast, grad_in, grad, left):
    if grad is not None:
        term = fold(pair[0] * waves[0]) + fold(pair[1] * waves[1])
        grad[...] = term if grad_in is None else grad_in[...] + term
    if left is not None:
        shots = pair[0].shape[0]
        for part in range(2):
            high, low = split(pair[part] + contrast[...] * waves[part])
            left[pl.ds(part * shots, shots), :] = high
            left[pl.ds((2 + part) * shots, shots), :] = low


def multiply(left, high, low, columns):
    shots = left.shape[0] // 4
    dot = functools.partial(jnp.dot, preferred_element_type=jnp.float32)

    def by(part):
        big = dot(left[...], high[part, :, columns])
        small = dot(left[pl.ds(0, 2 * shots), :], low[part, :, columns])
        real = big[:shots] + (big[2 * shots : 3 * shots] + small[:shots])
        imag = big[shots : 2 * shots] + (big[3 * shots :] + small[shots:])
        return real, imag

    real_real, imag_real = by(0)
    real_imag, imag_imag = by(1)
    return real_real - imag_imag, real_imag + imag_real


def injected(tick, sites, pulse, shape):
    shots, breadth = shape
    row = lax.broadcasted_iota(jnp.int32, (shots, shots), 0)
    column = lax.broadcasted_iota(jnp.int32, (shots, shots), 1)
    spread = jnp.broadcast_to(sites[pl.ds(tick - 1, 1), :], (shots, shots)).astype(jnp.float32)
    site = jnp.sum(jnp.where(row == column, spread, 0.0), axis=1, keepdims=True)
    lanes = lax.broadcasted_iota(jnp.int32, (shots, breadth), 1).astype(jnp.float32)
    hit = lanes == site
    return [jnp.where(hit, pulse[pl.ds(part, 1), pl.ds(tick - 1, 1)], 0.0) for part in range(2)]


def first_kernel(parity, chained, *refs):
    operator, contrast, residual, panel = refs[:4]
    outs = 2 - parity
    refs = refs[7:] if chained else refs[4:]
    out = refs[:outs]
    high, low, grad, whole, wave, arrived, left, sems = refs[outs:]

    @pl.when(is_odd() if parity else jnp.logical_not(is_odd()))
    def _():
        copies = [
            pltpu.make_async_copy(residual.at[0, 0, 0], wave, sems.at[0]),
            pltpu.make_async_copy(panel.at[0, 0], arrived, sems.at[1]),
            pltpu.make_async_copy(operator.at[0, 0, 0], whole.at[0], sems.at[2]),
            pltpu.make_async_copy(operator.at[0, 0, 1], whole.at[1], sems.at[3]),
        ]
        for copy in copies:
            copy.start()
        copies[0].wait()
        copies[1].wait()
        take(arrived, wave, contrast, None, grad, left)
        for part in range(2):
            copies[2 + part].wait()
            high[part], low[part] = split(whole[part])
        store(out, multiply(left, high, low, slice(None)))


def store(out, pair):
    if len(out) == 1:
        out[0][0], out[0][1] = pair
    else:
        out[0][...], out[1][...] = pair


def panel_shape(parity, shots, breadth):
    if parity:
        return [pltpu.VMEM((2, shots, breadth), jnp.float32)]
    return [pltpu.VMEM((shots, breadth), jnp.float32)] * 2


def first(parity, operator, contrast, residual, panel, carried):
    shots, breadth = panel.shape[3:]
    half = pltpu.VMEM((2, breadth, breadth), jnp.bfloat16)
    outs = panel_shape(parity, shots, breadth)
    return pl.pallas_call(
        functools.partial(first_kernel, parity, bool(carried)),
        out_shape=(*outs, half, half, pltpu.VMEM((8, breadth), jnp.float32)),
        in_specs=[IN_HBM, IN_VMEM, IN_HBM, IN_HBM] + [IN_VMEM] * len(carried),
        out_specs=(IN_VMEM,) * (len(outs) + 3),
        scratch_shapes=[
            pltpu.VMEM((2, breadth, breadth), jnp.float32),
            pltpu.VMEM((2, shots, breadth), jnp.float32),
            pltpu.VMEM((2, shots, breadth), jnp.float32),
            pltpu.VMEM((4 * shots, breadth), jnp.bfloat16),
            pltpu.SemaphoreType.DMA((4,)),
        ],
        input_output_aliases={4 + i: len(outs) + i for i in range(len(carried))},
        compiler_params=PARAMS,
        cost_estimate=QUICK if parity else LONGER,
        name=f"first_{parity}",
    )(kept(operator), contrast, kept(residual), kept(panel), *[pinned(value) for value in carried])


def arrive(tick, parity, panel, shared, grad_in, grad, left):
    residual, contrast, sites, pulse = shared
    waves = residual.at[0, 0, tick]
    if parity:
        take([part[...] for part in panel], waves, contrast, grad_in, grad, left)
        return
    surface = lax.axis_index("depth") == 0

    @pl.when(surface)
    def _():
        take(injected(tick, sites, pulse, panel.shape[1:]), waves, contrast, grad_in, grad, left)

    @pl.when(jnp.logical_not(surface))
    def _():
        take(panel, waves, contrast, grad_in, grad, left)


def step_kernel(tick, parity, *refs):
    panels = 1 + parity
    panel = refs[:panels] if parity else refs[0]
    shared, (high, low, grad_in) = refs[panels : panels + 4], refs[panels + 4 : panels + 7]
    *out, grad, left = refs[panels + 7 :]

    @pl.when(is_odd() if parity else jnp.logical_not(is_odd()))
    def _():
        arrive(tick, parity, panel, shared, grad_in, grad, left)
        store(out, multiply(left, high, low, slice(None)))


def step(tick, parity, panel, shared, high, low, grad):
    shots, breadth = panel[0].shape[-2:]
    outs = panel_shape(parity, shots, breadth)
    operands = [pinned(value) for value in (*panel, *shared, high, low, grad)]
    return pl.pallas_call(
        functools.partial(step_kernel, tick, parity),
        out_shape=(*outs, pltpu.VMEM(grad.shape, jnp.float32)),
        in_specs=[IN_VMEM] * len(operands),
        out_specs=(IN_VMEM,) * (len(outs) + 1),
        scratch_shapes=[pltpu.VMEM((4 * shots, breadth), jnp.bfloat16)],
        input_output_aliases={len(operands) - 1: len(outs)},
        compiler_params=PARAMS,
        cost_estimate=QUICK if parity else LONGER,
        name=f"step_{tick}_{parity}",
    )(*operands)


def final_arrive(refs, grad_in, grad, left):
    from_above, from_mate, shared = refs[0], refs[1:3], refs[3:7]

    @pl.when(is_odd())
    def _():
        arrive(TICKS - 1, 1, from_mate, shared, grad_in, grad, left)

    @pl.when(jnp.logical_not(is_odd()))
    def _():
        arrive(TICKS - 1, 0, from_above, shared, grad_in, grad, left)


def gradient_chunks(panels, shared, grad, scale):
    breadth = grad.shape[1]
    count = lax.axis_size("freq")
    width = breadth // count

    def body(*refs):
        chunks, total = refs[8 : 8 + count], refs[8 + count]
        final_arrive(refs, refs[7], total, None)
        gradient = jnp.sum(total[...], axis=0, keepdims=True) * scale
        me = lax.axis_index("freq")
        for distance in range(count):
            owner = lax.rem(me + distance, count)
            chunk = jnp.zeros((1, width), jnp.float32)
            for place in range(count):
                piece = gradient[:, place * width : (place + 1) * width]
                chunk = jnp.where(owner == place, piece, chunk)
            chunks[distance][...] = chunk

    operands = [pinned(value) for value in (*panels, *shared, grad)]
    return pl.pallas_call(
        body,
        out_shape=(pltpu.VMEM((1, width), jnp.float32),) * count,
        in_specs=[IN_VMEM] * len(operands),
        out_specs=(IN_VMEM,) * count,
        scratch_shapes=[pltpu.VMEM(grad.shape, jnp.float32)],
        compiler_params=PARAMS,
        cost_estimate=QUICK,
        name="gradient",
    )(*operands)


def last_kernel(*refs):
    high, low, out, left, held, sems = refs[7:]
    final_arrive(refs, None, None, left)
    halves = held.shape[0]
    width = held.shape[3]
    copies = []
    for half in range(halves):
        columns = pl.ds(half * width, width)
        held[half, 0], held[half, 1] = multiply(left, high, low, columns)
        copies.append(pltpu.make_async_copy(held.at[half], out.at[:, :, columns], sems.at[half]))
        copies[-1].start()
    for copy in copies:
        copy.wait()


def last(panels, shared, high, low):
    shots, breadth = panels[0].shape[1:]
    operands = [pinned(value) for value in (*panels, *shared, high, low)]
    return pl.pallas_call(
        last_kernel,
        out_shape=jax.ShapeDtypeStruct((2, shots, breadth), jnp.float32),
        in_specs=[IN_VMEM] * len(operands),
        out_specs=IN_HBM,
        scratch_shapes=[
            pltpu.VMEM((4 * shots, breadth), jnp.bfloat16),
            pltpu.VMEM((2, 2, shots, breadth // 2), jnp.float32),
            pltpu.SemaphoreType.DMA((2,)),
        ],
        compiler_params=PARAMS,
        cost_estimate=QUICK,
        name="last",
    )(*operands)


def cross_route(levels):
    route = {level: (level + 1) % levels for level in range(levels)}
    chips = levels // 2
    if chips % 2 == 0:
        for chip in range(chips - 1, 1, -2):
            route[levels - 1 if chip == chips - 1 else 2 * chip] = 2 * (chip - 2) + 1
        route[2 if chips > 2 else levels - 1] = 0
    return sorted(route.items())


def local(
    extrapolation_operator,
    impedance_contrast,
    ascending_residual,
    arriving_downward_matrices,
    shot_node_indices,
    emitted_pulse,
):
    levels = lax.axis_size("depth")
    freqs = lax.axis_size("freq")
    shots = arriving_downward_matrices.shape[3]
    mate_route = [(level, level ^ 1) for level in range(levels)]
    down_route = cross_route(levels)
    shared = (ascending_residual, impedance_contrast, shot_node_indices, emitted_pulse[0].T)

    def mate(parts):
        return [lax.ppermute(part, "depth", mate_route) for part in parts]

    def down(panel):
        return lax.ppermute(panel, "depth", down_route)

    start = (extrapolation_operator, pinned(impedance_contrast), ascending_residual, arriving_downward_matrices)
    odd, *carried = first(1, *start, ())
    from_above = down(odd)
    *even, high, low, grad = first(0, *start, carried)
    from_mate = mate(even)
    for tick in range(1, TICKS - 1):
        odd, grad = step(tick, 1, from_mate, shared, high, low, grad)
        later = down(odd)
        *even, grad = step(tick, 0, [from_above], shared, high, low, grad)
        from_mate = mate(even)
        from_above = later

    panels = (from_above, *from_mate)
    chunks = gradient_chunks(panels, shared, grad, 1.0 / math.sqrt(shots * TICKS))
    out = last(panels, shared, high, low)
    gradient = chunks[0]
    for distance in range(1, freqs):
        route = [(i, (i + distance) % freqs) for i in range(freqs)]
        gradient = gradient + lax.ppermute(chunks[distance], "freq", route)
    return (out[None, None], gradient)


def solution(mesh):
    placed = (
        P("freq", "depth", None, None, None),
        P("depth", None),
        P("freq", "depth", None, None, None, None),
        P("freq", "depth", None, None, None),
        P(),
        P("freq", None, None),
    )
    return jax.shard_map(
        local,
        mesh=mesh,
        in_specs=placed,
        out_specs=(P("freq", "depth", None, None, None), P("depth", "freq")),
        check_vma=False,
    )
```

```python
import functools
import math

import jax
import jax.numpy as jnp
from jax import lax
from jax.experimental import pallas as pl
from jax.experimental.pallas import tpu as pltpu
from jax.sharding import PartitionSpec as P

TICKS = 5
TAIL = 16
VMEM_LIMIT = 24 * 1024 * 1024
QUICK = pl.CostEstimate(flops=1, bytes_accessed=1, transcendentals=0)
LONGER = pl.CostEstimate(flops=500000000, bytes_accessed=1, transcendentals=0)
PARAMS = pltpu.CompilerParams(vmem_limit_bytes=VMEM_LIMIT)
IN_VMEM = pl.BlockSpec(memory_space=pltpu.VMEM)
IN_HBM = pl.BlockSpec(memory_space=pltpu.HBM)


def pinned(value):
    return pltpu.with_memory_space_constraint(value, pltpu.VMEM)


def kept(value):
    return pltpu.with_memory_space_constraint(value, pltpu.HBM)


def dot(left, right):
    return jnp.dot(left, right, preferred_element_type=jnp.float32)


def is_odd():
    return lax.axis_index("depth") % 2 == 1


def when_parity(parity):
    return pl.when(is_odd() if parity else jnp.logical_not(is_odd()))


def split(value):
    high = value.astype(jnp.bfloat16)
    low = (value - high.astype(jnp.float32)).astype(jnp.bfloat16)
    return high, low


def fold(product):
    return jnp.sum(product.reshape(-1, 8, product.shape[1]), axis=0)


def take(segments, waves, contrast, grad_in, grad, left):
    shots = left.shape[0] // 4
    total = None if grad_in is None else grad_in[...]
    for start, pair in segments:
        rows = pl.ds(start, pair[0].shape[0])
        for part in range(2):
            wave = waves[part, rows]
            term = fold(pair[part] * wave)
            total = term if total is None else total + term
            high, low = split(pair[part] + contrast[...] * wave)
            left[pl.ds(part * shots + start, rows.size), :] = high
            left[pl.ds((2 + part) * shots + start, rows.size), :] = low
    grad[...] = total


def multiply(left, high, low, columns):
    shots = left.shape[0] // 4

    def by(part):
        big = dot(left[...], high[part, :, columns])
        small = dot(left[pl.ds(0, 2 * shots), :], low[part, :, columns])
        total = big[: 2 * shots] + (big[2 * shots :] + small)
        return total[:shots], total[shots:]

    real_real, imag_real = by(0)
    real_imag, imag_imag = by(1)
    return real_real - imag_imag, real_imag + imag_real


def injected(tick, sites, pulse, shape):
    shots, breadth = shape
    row = lax.broadcasted_iota(jnp.int32, (shots, shots), 0)
    column = lax.broadcasted_iota(jnp.int32, (shots, shots), 1)
    spread = jnp.broadcast_to(sites[pl.ds(tick - 1, 1), :], (shots, shots)).astype(jnp.float32)
    site = jnp.sum(jnp.where(row == column, spread, 0.0), axis=1, keepdims=True)
    lanes = lax.broadcasted_iota(jnp.int32, (shots, breadth), 1).astype(jnp.float32)
    hit = lanes == site
    return [jnp.where(hit, pulse[pl.ds(part, 1), pl.ds(tick - 1, 1)], 0.0) for part in range(2)]


def first_kernel(parity, chained, *refs):
    operator, contrast, residual, panel = refs[:4]
    refs = refs[7:] if chained else refs[4:]
    out = refs[: 2 - parity]
    high, low, grad = refs[2 - parity : 5 - parity]
    whole, reflect, wave, arrived, left, sems = refs[-6:]
    shots, breadth = arrived.shape[1:]
    depth = breadth // 2

    @when_parity(parity)
    def _():
        copies = [
            pltpu.make_async_copy(contrast, reflect, sems.at[0]),
            pltpu.make_async_copy(residual.at[0, 0, 0], wave, sems.at[1]),
            pltpu.make_async_copy(panel.at[0, 0], arrived, sems.at[2]),
        ]
        pieces = [(part, pl.ds(half * depth, depth)) for half in range(2) for part in range(2)]
        for place, (part, rows) in enumerate(pieces):
            copies.append(
                pltpu.make_async_copy(operator.at[0, 0, part, rows], whole.at[part, rows], sems.at[3 + place])
            )
        for copy in copies:
            copy.start()
        for copy in copies[:3]:
            copy.wait()
        take([(0, arrived)], wave, reflect, None, grad, left)
        sums = [None, None]
        for place, (part, rows) in enumerate(pieces):
            copies[3 + place].wait()
            upper, lower = split(whole[part, rows])
            high[part, rows] = upper
            low[part, rows] = lower
            big = dot(left[:, rows], upper)
            small = dot(left[pl.ds(0, 2 * shots), rows], lower)
            total = big[: 2 * shots] + (big[2 * shots :] + small)
            sums[part] = total if sums[part] is None else sums[part] + total
        store(out, (sums[0][:shots] - sums[1][shots:], sums[1][:shots] + sums[0][shots:]))


def store(out, pair):
    start = 0
    for piece in out:
        for part in range(2):
            piece[part] = pair[part][start : start + piece.shape[1]]
        start += piece.shape[1]


def panel_shapes(parity, shots, breadth):
    rows = [shots] if parity else [shots - TAIL, TAIL]
    return tuple(pltpu.VMEM((2, count, breadth), jnp.float32) for count in rows)


def first(parity, operator, contrast, residual, panel, carried):
    shots, breadth = panel.shape[3:]
    half = pltpu.VMEM((2, breadth, breadth), jnp.bfloat16)
    outs = panel_shapes(parity, shots, breadth)
    return pl.pallas_call(
        functools.partial(first_kernel, parity, bool(carried)),
        out_shape=(*outs, half, half, pltpu.VMEM((8, breadth), jnp.float32)),
        in_specs=[IN_HBM] * 4 + [IN_VMEM] * len(carried),
        out_specs=(IN_VMEM,) * (len(outs) + 3),
        scratch_shapes=[
            pltpu.VMEM((2, breadth, breadth), jnp.float32),
            pltpu.VMEM((1, breadth), jnp.float32),
            pltpu.VMEM((2, shots, breadth), jnp.float32),
            pltpu.VMEM((2, shots, breadth), jnp.float32),
            pltpu.VMEM((4 * shots, breadth), jnp.bfloat16),
            pltpu.SemaphoreType.DMA((7,)),
        ],
        input_output_aliases={4 + i: len(outs) + i for i in range(len(carried))},
        compiler_params=PARAMS,
        cost_estimate=QUICK if parity else LONGER,
        name=f"first_{parity}",
    )(kept(operator), kept(contrast), kept(residual), kept(panel), *[pinned(value) for value in carried])


def arrive(tick, parity, panel, shared, grad_in, grad, left):
    residual, contrast, sites, pulse = shared
    rest = (residual.at[0, 0, tick], contrast, grad_in, grad, left)
    if parity:
        take([(0, panel[0]), (panel[0].shape[1], panel[1])], *rest)
        return
    surface = lax.axis_index("depth") == 0

    @pl.when(surface)
    def _():
        take([(0, injected(tick, sites, pulse, panel[0].shape[1:]))], *rest)

    @pl.when(jnp.logical_not(surface))
    def _():
        take([(0, panel[0])], *rest)


def step_kernel(tick, parity, *refs):
    panel, shared = refs[: 1 + parity], refs[1 + parity : 5 + parity]
    high, low, grad_in = refs[5 + parity : 8 + parity]
    *out, grad, left = refs[8 + parity :]

    @when_parity(parity)
    def _():
        arrive(tick, parity, panel, shared, grad_in, grad, left)
        store(out, multiply(left, high, low, slice(None)))


def step(tick, parity, panel, shared, high, low, grad, shots):
    breadth = grad.shape[1]
    outs = panel_shapes(parity, shots, breadth)
    operands = [pinned(value) for value in (*panel, *shared, high, low, grad)]
    return pl.pallas_call(
        functools.partial(step_kernel, tick, parity),
        out_shape=(*outs, pltpu.VMEM(grad.shape, jnp.float32)),
        in_specs=[IN_VMEM] * len(operands),
        out_specs=(IN_VMEM,) * (len(outs) + 1),
        scratch_shapes=[pltpu.VMEM((4 * shots, breadth), jnp.bfloat16)],
        input_output_aliases={len(operands) - 1: len(outs)},
        compiler_params=PARAMS,
        cost_estimate=QUICK if parity else LONGER,
        name=f"step_{tick}_{parity}",
    )(*operands)


def half_out(half, left, high, low, out, held, sem):
    width = held.shape[2]
    columns = pl.ds(half * width, width)
    held[0], held[1] = multiply(left, high, low, columns)
    return pltpu.make_async_copy(held, out.at[:, :, columns], sem)


def last_first(panels, shared, high, low, grad, scale):
    shots, breadth = panels[0].shape[1:]
    count = lax.axis_size("freq")
    width = breadth // count

    def body(from_above, from_mate, from_mate_tail, residual, contrast, sites, pulse, high, low, grad_in, out, left, *refs):
        chunks, (total, held, sem) = refs[:count], refs[count:]
        shared = (residual, contrast, sites, pulse)

        @when_parity(1)
        def _():
            arrive(TICKS - 1, 1, (from_mate, from_mate_tail), shared, grad_in, total, left)

        @when_parity(0)
        def _():
            arrive(TICKS - 1, 0, (from_above,), shared, grad_in, total, left)

        copy = half_out(0, left, high, low, out, held, sem)
        copy.start()
        gradient = jnp.sum(total[...], axis=0, keepdims=True) * scale
        me = lax.axis_index("freq")
        for distance in range(count):
            owner = lax.rem(me + distance, count)
            chunk = jnp.zeros((1, width), jnp.float32)
            for place in range(count):
                piece = gradient[:, place * width : (place + 1) * width]
                chunk = jnp.where(owner == place, piece, chunk)
            chunks[distance][...] = chunk
        copy.wait()

    operands = [pinned(value) for value in (*panels, *shared, high, low, grad)]
    chunk = pltpu.VMEM((1, width), jnp.float32)
    left = pltpu.VMEM((4 * shots, breadth), jnp.bfloat16)
    return pl.pallas_call(
        body,
        out_shape=(pltpu.HBM((2, shots, breadth), jnp.float32), left) + (chunk,) * count,
        in_specs=[IN_VMEM] * len(operands),
        out_specs=(IN_HBM,) + (IN_VMEM,) * (1 + count),
        scratch_shapes=[
            pltpu.VMEM(grad.shape, jnp.float32),
            pltpu.VMEM((2, shots, breadth // 2), jnp.float32),
            pltpu.SemaphoreType.DMA,
        ],
        compiler_params=PARAMS,
        cost_estimate=QUICK,
        name="last_first",
    )(*operands)


def last_second(out, left, high, low):
    def body(left, high, low, _, out, held, sem):
        copy = half_out(1, left, high, low, out, held, sem)
        copy.start()
        copy.wait()

    shots, breadth = out.shape[1:]
    return pl.pallas_call(
        body,
        out_shape=pltpu.HBM(out.shape, jnp.float32),
        in_specs=[IN_VMEM] * 3 + [IN_HBM],
        out_specs=IN_HBM,
        scratch_shapes=[pltpu.VMEM((2, shots, breadth // 2), jnp.float32), pltpu.SemaphoreType.DMA],
        input_output_aliases={3: 0},
        compiler_params=PARAMS,
        cost_estimate=QUICK,
        name="last_second",
    )(pinned(left), pinned(high), pinned(low), kept(out))


def cross_route(levels):
    route = {level: (level + 1) % levels for level in range(levels)}
    chips = levels // 2
    if chips % 2 == 0:
        for chip in range(chips - 1, 1, -2):
            route[levels - 1 if chip == chips - 1 else 2 * chip] = 2 * (chip - 2) + 1
        route[2 if chips > 2 else levels - 1] = 0
    return sorted(route.items())


def local(
    extrapolation_operator,
    impedance_contrast,
    ascending_residual,
    arriving_downward_matrices,
    shot_node_indices,
    emitted_pulse,
):
    levels = lax.axis_size("depth")
    freqs = lax.axis_size("freq")
    shots = arriving_downward_matrices.shape[3]
    mate_route = [(level, level ^ 1) for level in range(levels)]
    down_route = cross_route(levels)
    shared = (ascending_residual, impedance_contrast, shot_node_indices, emitted_pulse[0].T)

    def mate(pieces):
        return [lax.ppermute(piece, "depth", mate_route) for piece in pieces]

    def down(panel):
        return lax.ppermute(panel, "depth", down_route)

    start = (extrapolation_operator, impedance_contrast, ascending_residual, arriving_downward_matrices)
    odd, *carried = first(1, *start, ())
    from_above = down(odd)
    *even, high, low, grad = first(0, *start, carried)
    from_mate = mate(even)
    for tick in range(1, TICKS - 1):
        odd, grad = step(tick, 1, from_mate, shared, high, low, grad, shots)
        later = down(odd)
        *even, grad = step(tick, 0, (from_above,), shared, high, low, grad, shots)
        from_mate = mate(even)
        from_above = later

    scale = 1.0 / math.sqrt(shots * TICKS)
    out, left, *chunks = last_first((from_above, *from_mate), shared, high, low, grad, scale)
    gradient = chunks[0]
    for distance in range(1, freqs):
        route = [(i, (i + distance) % freqs) for i in range(freqs)]
        gradient = gradient + lax.ppermute(chunks[distance], "freq", route)
    out = last_second(out, left, high, low)
    return (out[None, None], gradient)


def solution(mesh):
    placed = (
        P("freq", "depth", None, None, None),
        P("depth", None),
        P("freq", "depth", None, None, None, None),
        P("freq", "depth", None, None, None),
        P(),
        P("freq", None, None),
    )
    return jax.shard_map(
        local,
        mesh=mesh,
        in_specs=placed,
        out_specs=(P("freq", "depth", None, None, None), P("depth", "freq")),
        check_vma=False,
    )
```

```python
import functools
import math

import jax
import jax.numpy as jnp
from jax import lax
from jax.experimental import pallas as pl
from jax.experimental.pallas import tpu as pltpu
from jax.sharding import PartitionSpec as P

TICKS = 5
HALVES = 2
TAIL = 16
VMEM_LIMIT = 24 * 1024 * 1024
WEIGHTS = {"step_1_0": 10000000, "step_0_1": 1000000, "step_1_1": 200000000, "last_0": 200000000, "gradient": 10000000}
PARAMS = pltpu.CompilerParams(vmem_limit_bytes=VMEM_LIMIT)
IN_VMEM = pl.BlockSpec(memory_space=pltpu.VMEM)
IN_HBM = pl.BlockSpec(memory_space=pltpu.HBM)


def pinned(value):
    return pltpu.with_memory_space_constraint(value, pltpu.VMEM)


def kept(value):
    return pltpu.with_memory_space_constraint(value, pltpu.HBM)


def cost(kind):
    return pl.CostEstimate(flops=WEIGHTS.get(kind, 1), bytes_accessed=1, transcendentals=0)


def dot(left, right):
    return jnp.dot(left, right, preferred_element_type=jnp.float32)


def is_odd():
    return lax.axis_index("depth") % 2 == 1


def when_parity(parity):
    return pl.when(is_odd() if parity else jnp.logical_not(is_odd()))


def split(value):
    high = value.astype(jnp.bfloat16)
    low = (value - high.astype(jnp.float32)).astype(jnp.bfloat16)
    return high, low


def fold(product):
    return jnp.sum(product.reshape(-1, 8, product.shape[1]), axis=0)


def take(pair, start, waves, contrast, grad_in, grad, left, offset=0):
    count = pair[0].shape[0]
    total = None if grad_in is None else grad_in[...]
    for part in range(2):
        wave = waves[part, pl.ds(start + offset, count)]
        if grad is not None:
            term = fold(pair[part] * wave)
            total = term if total is None else total + term
        if left is not None:
            shots = left.shape[0] // 4
            high, low = split(pair[part] + contrast[...] * wave)
            left[pl.ds(part * shots + offset, count), :] = high
            left[pl.ds((2 + part) * shots + offset, count), :] = low
    if grad is not None:
        grad[...] = total


def multiply(left, high, low, columns):
    shots = left.shape[0] // 4

    def by(part):
        big = dot(left[...], high[part, :, columns])
        small = dot(left[pl.ds(0, 2 * shots), :], low[part, :, columns])
        total = big[: 2 * shots] + (big[2 * shots :] + small)
        return total[:shots], total[shots:]

    real_real, imag_real = by(0)
    real_imag, imag_imag = by(1)
    return real_real - imag_imag, real_imag + imag_real


def injected(tick, start, sites, pulse, shape):
    rows, breadth = shape
    shots = sites.shape[1]
    row = lax.broadcasted_iota(jnp.int32, (rows, shots), 0) + start
    column = lax.broadcasted_iota(jnp.int32, (rows, shots), 1)
    spread = jnp.broadcast_to(sites[pl.ds(tick - 1, 1), :], (rows, shots)).astype(jnp.float32)
    site = jnp.sum(jnp.where(row == column, spread, 0.0), axis=1, keepdims=True)
    lanes = lax.broadcasted_iota(jnp.int32, (rows, breadth), 1).astype(jnp.float32)
    hit = lanes == site
    return [jnp.where(hit, pulse[pl.ds(part, 1), pl.ds(tick - 1, 1)], 0.0) for part in range(2)]


def first_kernel(parity, chained, *refs):
    operator, contrast, residual, panel = refs[:4]
    refs = refs[7:] if chained else refs[4:]
    pieces = HALVES * (2 - parity)
    out = refs[:pieces]
    high, low, grad = refs[pieces : pieces + 3]
    whole, reflect, wave, arrived, left, sems = refs[-6:]
    shots, breadth = arrived.shape[1:]
    depth = breadth // 2

    @when_parity(parity)
    def _():
        copies = [
            pltpu.make_async_copy(contrast, reflect, sems.at[0]),
            pltpu.make_async_copy(residual.at[0, 0, 0], wave, sems.at[1]),
            pltpu.make_async_copy(panel.at[0, 0], arrived, sems.at[2]),
        ]
        pieces = [(part, pl.ds(half * depth, depth)) for half in range(2) for part in range(2)]
        for place, (part, rows) in enumerate(pieces):
            copies.append(
                pltpu.make_async_copy(operator.at[0, 0, part, rows], whole.at[part, rows], sems.at[3 + place])
            )
        for copy in copies:
            copy.start()
        for copy in copies[:3]:
            copy.wait()
        take(arrived, 0, wave, reflect, None, grad, left)
        sums = [None, None]
        for place, (part, rows) in enumerate(pieces):
            copies[3 + place].wait()
            upper, lower = split(whole[part, rows])
            high[part, rows] = upper
            low[part, rows] = lower
            big = dot(left[:, rows], upper)
            small = dot(left[pl.ds(0, 2 * shots), rows], lower)
            total = big[: 2 * shots] + (big[2 * shots :] + small)
            sums[part] = total if sums[part] is None else sums[part] + total
        parts = sums[0][:shots] - sums[1][shots:], sums[1][:shots] + sums[0][shots:]
        store(out, parts)


def store(out, parts):
    start = 0
    for piece in out:
        for part in range(2):
            piece[part] = parts[part][start : start + piece.shape[1]]
        start += piece.shape[1]


def piece_shapes(parity, rows, breadth):
    counts = [rows] if parity else [rows - TAIL, TAIL]
    return tuple(pltpu.VMEM((2, count, breadth), jnp.float32) for count in counts)


def first(parity, operator, contrast, residual, panel, carried):
    shots, breadth = panel.shape[3:]
    half = pltpu.VMEM((2, breadth, breadth), jnp.bfloat16)
    outs = piece_shapes(parity, shots // HALVES, breadth) * HALVES
    return pl.pallas_call(
        functools.partial(first_kernel, parity, bool(carried)),
        out_shape=(*outs, half, half, pltpu.VMEM((8, breadth), jnp.float32)),
        in_specs=[IN_HBM] * 4 + [IN_VMEM] * len(carried),
        out_specs=(IN_VMEM,) * (len(outs) + 3),
        scratch_shapes=[
            pltpu.VMEM((2, breadth, breadth), jnp.float32),
            pltpu.VMEM((1, breadth), jnp.float32),
            pltpu.VMEM((2, shots, breadth), jnp.float32),
            pltpu.VMEM((2, shots, breadth), jnp.float32),
            pltpu.VMEM((4 * shots, breadth), jnp.bfloat16),
            pltpu.SemaphoreType.DMA((7,)),
        ],
        input_output_aliases={4 + i: len(outs) + i for i in range(len(carried))},
        compiler_params=PARAMS,
        cost_estimate=cost(f"first_{parity}"),
        name=f"first_{parity}",
    )(kept(operator), kept(contrast), kept(residual), kept(panel), *[pinned(value) for value in carried])


def arrive(tick, half, parity, panel, shared, grad_in, grad, left):
    residual, contrast, sites, pulse = shared
    rows = sum(piece.shape[1] for piece in panel)
    start = half * rows
    waves = residual.at[0, 0, tick]
    rest = (start, waves, contrast, grad_in, grad, left)
    if parity:
        take(panel[0], *rest)
        take(panel[1], start, waves, contrast, grad, grad, left, panel[0].shape[1])
        return
    surface = lax.axis_index("depth") == 0

    @pl.when(surface)
    def _():
        take(injected(tick, start, sites, pulse, panel[0].shape[1:]), *rest)

    @pl.when(jnp.logical_not(surface))
    def _():
        take(panel[0], *rest)


def arrive_either(half, above, mate, shared, grad_in, grad, left):
    @when_parity(1)
    def _():
        arrive(TICKS - 1, half, 1, mate, shared, grad_in, grad, left)

    @when_parity(0)
    def _():
        arrive(TICKS - 1, half, 0, (above,), shared, grad_in, grad, left)


def step_kernel(tick, half, parity, *refs):
    panel, refs = refs[: 1 + parity], refs[1 + parity :]
    shared, (high, low, grad_in) = refs[:4], refs[4:7]
    *out, grad, left = refs[7:]

    @when_parity(parity)
    def _():
        arrive(tick, half, parity, panel, shared, grad_in, grad, left)
        store(out, multiply(left, high, low, slice(None)))


def step(tick, half, parity, panel, shared, high, low, grad, rows):
    breadth = grad.shape[1]
    outs = piece_shapes(parity, rows, breadth)
    operands = [pinned(value) for value in (*panel, *shared, high, low, grad)]
    return pl.pallas_call(
        functools.partial(step_kernel, tick, half, parity),
        out_shape=(*outs, pltpu.VMEM(grad.shape, jnp.float32)),
        in_specs=[IN_VMEM] * len(operands),
        out_specs=(IN_VMEM,) * (len(outs) + 1),
        scratch_shapes=[pltpu.VMEM((4 * rows, breadth), jnp.bfloat16)],
        input_output_aliases={len(operands) - 1: len(outs)},
        compiler_params=PARAMS,
        cost_estimate=cost(f"step_{half}_{parity}"),
        name=f"step_{tick}_{half}_{parity}",
    )(*operands)


def gradient_chunks(above, mate, shared, grad, scale):
    breadth = grad.shape[1]
    count = lax.axis_size("freq")
    width = breadth // count

    def body(above, mate, mate_tail, residual, contrast, sites, pulse, grad_in, *refs):
        chunks, total = refs[:count], refs[count]
        arrive_either(HALVES - 1, above, (mate, mate_tail), (residual, contrast, sites, pulse), grad_in, total, None)
        gradient = jnp.sum(total[...], axis=0, keepdims=True) * scale
        me = lax.axis_index("freq")
        for distance in range(count):
            owner = lax.rem(me + distance, count)
            chunk = jnp.zeros((1, width), jnp.float32)
            for place in range(count):
                piece = gradient[:, place * width : (place + 1) * width]
                chunk = jnp.where(owner == place, piece, chunk)
            chunks[distance][...] = chunk

    operands = [pinned(value) for value in (above, *mate, *shared, grad)]
    return pl.pallas_call(
        body,
        out_shape=(pltpu.VMEM((1, width), jnp.float32),) * count,
        in_specs=[IN_VMEM] * len(operands),
        out_specs=(IN_VMEM,) * count,
        scratch_shapes=[pltpu.VMEM(grad.shape, jnp.float32)],
        compiler_params=PARAMS,
        cost_estimate=cost("gradient"),
        name="gradient",
    )(*operands)


def last_kernel(half, chained, above, mate, mate_tail, *refs):
    shared, high, low = refs[:4], refs[4], refs[5]
    if chained:
        out, left, held, sem = refs[7:]
        grad_in = grad = None
    else:
        grad_in, out, grad, left, held, sem = refs[6:]
    arrive_either(half, above, (mate, mate_tail), shared, grad_in, grad, left)
    held[0], held[1] = multiply(left, high, low, slice(None))
    rows = held.shape[1]
    copy = pltpu.make_async_copy(held, out.at[:, pl.ds(half * rows, rows)], sem)
    copy.start()
    copy.wait()


def last(half, above, mate, shared, high, low, grad, out):
    rows, breadth = above.shape[1:]
    operands = [pinned(value) for value in (above, *mate, *shared, high, low)]
    whole = pltpu.HBM((2, rows * HALVES, breadth), jnp.float32)
    if out is None:
        operands.append(pinned(grad))
        out_shape, aliases = (whole, pltpu.VMEM(grad.shape, jnp.float32)), {9: 1}
    else:
        operands.append(kept(out))
        out_shape, aliases = (whole,), {9: 0}
    return pl.pallas_call(
        functools.partial(last_kernel, half, out is not None),
        out_shape=out_shape,
        in_specs=[IN_VMEM] * 9 + [IN_VMEM if out is None else IN_HBM],
        out_specs=(IN_HBM, IN_VMEM)[: len(out_shape)],
        scratch_shapes=[
            pltpu.VMEM((4 * rows, breadth), jnp.bfloat16),
            pltpu.VMEM((2, rows, breadth), jnp.float32),
            pltpu.SemaphoreType.DMA,
        ],
        input_output_aliases=aliases,
        compiler_params=PARAMS,
        cost_estimate=cost(f"last_{half}"),
        name=f"last_{half}",
    )(*operands)


def cross_route(levels):
    route = {level: (level + 1) % levels for level in range(levels)}
    chips = levels // 2
    if chips % 2 == 0:
        for chip in range(chips - 1, 1, -2):
            route[levels - 1 if chip == chips - 1 else 2 * chip] = 2 * (chip - 2) + 1
        route[2 if chips > 2 else levels - 1] = 0
    return sorted(route.items())


def local(
    extrapolation_operator,
    impedance_contrast,
    ascending_residual,
    arriving_downward_matrices,
    shot_node_indices,
    emitted_pulse,
):
    levels = lax.axis_size("depth")
    freqs = lax.axis_size("freq")
    shots = arriving_downward_matrices.shape[3]
    mate_route = [(level, level ^ 1) for level in range(levels)]
    down_route = cross_route(levels)
    shared = (ascending_residual, impedance_contrast, shot_node_indices, emitted_pulse[0].T)

    def mate(pieces):
        return [lax.ppermute(piece, "depth", mate_route) for piece in pieces]

    def down(piece):
        return lax.ppermute(piece, "depth", down_route)

    rows = shots // HALVES
    start = (extrapolation_operator, impedance_contrast, ascending_residual, arriving_downward_matrices)
    results = first(1, *start, ())
    above = [down(piece) for piece in results[:HALVES]]
    *even, high, low, grad = first(0, *start, results[HALVES:])
    beside = [mate(even[2 * half : 2 * half + 2]) for half in range(HALVES)]
    for tick in range(1, TICKS - 1):
        later = []
        for half in range(HALVES):
            odd, grad = step(tick, half, 1, beside[half], shared, high, low, grad, rows)
            later.append(down(odd))
        beside = []
        for half in range(HALVES):
            *even, grad = step(tick, half, 0, (above[half],), shared, high, low, grad, rows)
            beside.append(mate(even))
        above = later

    scale = 1.0 / math.sqrt(shots * TICKS)
    out, grad = last(0, above[0], beside[0], shared, high, low, grad, None)
    chunks = gradient_chunks(above[1], beside[1], shared, grad, scale)
    gradient = chunks[0]
    for distance in range(1, freqs):
        route = [(i, (i + distance) % freqs) for i in range(freqs)]
        gradient = gradient + lax.ppermute(chunks[distance], "freq", route)
    (out,) = last(1, above[1], beside[1], shared, high, low, None, out)
    return (out[None, None], gradient)


def solution(mesh):
    placed = (
        P("freq", "depth", None, None, None),
        P("depth", None),
        P("freq", "depth", None, None, None, None),
        P("freq", "depth", None, None, None),
        P(),
        P("freq", None, None),
    )
    return jax.shard_map(
        local,
        mesh=mesh,
        in_specs=placed,
        out_specs=(P("freq", "depth", None, None, None), P("depth", "freq")),
        check_vma=False,
    )
```

```python
import functools
import math

import jax
import jax.numpy as jnp
from jax import lax
from jax.experimental import pallas as pl
from jax.experimental.pallas import tpu as pltpu
from jax.sharding import PartitionSpec as P

TICKS = 5
HALVES = 2
TAIL = 16
VMEM_LIMIT = 24 * 1024 * 1024
WEIGHTS = {
    "first_0": 30000000,
    "first_1": 30000000,
    "step_1_0_0": 1000000,
    "step_1_1_0": 1000000,
    "step_2_0_0": 1000000,
    "step_2_1_0": 1000000000,
    "step_2_1_1": 500000000,
    "step_3_0_0": 1000000,
    "step_3_0_1": 500000000,
    "step_3_1_0": 500000000,
    "step_3_1_1": 1000000,
    "last_0": 30000000,
    "gradient": 100000000,
}
PARAMS = pltpu.CompilerParams(vmem_limit_bytes=VMEM_LIMIT)
IN_VMEM = pl.BlockSpec(memory_space=pltpu.VMEM)
IN_HBM = pl.BlockSpec(memory_space=pltpu.HBM)


def pinned(value):
    return pltpu.with_memory_space_constraint(value, pltpu.VMEM)


def kept(value):
    return pltpu.with_memory_space_constraint(value, pltpu.HBM)


def cost(kind):
    return pl.CostEstimate(flops=WEIGHTS.get(kind, 1), bytes_accessed=1, transcendentals=0)


def dot(left, right):
    return jnp.dot(left, right, preferred_element_type=jnp.float32)


def is_odd():
    return lax.axis_index("depth") % 2 == 1


def when_parity(parity):
    return pl.when(is_odd() if parity else jnp.logical_not(is_odd()))


def split(value):
    high = value.astype(jnp.bfloat16)
    low = (value - high.astype(jnp.float32)).astype(jnp.bfloat16)
    return high, low


def fold(product):
    return jnp.sum(product.reshape(-1, 8, product.shape[1]), axis=0)


def take(pair, start, waves, contrast, grad_in, grad, left, offset=0):
    count = pair[0].shape[0]
    total = None if grad_in is None else grad_in[...]
    for part in range(2):
        wave = waves[part, pl.ds(start + offset, count)]
        if grad is not None:
            term = fold(pair[part] * wave)
            total = term if total is None else total + term
        if left is not None:
            shots = left.shape[0] // 4
            high, low = split(pair[part] + contrast[...] * wave)
            left[pl.ds(part * shots + offset, count), :] = high
            left[pl.ds((2 + part) * shots + offset, count), :] = low
    if grad is not None:
        grad[...] = total


def multiply(left, high, low, columns):
    shots = left.shape[0] // 4

    def by(part):
        big = dot(left[...], high[part, :, columns])
        small = dot(left[pl.ds(0, 2 * shots), :], low[part, :, columns])
        total = big[: 2 * shots] + (big[2 * shots :] + small)
        return total[:shots], total[shots:]

    real_real, imag_real = by(0)
    real_imag, imag_imag = by(1)
    return real_real - imag_imag, real_imag + imag_real


def injected(tick, start, sites, pulse, shape):
    rows, breadth = shape
    shots = sites.shape[1]
    row = lax.broadcasted_iota(jnp.int32, (rows, shots), 0) + start
    column = lax.broadcasted_iota(jnp.int32, (rows, shots), 1)
    spread = jnp.broadcast_to(sites[pl.ds(tick - 1, 1), :], (rows, shots)).astype(jnp.float32)
    site = jnp.sum(jnp.where(row == column, spread, 0.0), axis=1, keepdims=True)
    lanes = lax.broadcasted_iota(jnp.int32, (rows, breadth), 1).astype(jnp.float32)
    hit = lanes == site
    return [jnp.where(hit, pulse[pl.ds(part, 1), pl.ds(tick - 1, 1)], 0.0) for part in range(2)]


def first_kernel(parity, chained, *refs):
    operator, contrast, residual, panel = refs[:4]
    refs = refs[7:] if chained else refs[4:]
    pieces = HALVES * (2 - parity)
    out = refs[:pieces]
    high, low, grad = refs[pieces : pieces + 3]
    whole, reflect, wave, arrived, left, sems = refs[-6:]
    shots, breadth = arrived.shape[1:]
    depth = breadth // 2

    @when_parity(parity)
    def _():
        copies = [
            pltpu.make_async_copy(contrast, reflect, sems.at[0]),
            pltpu.make_async_copy(residual.at[0, 0, 0], wave, sems.at[1]),
            pltpu.make_async_copy(panel.at[0, 0], arrived, sems.at[2]),
        ]
        pieces = [(part, pl.ds(half * depth, depth)) for half in range(2) for part in range(2)]
        for place, (part, rows) in enumerate(pieces):
            copies.append(
                pltpu.make_async_copy(operator.at[0, 0, part, rows], whole.at[part, rows], sems.at[3 + place])
            )
        for copy in copies:
            copy.start()
        for copy in copies[:3]:
            copy.wait()
        take(arrived, 0, wave, reflect, None, grad, left)
        sums = [None, None]
        for place, (part, rows) in enumerate(pieces):
            copies[3 + place].wait()
            upper, lower = split(whole[part, rows])
            high[part, rows] = upper
            low[part, rows] = lower
            big = dot(left[:, rows], upper)
            small = dot(left[pl.ds(0, 2 * shots), rows], lower)
            total = big[: 2 * shots] + (big[2 * shots :] + small)
            sums[part] = total if sums[part] is None else sums[part] + total
        parts = sums[0][:shots] - sums[1][shots:], sums[1][:shots] + sums[0][shots:]
        store(out, parts)


def store(out, parts):
    start = 0
    for piece in out:
        for part in range(2):
            piece[part] = parts[part][start : start + piece.shape[1]]
        start += piece.shape[1]


def piece_shapes(parity, rows, breadth):
    counts = [rows] if parity else [rows - TAIL, TAIL]
    return tuple(pltpu.VMEM((2, count, breadth), jnp.float32) for count in counts)


def first(parity, operator, contrast, residual, panel, carried):
    shots, breadth = panel.shape[3:]
    half = pltpu.VMEM((2, breadth, breadth), jnp.bfloat16)
    outs = piece_shapes(parity, shots // HALVES, breadth) * HALVES
    return pl.pallas_call(
        functools.partial(first_kernel, parity, bool(carried)),
        out_shape=(*outs, half, half, pltpu.VMEM((8, breadth), jnp.float32)),
        in_specs=[IN_HBM] * 4 + [IN_VMEM] * len(carried),
        out_specs=(IN_VMEM,) * (len(outs) + 3),
        scratch_shapes=[
            pltpu.VMEM((2, breadth, breadth), jnp.float32),
            pltpu.VMEM((1, breadth), jnp.float32),
            pltpu.VMEM((2, shots, breadth), jnp.float32),
            pltpu.VMEM((2, shots, breadth), jnp.float32),
            pltpu.VMEM((4 * shots, breadth), jnp.bfloat16),
            pltpu.SemaphoreType.DMA((7,)),
        ],
        input_output_aliases={4 + i: len(outs) + i for i in range(len(carried))},
        compiler_params=PARAMS,
        cost_estimate=cost(f"first_{parity}"),
        name=f"first_{parity}",
    )(kept(operator), kept(contrast), kept(residual), kept(panel), *[pinned(value) for value in carried])


def arrive(tick, half, parity, panel, shared, grad_in, grad, left):
    residual, contrast, sites, pulse = shared
    rows = sum(piece.shape[1] for piece in panel)
    start = half * rows
    waves = residual.at[0, 0, tick]
    rest = (start, waves, contrast, grad_in, grad, left)
    if parity:
        take(panel[0], *rest)
        take(panel[1], start, waves, contrast, grad, grad, left, panel[0].shape[1])
        return
    surface = lax.axis_index("depth") == 0

    @pl.when(surface)
    def _():
        take(injected(tick, start, sites, pulse, panel[0].shape[1:]), *rest)

    @pl.when(jnp.logical_not(surface))
    def _():
        take(panel[0], *rest)


def arrive_either(half, above, mate, shared, grad_in, grad, left):
    @when_parity(1)
    def _():
        arrive(TICKS - 1, half, 1, mate, shared, grad_in, grad, left)

    @when_parity(0)
    def _():
        arrive(TICKS - 1, half, 0, (above,), shared, grad_in, grad, left)


def step_kernel(tick, half, parity, *refs):
    panel, refs = refs[: 1 + parity], refs[1 + parity :]
    shared, (high, low, grad_in) = refs[:4], refs[4:7]
    *out, grad, left = refs[7:]

    @when_parity(parity)
    def _():
        arrive(tick, half, parity, panel, shared, grad_in, grad, left)
        store(out, multiply(left, high, low, slice(None)))


def step(tick, half, parity, panel, shared, high, low, grad, rows):
    breadth = grad.shape[1]
    outs = piece_shapes(parity, rows, breadth)
    operands = [pinned(value) for value in (*panel, *shared, high, low, grad)]
    return pl.pallas_call(
        functools.partial(step_kernel, tick, half, parity),
        out_shape=(*outs, pltpu.VMEM(grad.shape, jnp.float32)),
        in_specs=[IN_VMEM] * len(operands),
        out_specs=(IN_VMEM,) * (len(outs) + 1),
        scratch_shapes=[pltpu.VMEM((4 * rows, breadth), jnp.bfloat16)],
        input_output_aliases={len(operands) - 1: len(outs)},
        compiler_params=PARAMS,
        cost_estimate=cost(f"step_{tick}_{half}_{parity}"),
        name=f"step_{tick}_{half}_{parity}",
    )(*operands)


def gradient_chunks(above, mate, shared, grad, scale):
    breadth = grad.shape[1]
    count = lax.axis_size("freq")
    width = breadth // count

    def body(above, mate, mate_tail, residual, contrast, sites, pulse, grad_in, *refs):
        chunks, total = refs[:count], refs[count]
        arrive_either(HALVES - 1, above, (mate, mate_tail), (residual, contrast, sites, pulse), grad_in, total, None)
        gradient = jnp.sum(total[...], axis=0, keepdims=True) * scale
        me = lax.axis_index("freq")
        for distance in range(count):
            owner = lax.rem(me + distance, count)
            chunk = jnp.zeros((1, width), jnp.float32)
            for place in range(count):
                piece = gradient[:, place * width : (place + 1) * width]
                chunk = jnp.where(owner == place, piece, chunk)
            chunks[distance][...] = chunk

    operands = [pinned(value) for value in (above, *mate, *shared, grad)]
    return pl.pallas_call(
        body,
        out_shape=(pltpu.VMEM((1, width), jnp.float32),) * count,
        in_specs=[IN_VMEM] * len(operands),
        out_specs=(IN_VMEM,) * count,
        scratch_shapes=[pltpu.VMEM(grad.shape, jnp.float32)],
        compiler_params=PARAMS,
        cost_estimate=cost("gradient"),
        name="gradient",
    )(*operands)


def last_kernel(half, above, mate, mate_tail, *refs):
    shared, high, low = refs[:4], refs[4], refs[5]
    if half == 0:
        grad_in, held, grad, left = refs[6:]
        arrive_either(half, above, (mate, mate_tail), shared, grad_in, grad, left)
        held[0], held[1] = multiply(left, high, low, slice(None))
        return
    before, out, left, held, sems = refs[6:]
    rows = held.shape[1]
    copies = [
        pltpu.make_async_copy(piece, out.at[:, pl.ds(place * rows, rows)], sems.at[place])
        for place, piece in enumerate((before, held))
    ]
    copies[0].start()
    arrive_either(half, above, (mate, mate_tail), shared, None, None, left)
    held[0], held[1] = multiply(left, high, low, slice(None))
    copies[1].start()
    for copy in copies:
        copy.wait()


def last(half, above, mate, shared, high, low, grad, held):
    rows, breadth = above.shape[1:]
    left = pltpu.VMEM((4 * rows, breadth), jnp.bfloat16)
    piece = pltpu.VMEM((2, rows, breadth), jnp.float32)
    if half == 0:
        out_shape, out_specs, scratch, aliases = (piece, pltpu.VMEM(grad.shape, jnp.float32)), (IN_VMEM,) * 2, [left], {9: 1}
    else:
        out_shape, out_specs, aliases = (pltpu.HBM((2, rows * HALVES, breadth), jnp.float32),), (IN_HBM,), {}
        scratch = [left, piece, pltpu.SemaphoreType.DMA((HALVES,))]
    operands = [pinned(value) for value in (above, *mate, *shared, high, low, grad if half == 0 else held)]
    return pl.pallas_call(
        functools.partial(last_kernel, half),
        out_shape=out_shape,
        in_specs=[IN_VMEM] * len(operands),
        out_specs=out_specs,
        scratch_shapes=scratch,
        input_output_aliases=aliases,
        compiler_params=PARAMS,
        cost_estimate=cost(f"last_{half}"),
        name=f"last_{half}",
    )(*operands)


def cross_route(levels):
    route = {level: (level + 1) % levels for level in range(levels)}
    chips = levels // 2
    if chips % 2 == 0:
        for chip in range(chips - 1, 1, -2):
            route[levels - 1 if chip == chips - 1 else 2 * chip] = 2 * (chip - 2) + 1
        route[2 if chips > 2 else levels - 1] = 0
    return sorted(route.items())


def local(
    extrapolation_operator,
    impedance_contrast,
    ascending_residual,
    arriving_downward_matrices,
    shot_node_indices,
    emitted_pulse,
):
    levels = lax.axis_size("depth")
    freqs = lax.axis_size("freq")
    shots = arriving_downward_matrices.shape[3]
    mate_route = [(level, level ^ 1) for level in range(levels)]
    down_route = cross_route(levels)
    shared = (ascending_residual, impedance_contrast, shot_node_indices, emitted_pulse[0].T)

    def mate(pieces):
        return [lax.ppermute(piece, "depth", mate_route) for piece in pieces]

    def down(piece):
        return lax.ppermute(piece, "depth", down_route)

    rows = shots // HALVES
    start = (extrapolation_operator, impedance_contrast, ascending_residual, arriving_downward_matrices)
    results = first(1, *start, ())
    above = [down(piece) for piece in results[:HALVES]]
    *even, high, low, grad = first(0, *start, results[HALVES:])
    beside = [mate(even[2 * half : 2 * half + 2]) for half in range(HALVES)]
    grads = [grad]

    def odd_step(tick, half):
        odd, grads[0] = step(tick, half, 1, beside[half], shared, high, low, grads[0], rows)
        return down(odd)

    def even_step(tick, half):
        *even, grads[0] = step(tick, half, 0, (above[half],), shared, high, low, grads[0], rows)
        return mate(even)

    for tick in range(1, TICKS - 1):
        later = [odd_step(tick, half) for half in range(HALVES)]
        beside[:] = [even_step(tick, half) for half in range(HALVES)]
        above = later

    scale = 1.0 / math.sqrt(shots * TICKS)
    held, grad = last(0, above[0], beside[0], shared, high, low, grads[0], None)
    chunks = gradient_chunks(above[1], beside[1], shared, grad, scale)
    gradient = chunks[0]
    for distance in range(1, freqs):
        route = [(i, (i + distance) % freqs) for i in range(freqs)]
        gradient = gradient + lax.ppermute(chunks[distance], "freq", route)
    (out,) = last(1, above[1], beside[1], shared, high, low, None, held)
    return (out[None, None], gradient)


def solution(mesh):
    placed = (
        P("freq", "depth", None, None, None),
        P("depth", None),
        P("freq", "depth", None, None, None, None),
        P("freq", "depth", None, None, None),
        P(),
        P("freq", None, None),
    )
    return jax.shard_map(
        local,
        mesh=mesh,
        in_specs=placed,
        out_specs=(P("freq", "depth", None, None, None), P("depth", "freq")),
        check_vma=False,
    )
```

```python
import functools
import math

import jax
import jax.numpy as jnp
from jax import lax
from jax.experimental import pallas as pl
from jax.experimental.pallas import tpu as pltpu
from jax.sharding import PartitionSpec as P

TICKS = 5
HALVES = 2
TAIL = 16
VMEM_LIMIT = 24 * 1024 * 1024
WEIGHTS = {
    "first_0": 30000000,
    "first_1": 200000000,
    "step_1_0_0": 500000000,
    "step_1_0_1": 10000000,
    "step_1_1_0": 30000000,
    "step_2_0_0": 1000000,
    "step_2_0_1": 100000000,
    "step_2_1_0": 30000000,
    "step_2_1_1": 30000000,
    "step_3_0_0": 500000000,
    "step_3_0_1": 1000000,
    "step_3_1_0": 1000000000,
    "step_3_1_1": 1000000,
    "last_0": 1000000000,
    "gradient": 500000000,
}
PARAMS = pltpu.CompilerParams(vmem_limit_bytes=VMEM_LIMIT)
IN_VMEM = pl.BlockSpec(memory_space=pltpu.VMEM)
IN_HBM = pl.BlockSpec(memory_space=pltpu.HBM)


def pinned(value):
    return pltpu.with_memory_space_constraint(value, pltpu.VMEM)


def kept(value):
    return pltpu.with_memory_space_constraint(value, pltpu.HBM)


def cost(kind):
    return pl.CostEstimate(flops=WEIGHTS.get(kind, 1), bytes_accessed=1, transcendentals=0)


def dot(left, right):
    return jnp.dot(left, right, preferred_element_type=jnp.float32)


def is_odd():
    return lax.axis_index("depth") % 2 == 1


def when_parity(parity):
    return pl.when(is_odd() if parity else jnp.logical_not(is_odd()))


def split(value):
    high = value.astype(jnp.bfloat16)
    low = (value - high.astype(jnp.float32)).astype(jnp.bfloat16)
    return high, low


def fold(product):
    return jnp.sum(product.reshape(-1, 8, product.shape[1]), axis=0)


def take(pair, start, waves, contrast, grad_in, grad, left, offset=0):
    count = pair[0].shape[0]
    total = None if grad_in is None else grad_in[...]
    for part in range(2):
        wave = waves[part, pl.ds(start + offset, count)]
        if grad is not None:
            term = fold(pair[part] * wave)
            total = term if total is None else total + term
        if left is not None:
            shots = left.shape[0] // 4
            high, low = split(pair[part] + contrast[...] * wave)
            left[pl.ds(part * shots + offset, count), :] = high
            left[pl.ds((2 + part) * shots + offset, count), :] = low
    if grad is not None:
        grad[...] = total


def multiply(left, high, low, columns):
    shots = left.shape[0] // 4

    def by(part):
        big = dot(left[...], high[part, :, columns])
        small = dot(left[pl.ds(0, 2 * shots), :], low[part, :, columns])
        total = big[: 2 * shots] + (big[2 * shots :] + small)
        return total[:shots], total[shots:]

    real_real, imag_real = by(0)
    real_imag, imag_imag = by(1)
    return real_real - imag_imag, real_imag + imag_real


def injected(tick, start, sites, pulse, shape):
    rows, breadth = shape
    shots = sites.shape[1]
    row = lax.broadcasted_iota(jnp.int32, (rows, shots), 0) + start
    column = lax.broadcasted_iota(jnp.int32, (rows, shots), 1)
    spread = jnp.broadcast_to(sites[pl.ds(tick - 1, 1), :], (rows, shots)).astype(jnp.float32)
    site = jnp.sum(jnp.where(row == column, spread, 0.0), axis=1, keepdims=True)
    lanes = lax.broadcasted_iota(jnp.int32, (rows, breadth), 1).astype(jnp.float32)
    hit = lanes == site
    return [jnp.where(hit, pulse[pl.ds(part, 1), pl.ds(tick - 1, 1)], 0.0) for part in range(2)]


def first_kernel(parity, chained, *refs):
    operator, contrast, residual, panel = refs[:4]
    refs = refs[7:] if chained else refs[4:]
    pieces = 1 if parity else 2 * HALVES
    out = refs[:pieces]
    high, low, grad = refs[pieces : pieces + 3]
    whole, reflect, wave, arrived, left, sems = refs[-6:]
    shots, breadth = arrived.shape[1:]
    depth = breadth // 2

    @when_parity(parity)
    def _():
        copies = [
            pltpu.make_async_copy(contrast, reflect, sems.at[0]),
            pltpu.make_async_copy(residual.at[0, 0, 0], wave, sems.at[1]),
            pltpu.make_async_copy(panel.at[0, 0], arrived, sems.at[2]),
        ]
        pieces = [(part, pl.ds(half * depth, depth)) for half in range(2) for part in range(2)]
        for place, (part, rows) in enumerate(pieces):
            copies.append(
                pltpu.make_async_copy(operator.at[0, 0, part, rows], whole.at[part, rows], sems.at[3 + place])
            )
        for copy in copies:
            copy.start()
        for copy in copies[:3]:
            copy.wait()
        take(arrived, 0, wave, reflect, None, grad, left)
        sums = [None, None]
        for place, (part, rows) in enumerate(pieces):
            copies[3 + place].wait()
            upper, lower = split(whole[part, rows])
            high[part, rows] = upper
            low[part, rows] = lower
            big = dot(left[:, rows], upper)
            small = dot(left[pl.ds(0, 2 * shots), rows], lower)
            total = big[: 2 * shots] + (big[2 * shots :] + small)
            sums[part] = total if sums[part] is None else sums[part] + total
        parts = sums[0][:shots] - sums[1][shots:], sums[1][:shots] + sums[0][shots:]
        store(out, parts)


def store(out, parts):
    start = 0
    for piece in out:
        for part in range(2):
            piece[part] = parts[part][start : start + piece.shape[1]]
        start += piece.shape[1]


def piece_shapes(parity, rows, breadth):
    counts = [rows] if parity else [rows - TAIL, TAIL]
    return tuple(pltpu.VMEM((2, count, breadth), jnp.float32) for count in counts)


def first(parity, operator, contrast, residual, panel, carried):
    shots, breadth = panel.shape[3:]
    half = pltpu.VMEM((2, breadth, breadth), jnp.bfloat16)
    outs = piece_shapes(1, shots, breadth) if parity else piece_shapes(0, shots // HALVES, breadth) * HALVES
    return pl.pallas_call(
        functools.partial(first_kernel, parity, bool(carried)),
        out_shape=(*outs, half, half, pltpu.VMEM((8, breadth), jnp.float32)),
        in_specs=[IN_HBM] * 4 + [IN_VMEM] * len(carried),
        out_specs=(IN_VMEM,) * (len(outs) + 3),
        scratch_shapes=[
            pltpu.VMEM((2, breadth, breadth), jnp.float32),
            pltpu.VMEM((1, breadth), jnp.float32),
            pltpu.VMEM((2, shots, breadth), jnp.float32),
            pltpu.VMEM((2, shots, breadth), jnp.float32),
            pltpu.VMEM((4 * shots, breadth), jnp.bfloat16),
            pltpu.SemaphoreType.DMA((7,)),
        ],
        input_output_aliases={4 + i: len(outs) + i for i in range(len(carried))},
        compiler_params=PARAMS,
        cost_estimate=cost(f"first_{parity}"),
        name=f"first_{parity}",
    )(kept(operator), kept(contrast), kept(residual), kept(panel), *[pinned(value) for value in carried])


def arrive(tick, half, parity, panel, shared, grad_in, grad, left):
    residual, contrast, sites, pulse = shared
    rows = left.shape[0] // 4 if left is not None else sum(piece.shape[1] for piece in panel)
    start = half * rows
    waves = residual.at[0, 0, tick]
    rest = (start, waves, contrast, grad_in, grad, left)
    if parity:
        take(panel[0], *rest)
        take(panel[1], start, waves, contrast, grad, grad, left, panel[0].shape[1])
        return
    surface = lax.axis_index("depth") == 0

    piece = panel[0]
    if piece.shape[1] > rows:
        piece = piece.at[:, pl.ds(start, rows)]

    @pl.when(surface)
    def _():
        take(injected(tick, start, sites, pulse, (rows, piece.shape[2])), *rest)

    @pl.when(jnp.logical_not(surface))
    def _():
        take(piece, *rest)


def arrive_either(half, above, mate, shared, grad_in, grad, left):
    @when_parity(1)
    def _():
        arrive(TICKS - 1, half, 1, mate, shared, grad_in, grad, left)

    @when_parity(0)
    def _():
        arrive(TICKS - 1, half, 0, (above,), shared, grad_in, grad, left)


def step_kernel(tick, half, parity, *refs):
    panel, refs = refs[: 1 + parity], refs[1 + parity :]
    shared, (high, low, grad_in) = refs[:4], refs[4:7]
    *out, grad, left = refs[7:]

    @when_parity(parity)
    def _():
        arrive(tick, half, parity, panel, shared, grad_in, grad, left)
        store(out, multiply(left, high, low, slice(None)))


def step(tick, half, parity, panel, shared, high, low, grad, rows):
    breadth = grad.shape[1]
    outs = piece_shapes(parity, rows, breadth)
    operands = [pinned(value) for value in (*panel, *shared, high, low, grad)]
    return pl.pallas_call(
        functools.partial(step_kernel, tick, half, parity),
        out_shape=(*outs, pltpu.VMEM(grad.shape, jnp.float32)),
        in_specs=[IN_VMEM] * len(operands),
        out_specs=(IN_VMEM,) * (len(outs) + 1),
        scratch_shapes=[pltpu.VMEM((4 * rows, breadth), jnp.bfloat16)],
        input_output_aliases={len(operands) - 1: len(outs)},
        compiler_params=PARAMS,
        cost_estimate=cost(f"step_{tick}_{half}_{parity}"),
        name=f"step_{tick}_{half}_{parity}",
    )(*operands)


def gradient_chunks(above, mate, shared, grad, scale):
    breadth = grad.shape[1]
    count = lax.axis_size("freq")
    width = breadth // count

    def body(above, mate, mate_tail, residual, contrast, sites, pulse, grad_in, *refs):
        chunks, total = refs[:count], refs[count]
        arrive_either(HALVES - 1, above, (mate, mate_tail), (residual, contrast, sites, pulse), grad_in, total, None)
        gradient = jnp.sum(total[...], axis=0, keepdims=True) * scale
        me = lax.axis_index("freq")
        for distance in range(count):
            owner = lax.rem(me + distance, count)
            chunk = jnp.zeros((1, width), jnp.float32)
            for place in range(count):
                piece = gradient[:, place * width : (place + 1) * width]
                chunk = jnp.where(owner == place, piece, chunk)
            chunks[distance][...] = chunk

    operands = [pinned(value) for value in (above, *mate, *shared, grad)]
    return pl.pallas_call(
        body,
        out_shape=(pltpu.VMEM((1, width), jnp.float32),) * count,
        in_specs=[IN_VMEM] * len(operands),
        out_specs=(IN_VMEM,) * count,
        scratch_shapes=[pltpu.VMEM(grad.shape, jnp.float32)],
        compiler_params=PARAMS,
        cost_estimate=cost("gradient"),
        name="gradient",
    )(*operands)


def last_kernel(half, above, mate, mate_tail, *refs):
    shared, high, low = refs[:4], refs[4], refs[5]
    if half == 0:
        grad_in, held, grad, left = refs[6:]
        arrive_either(half, above, (mate, mate_tail), shared, grad_in, grad, left)
        held[0], held[1] = multiply(left, high, low, slice(None))
        return
    before, out, left, held, sems = refs[6:]
    rows = held.shape[1]
    copies = [
        pltpu.make_async_copy(piece, out.at[:, pl.ds(place * rows, rows)], sems.at[place])
        for place, piece in enumerate((before, held))
    ]
    copies[0].start()
    arrive_either(half, above, (mate, mate_tail), shared, None, None, left)
    held[0], held[1] = multiply(left, high, low, slice(None))
    copies[1].start()
    for copy in copies:
        copy.wait()


def last(half, above, mate, shared, high, low, grad, held):
    rows, breadth = above.shape[1:]
    left = pltpu.VMEM((4 * rows, breadth), jnp.bfloat16)
    piece = pltpu.VMEM((2, rows, breadth), jnp.float32)
    if half == 0:
        out_shape, out_specs, scratch, aliases = (piece, pltpu.VMEM(grad.shape, jnp.float32)), (IN_VMEM,) * 2, [left], {9: 1}
    else:
        out_shape, out_specs, aliases = (pltpu.HBM((2, rows * HALVES, breadth), jnp.float32),), (IN_HBM,), {}
        scratch = [left, piece, pltpu.SemaphoreType.DMA((HALVES,))]
    operands = [pinned(value) for value in (above, *mate, *shared, high, low, grad if half == 0 else held)]
    return pl.pallas_call(
        functools.partial(last_kernel, half),
        out_shape=out_shape,
        in_specs=[IN_VMEM] * len(operands),
        out_specs=out_specs,
        scratch_shapes=scratch,
        input_output_aliases=aliases,
        compiler_params=PARAMS,
        cost_estimate=cost(f"last_{half}"),
        name=f"last_{half}",
    )(*operands)


def cross_route(levels):
    route = {level: (level + 1) % levels for level in range(levels)}
    chips = levels // 2
    if chips % 2 == 0:
        for chip in range(chips - 1, 1, -2):
            route[levels - 1 if chip == chips - 1 else 2 * chip] = 2 * (chip - 2) + 1
        route[2 if chips > 2 else levels - 1] = 0
    return sorted(route.items())


def local(
    extrapolation_operator,
    impedance_contrast,
    ascending_residual,
    arriving_downward_matrices,
    shot_node_indices,
    emitted_pulse,
):
    levels = lax.axis_size("depth")
    freqs = lax.axis_size("freq")
    shots = arriving_downward_matrices.shape[3]
    mate_route = [(level, level ^ 1) for level in range(levels)]
    down_route = cross_route(levels)
    open_route = [(level, level + 1) for level in range(1, levels - 1, 2)]
    shared = (ascending_residual, impedance_contrast, shot_node_indices, emitted_pulse[0].T)

    def mate(pieces):
        return [lax.ppermute(piece, "depth", mate_route) for piece in pieces]

    def down(piece, closed=True):
        return lax.ppermute(piece, "depth", down_route if closed else open_route)

    rows = shots // HALVES
    start = (extrapolation_operator, impedance_contrast, ascending_residual, arriving_downward_matrices)
    odd, *carried = first(1, *start, ())
    above = [down(odd, closed=False)] * HALVES
    *even, high, low, grad = first(0, *start, carried)
    beside = [mate(even[2 * half : 2 * half + 2]) for half in range(HALVES)]
    grads = [grad]

    def odd_step(tick, half):
        odd, grads[0] = step(tick, half, 1, beside[half], shared, high, low, grads[0], rows)
        return down(odd, closed=tick < TICKS - 2 or half < HALVES - 1)

    def even_step(tick, half):
        *even, grads[0] = step(tick, half, 0, (above[half],), shared, high, low, grads[0], rows)
        return mate(even)

    for tick in range(1, TICKS - 1):
        later = [odd_step(tick, half) for half in range(HALVES)]
        beside[:] = [even_step(tick, half) for half in range(HALVES)]
        above = later

    scale = 1.0 / math.sqrt(shots * TICKS)
    held, grad = last(0, above[0], beside[0], shared, high, low, grads[0], None)
    chunks = gradient_chunks(above[1], beside[1], shared, grad, scale)
    gradient = chunks[0]
    for distance in range(1, freqs):
        route = [(i, (i + distance) % freqs) for i in range(freqs)]
        gradient = gradient + lax.ppermute(chunks[distance], "freq", route)
    (out,) = last(1, above[1], beside[1], shared, high, low, None, held)
    return (out[None, None], gradient)


def solution(mesh):
    placed = (
        P("freq", "depth", None, None, None),
        P("depth", None),
        P("freq", "depth", None, None, None, None),
        P("freq", "depth", None, None, None),
        P(),
        P("freq", None, None),
    )
    return jax.shard_map(
        local,
        mesh=mesh,
        in_specs=placed,
        out_specs=(P("freq", "depth", None, None, None), P("depth", "freq")),
        check_vma=False,
    )
```

```python
import functools
import math

import jax
import jax.numpy as jnp
from jax import lax
from jax.experimental import pallas as pl
from jax.experimental.pallas import tpu as pltpu
from jax.sharding import PartitionSpec as P

TICKS = 5
HALVES = 2
TAIL = 16
VMEM_LIMIT = 24 * 1024 * 1024
WEIGHTS = {
    "first_0": 30000000,
    "first_1": 30000000,
    "step_1_0_0": 1000000,
    "step_1_1_0": 1000000,
    "step_2_0_0": 1000000,
    "step_2_1_0": 1000000000,
    "step_2_1_1": 500000000,
    "step_3_0_0": 1000000,
    "step_3_0_1": 500000000,
    "step_3_1_0": 500000000,
    "step_3_1_1": 1000000,
    "last_0": 30000000,
    "gradient": 100000000,
}
PARAMS = pltpu.CompilerParams(vmem_limit_bytes=VMEM_LIMIT)
IN_VMEM = pl.BlockSpec(memory_space=pltpu.VMEM)
IN_HBM = pl.BlockSpec(memory_space=pltpu.HBM)


def pinned(value):
    return pltpu.with_memory_space_constraint(value, pltpu.VMEM)


def kept(value):
    return pltpu.with_memory_space_constraint(value, pltpu.HBM)


def cost(kind):
    return pl.CostEstimate(flops=WEIGHTS.get(kind, 1), bytes_accessed=1, transcendentals=0)


def dot(left, right):
    return jnp.dot(left, right, preferred_element_type=jnp.float32)


def is_odd():
    return lax.axis_index("depth") % 2 == 1


def when_parity(parity):
    return pl.when(is_odd() if parity else jnp.logical_not(is_odd()))


def split(value):
    high = value.astype(jnp.bfloat16)
    low = (value - high.astype(jnp.float32)).astype(jnp.bfloat16)
    return high, low


def fold(product):
    return jnp.sum(product.reshape(-1, 8, product.shape[1]), axis=0)


def take(pair, start, waves, contrast, grad_in, grad, left, offset=0):
    count = pair[0].shape[0]
    total = None if grad_in is None else grad_in[...]
    for part in range(2):
        wave = waves[part, pl.ds(start + offset, count)]
        if grad is not None:
            term = fold(pair[part] * wave)
            total = term if total is None else total + term
        if left is not None:
            shots = left.shape[0] // 4
            high, low = split(pair[part] + contrast[...] * wave)
            left[pl.ds(part * shots + offset, count), :] = high
            left[pl.ds((2 + part) * shots + offset, count), :] = low
    if grad is not None:
        grad[...] = total


def multiply(left, high, low, columns):
    shots = left.shape[0] // 4

    def by(part):
        big = dot(left[...], high[part, :, columns])
        small = dot(left[pl.ds(0, 2 * shots), :], low[part, :, columns])
        total = big[: 2 * shots] + (big[2 * shots :] + small)
        return total[:shots], total[shots:]

    real_real, imag_real = by(0)
    real_imag, imag_imag = by(1)
    return real_real - imag_imag, real_imag + imag_real


def injected(tick, start, sites, pulse, shape):
    rows, breadth = shape
    shots = sites.shape[1]
    row = lax.broadcasted_iota(jnp.int32, (rows, shots), 0) + start
    column = lax.broadcasted_iota(jnp.int32, (rows, shots), 1)
    spread = jnp.broadcast_to(sites[pl.ds(tick - 1, 1), :], (rows, shots)).astype(jnp.float32)
    site = jnp.sum(jnp.where(row == column, spread, 0.0), axis=1, keepdims=True)
    lanes = lax.broadcasted_iota(jnp.int32, (rows, breadth), 1).astype(jnp.float32)
    hit = lanes == site
    return [jnp.where(hit, pulse[pl.ds(part, 1), pl.ds(tick - 1, 1)], 0.0) for part in range(2)]


def first_kernel(parity, chained, *refs):
    operator, contrast, residual, panel = refs[:4]
    refs = refs[7:] if chained else refs[4:]
    pieces = HALVES * (2 - parity)
    out = refs[:pieces]
    high, low, grad = refs[pieces : pieces + 3]
    whole, reflect, wave, arrived, left, sems = refs[-6:]
    shots, breadth = arrived.shape[1:]
    depth = breadth // 2

    @when_parity(parity)
    def _():
        copies = [
            pltpu.make_async_copy(contrast, reflect, sems.at[0]),
            pltpu.make_async_copy(residual.at[0, 0, 0], wave, sems.at[1]),
            pltpu.make_async_copy(panel.at[0, 0], arrived, sems.at[2]),
        ]
        pieces = [(part, pl.ds(half * depth, depth)) for half in range(2) for part in range(2)]
        for place, (part, rows) in enumerate(pieces):
            copies.append(
                pltpu.make_async_copy(operator.at[0, 0, part, rows], whole.at[part, rows], sems.at[3 + place])
            )
        for copy in copies:
            copy.start()
        for copy in copies[:3]:
            copy.wait()
        take(arrived, 0, wave, reflect, None, grad, left)
        sums = [None, None]
        for place, (part, rows) in enumerate(pieces):
            copies[3 + place].wait()
            upper, lower = split(whole[part, rows])
            high[part, rows] = upper
            low[part, rows] = lower
            big = dot(left[:, rows], upper)
            small = dot(left[pl.ds(0, 2 * shots), rows], lower)
            total = big[: 2 * shots] + (big[2 * shots :] + small)
            sums[part] = total if sums[part] is None else sums[part] + total
        parts = sums[0][:shots] - sums[1][shots:], sums[1][:shots] + sums[0][shots:]
        store(out, parts)


def store(out, parts):
    start = 0
    for piece in out:
        for part in range(2):
            piece[part] = parts[part][start : start + piece.shape[1]]
        start += piece.shape[1]


def piece_shapes(parity, rows, breadth):
    counts = [rows] if parity else [rows - TAIL, TAIL]
    return tuple(pltpu.VMEM((2, count, breadth), jnp.float32) for count in counts)


def first(parity, operator, contrast, residual, panel, carried):
    shots, breadth = panel.shape[3:]
    half = pltpu.VMEM((2, breadth, breadth), jnp.bfloat16)
    outs = piece_shapes(parity, shots // HALVES, breadth) * HALVES
    return pl.pallas_call(
        functools.partial(first_kernel, parity, bool(carried)),
        out_shape=(*outs, half, half, pltpu.VMEM((8, breadth), jnp.float32)),
        in_specs=[IN_HBM] * 4 + [IN_VMEM] * len(carried),
        out_specs=(IN_VMEM,) * (len(outs) + 3),
        scratch_shapes=[
            pltpu.VMEM((2, breadth, breadth), jnp.float32),
            pltpu.VMEM((1, breadth), jnp.float32),
            pltpu.VMEM((2, shots, breadth), jnp.float32),
            pltpu.VMEM((2, shots, breadth), jnp.float32),
            pltpu.VMEM((4 * shots, breadth), jnp.bfloat16),
            pltpu.SemaphoreType.DMA((7,)),
        ],
        input_output_aliases={4 + i: len(outs) + i for i in range(len(carried))},
        compiler_params=PARAMS,
        cost_estimate=cost(f"first_{parity}"),
        name=f"first_{parity}",
    )(kept(operator), kept(contrast), kept(residual), kept(panel), *[pinned(value) for value in carried])


def arrive(tick, half, parity, panel, shared, grad_in, grad, left):
    residual, contrast, sites, pulse = shared
    rows = sum(piece.shape[1] for piece in panel)
    start = half * rows
    waves = residual.at[0, 0, tick]
    rest = (start, waves, contrast, grad_in, grad, left)
    if parity:
        take(panel[0], *rest)
        take(panel[1], start, waves, contrast, grad, grad, left, panel[0].shape[1])
        return
    surface = lax.axis_index("depth") == 0

    @pl.when(surface)
    def _():
        take(injected(tick, start, sites, pulse, panel[0].shape[1:]), *rest)

    @pl.when(jnp.logical_not(surface))
    def _():
        take(panel[0], *rest)


def arrive_either(half, above, mate, shared, grad_in, grad, left):
    @when_parity(1)
    def _():
        arrive(TICKS - 1, half, 1, mate, shared, grad_in, grad, left)

    @when_parity(0)
    def _():
        arrive(TICKS - 1, half, 0, (above,), shared, grad_in, grad, left)


def step_kernel(tick, half, parity, *refs):
    panel, refs = refs[: 1 + parity], refs[1 + parity :]
    shared, (high, low, grad_in) = refs[:4], refs[4:7]
    *out, grad, left = refs[7:]

    @when_parity(parity)
    def _():
        arrive(tick, half, parity, panel, shared, grad_in, grad, left)
        store(out, multiply(left, high, low, slice(None)))


def step(tick, half, parity, panel, shared, high, low, grad, rows):
    breadth = grad.shape[1]
    outs = piece_shapes(parity, rows, breadth)
    operands = [pinned(value) for value in (*panel, *shared, high, low, grad)]
    return pl.pallas_call(
        functools.partial(step_kernel, tick, half, parity),
        out_shape=(*outs, pltpu.VMEM(grad.shape, jnp.float32)),
        in_specs=[IN_VMEM] * len(operands),
        out_specs=(IN_VMEM,) * (len(outs) + 1),
        scratch_shapes=[pltpu.VMEM((4 * rows, breadth), jnp.bfloat16)],
        input_output_aliases={len(operands) - 1: len(outs)},
        compiler_params=PARAMS,
        cost_estimate=cost(f"step_{tick}_{half}_{parity}"),
        name=f"step_{tick}_{half}_{parity}",
    )(*operands)


def gradient_chunks(above, mate, shared, grad, scale):
    breadth = grad.shape[1]
    count = lax.axis_size("freq")
    width = breadth // count

    def body(above, mate, mate_tail, residual, contrast, sites, pulse, grad_in, *refs):
        chunks, total = refs[:count], refs[count]
        arrive_either(HALVES - 1, above, (mate, mate_tail), (residual, contrast, sites, pulse), grad_in, total, None)
        gradient = jnp.sum(total[...], axis=0, keepdims=True) * scale
        me = lax.axis_index("freq")
        for distance in range(count):
            owner = lax.rem(me + distance, count)
            chunk = jnp.zeros((1, width), jnp.float32)
            for place in range(count):
                piece = gradient[:, place * width : (place + 1) * width]
                chunk = jnp.where(owner == place, piece, chunk)
            chunks[distance][...] = chunk

    operands = [pinned(value) for value in (above, *mate, *shared, grad)]
    return pl.pallas_call(
        body,
        out_shape=(pltpu.VMEM((1, width), jnp.float32),) * count,
        in_specs=[IN_VMEM] * len(operands),
        out_specs=(IN_VMEM,) * count,
        scratch_shapes=[pltpu.VMEM(grad.shape, jnp.float32)],
        compiler_params=PARAMS,
        cost_estimate=cost("gradient"),
        name="gradient",
    )(*operands)


def last_kernel(half, above, mate, mate_tail, *refs):
    shared, high, low = refs[:4], refs[4], refs[5]
    if half == 0:
        grad_in, held, grad, left = refs[6:]
        arrive_either(half, above, (mate, mate_tail), shared, grad_in, grad, left)
        held[0], held[1] = multiply(left, high, low, slice(None))
        return
    before, out, left, held, sems = refs[6:]
    rows = held.shape[1]
    copies = [
        pltpu.make_async_copy(piece, out.at[:, pl.ds(place * rows, rows)], sems.at[place])
        for place, piece in enumerate((before, held))
    ]
    copies[0].start()
    arrive_either(half, above, (mate, mate_tail), shared, None, None, left)
    held[0], held[1] = multiply(left, high, low, slice(None))
    copies[1].start()
    for copy in copies:
        copy.wait()


def last(half, above, mate, shared, high, low, grad, held):
    rows, breadth = above.shape[1:]
    left = pltpu.VMEM((4 * rows, breadth), jnp.bfloat16)
    piece = pltpu.VMEM((2, rows, breadth), jnp.float32)
    if half == 0:
        out_shape, out_specs, scratch, aliases = (piece, pltpu.VMEM(grad.shape, jnp.float32)), (IN_VMEM,) * 2, [left], {9: 1}
    else:
        out_shape, out_specs, aliases = (pltpu.HBM((2, rows * HALVES, breadth), jnp.float32),), (IN_HBM,), {}
        scratch = [left, piece, pltpu.SemaphoreType.DMA((HALVES,))]
    operands = [pinned(value) for value in (above, *mate, *shared, high, low, grad if half == 0 else held)]
    return pl.pallas_call(
        functools.partial(last_kernel, half),
        out_shape=out_shape,
        in_specs=[IN_VMEM] * len(operands),
        out_specs=out_specs,
        scratch_shapes=scratch,
        input_output_aliases=aliases,
        compiler_params=PARAMS,
        cost_estimate=cost(f"last_{half}"),
        name=f"last_{half}",
    )(*operands)


def cross_route(levels):
    route = {level: (level + 1) % levels for level in range(levels)}
    chips = levels // 2
    if chips % 2 == 0:
        for chip in range(chips - 1, 1, -2):
            route[levels - 1 if chip == chips - 1 else 2 * chip] = 2 * (chip - 2) + 1
        route[2 if chips > 2 else levels - 1] = 0
    return sorted(route.items())


def local(
    extrapolation_operator,
    impedance_contrast,
    ascending_residual,
    arriving_downward_matrices,
    shot_node_indices,
    emitted_pulse,
):
    levels = lax.axis_size("depth")
    freqs = lax.axis_size("freq")
    shots = arriving_downward_matrices.shape[3]
    mate_route = [(level, level ^ 1) for level in range(levels)]
    down_route = cross_route(levels)
    open_route = [(level, level + 1) for level in range(1, levels - 1, 2)]
    shared = (ascending_residual, impedance_contrast, shot_node_indices, emitted_pulse[0].T)

    def mate(pieces):
        return [lax.ppermute(piece, "depth", mate_route) for piece in pieces]

    def down(piece, closed=True):
        return lax.ppermute(piece, "depth", down_route if closed else open_route)

    rows = shots // HALVES
    start = (extrapolation_operator, impedance_contrast, ascending_residual, arriving_downward_matrices)
    results = first(1, *start, ())
    above = [down(piece) for piece in results[:HALVES]]
    *even, high, low, grad = first(0, *start, results[HALVES:])
    beside = [mate(even[2 * half : 2 * half + 2]) for half in range(HALVES)]
    grads = [grad]

    def odd_step(tick, half):
        odd, grads[0] = step(tick, half, 1, beside[half], shared, high, low, grads[0], rows)
        return down(odd, closed=tick < TICKS - 2 or half < HALVES - 1)

    def even_step(tick, half):
        *even, grads[0] = step(tick, half, 0, (above[half],), shared, high, low, grads[0], rows)
        return mate(even)

    for tick in range(1, TICKS - 1):
        later = [odd_step(tick, half) for half in range(HALVES)]
        beside[:] = [even_step(tick, half) for half in range(HALVES)]
        above = later

    scale = 1.0 / math.sqrt(shots * TICKS)
    held, grad = last(0, above[0], beside[0], shared, high, low, grads[0], None)
    chunks = gradient_chunks(above[1], beside[1], shared, grad, scale)
    gradient = chunks[0]
    for distance in range(1, freqs):
        route = [(i, (i + distance) % freqs) for i in range(freqs)]
        gradient = gradient + lax.ppermute(chunks[distance], "freq", route)
    (out,) = last(1, above[1], beside[1], shared, high, low, None, held)
    return (out[None, None], gradient)


def solution(mesh):
    placed = (
        P("freq", "depth", None, None, None),
        P("depth", None),
        P("freq", "depth", None, None, None, None),
        P("freq", "depth", None, None, None),
        P(),
        P("freq", None, None),
    )
    return jax.shard_map(
        local,
        mesh=mesh,
        in_specs=placed,
        out_specs=(P("freq", "depth", None, None, None), P("depth", "freq")),
        check_vma=False,
    )
```

```python
import functools
import math

import jax
import jax.numpy as jnp
from jax import lax
from jax.experimental import pallas as pl
from jax.experimental.pallas import tpu as pltpu
from jax.sharding import PartitionSpec as P

TICKS = 5
HALVES = 2
TAIL = 16
VMEM_LIMIT = 24 * 1024 * 1024
WEIGHTS = {
    "first_0": 500000000,
    "first_1": 1000000000,
    "step_1_0_0": 1000000,
    "step_1_0_1": 1000000000,
    "step_1_1_0": 1000000000,
    "step_1_1_1": 30000000,
    "step_2_0_0": 10000000,
    "step_2_0_1": 1000000,
    "step_2_1_0": 30000000,
    "step_2_1_1": 30000000,
    "step_3_0_0": 10000000,
    "step_3_0_1": 30000000,
    "step_3_1_0": 200000000,
    "last_0": 100000000,
    "gradient": 200000000,
}
PARAMS = pltpu.CompilerParams(vmem_limit_bytes=VMEM_LIMIT)
IN_VMEM = pl.BlockSpec(memory_space=pltpu.VMEM)
IN_HBM = pl.BlockSpec(memory_space=pltpu.HBM)


def pinned(value):
    return pltpu.with_memory_space_constraint(value, pltpu.VMEM)


def kept(value):
    return pltpu.with_memory_space_constraint(value, pltpu.HBM)


def cost(kind):
    return pl.CostEstimate(flops=WEIGHTS.get(kind, 1), bytes_accessed=1, transcendentals=0)


def dot(left, right):
    return jnp.dot(left, right, preferred_element_type=jnp.float32)


def is_odd():
    return lax.axis_index("depth") % 2 == 1


def when_parity(parity):
    return pl.when(is_odd() if parity else jnp.logical_not(is_odd()))


def split(value):
    high = value.astype(jnp.bfloat16)
    low = (value - high.astype(jnp.float32)).astype(jnp.bfloat16)
    return high, low


def fold(product):
    return jnp.sum(product.reshape(-1, 8, product.shape[1]), axis=0)


def take(pair, start, waves, contrast, grad_in, grad, left, offset=0):
    count = pair[0].shape[0]
    total = None if grad_in is None else grad_in[...]
    for part in range(2):
        wave = waves[part, pl.ds(start + offset, count)]
        if grad is not None:
            term = fold(pair[part] * wave)
            total = term if total is None else total + term
        if left is not None:
            shots = left.shape[0] // 4
            high, low = split(pair[part] + contrast[...] * wave)
            left[pl.ds(part * shots + offset, count), :] = high
            left[pl.ds((2 + part) * shots + offset, count), :] = low
    if grad is not None:
        grad[...] = total


def multiply(left, high, low, columns):
    shots = left.shape[0] // 4

    def by(part):
        big = dot(left[...], high[part, :, columns])
        small = dot(left[pl.ds(0, 2 * shots), :], low[part, :, columns])
        total = big[: 2 * shots] + (big[2 * shots :] + small)
        return total[:shots], total[shots:]

    real_real, imag_real = by(0)
    real_imag, imag_imag = by(1)
    return real_real - imag_imag, real_imag + imag_real


def injected(tick, start, sites, pulse, shape):
    rows, breadth = shape
    shots = sites.shape[1]
    row = lax.broadcasted_iota(jnp.int32, (rows, shots), 0) + start
    column = lax.broadcasted_iota(jnp.int32, (rows, shots), 1)
    spread = jnp.broadcast_to(sites[pl.ds(tick - 1, 1), :], (rows, shots)).astype(jnp.float32)
    site = jnp.sum(jnp.where(row == column, spread, 0.0), axis=1, keepdims=True)
    lanes = lax.broadcasted_iota(jnp.int32, (rows, breadth), 1).astype(jnp.float32)
    hit = lanes == site
    return [jnp.where(hit, pulse[pl.ds(part, 1), pl.ds(tick - 1, 1)], 0.0) for part in range(2)]


def first_kernel(parity, chained, *refs):
    operator, contrast, residual, panel = refs[:4]
    refs = refs[7:] if chained else refs[4:]
    pieces = HALVES * (2 - parity)
    out = refs[:pieces]
    high, low, grad = refs[pieces : pieces + 3]
    whole, reflect, wave, arrived, left, sems = refs[-6:]
    shots, breadth = arrived.shape[1:]
    depth = breadth // 2

    @when_parity(parity)
    def _():
        copies = [
            pltpu.make_async_copy(contrast, reflect, sems.at[0]),
            pltpu.make_async_copy(residual.at[0, 0, 0], wave, sems.at[1]),
            pltpu.make_async_copy(panel.at[0, 0], arrived, sems.at[2]),
        ]
        pieces = [(part, pl.ds(half * depth, depth)) for half in range(2) for part in range(2)]
        for place, (part, rows) in enumerate(pieces):
            copies.append(
                pltpu.make_async_copy(operator.at[0, 0, part, rows], whole.at[part, rows], sems.at[3 + place])
            )
        for copy in copies:
            copy.start()
        for copy in copies[:3]:
            copy.wait()
        take(arrived, 0, wave, reflect, None, grad, left)
        sums = [None, None]
        for place, (part, rows) in enumerate(pieces):
            copies[3 + place].wait()
            upper, lower = split(whole[part, rows])
            high[part, rows] = upper
            low[part, rows] = lower
            big = dot(left[:, rows], upper)
            small = dot(left[pl.ds(0, 2 * shots), rows], lower)
            total = big[: 2 * shots] + (big[2 * shots :] + small)
            sums[part] = total if sums[part] is None else sums[part] + total
        parts = sums[0][:shots] - sums[1][shots:], sums[1][:shots] + sums[0][shots:]
        store(out, parts)


def store(out, parts):
    start = 0
    for piece in out:
        for part in range(2):
            piece[part] = parts[part][start : start + piece.shape[1]]
        start += piece.shape[1]


def piece_shapes(parity, rows, breadth):
    counts = [rows] if parity else [rows - TAIL, TAIL]
    return tuple(pltpu.VMEM((2, count, breadth), jnp.float32) for count in counts)


def first(parity, operator, contrast, residual, panel, carried):
    shots, breadth = panel.shape[3:]
    half = pltpu.VMEM((2, breadth, breadth), jnp.bfloat16)
    outs = piece_shapes(parity, shots // HALVES, breadth) * HALVES
    return pl.pallas_call(
        functools.partial(first_kernel, parity, bool(carried)),
        out_shape=(*outs, half, half, pltpu.VMEM((8, breadth), jnp.float32)),
        in_specs=[IN_HBM] * 4 + [IN_VMEM] * len(carried),
        out_specs=(IN_VMEM,) * (len(outs) + 3),
        scratch_shapes=[
            pltpu.VMEM((2, breadth, breadth), jnp.float32),
            pltpu.VMEM((1, breadth), jnp.float32),
            pltpu.VMEM((2, shots, breadth), jnp.float32),
            pltpu.VMEM((2, shots, breadth), jnp.float32),
            pltpu.VMEM((4 * shots, breadth), jnp.bfloat16),
            pltpu.SemaphoreType.DMA((7,)),
        ],
        input_output_aliases={4 + i: len(outs) + i for i in range(len(carried))},
        compiler_params=PARAMS,
        cost_estimate=cost(f"first_{parity}"),
        name=f"first_{parity}",
    )(kept(operator), kept(contrast), kept(residual), kept(panel), *[pinned(value) for value in carried])


def arrive(tick, start, parity, pieces, shared, grad_in, grad, left):
    residual, contrast, sites, pulse = shared
    waves = residual.at[0, 0, tick]

    def take_pieces():
        offset = 0
        for piece in pieces:
            take(piece, start, waves, contrast, grad if offset else grad_in, grad, left, offset)
            offset += piece.shape[1]

    if parity:
        take_pieces()
        return
    surface = lax.axis_index("depth") == 0
    shape = sum(piece.shape[1] for piece in pieces), pieces[0].shape[2]

    @pl.when(surface)
    def _():
        take(injected(tick, start, sites, pulse, shape), start, waves, contrast, grad_in, grad, left)

    pl.when(jnp.logical_not(surface))(take_pieces)


def arrive_either(half, above, mate, shared, grad_in, grad, left):
    start = half * above.shape[1]

    @when_parity(1)
    def _():
        arrive(TICKS - 1, start, 1, mate, shared, grad_in, grad, left)

    @when_parity(0)
    def _():
        arrive(TICKS - 1, start, 0, (above,), shared, grad_in, grad, left)


def step_kernel(tick, start, parity, count, *refs):
    pieces, refs = refs[:count], refs[count:]
    shared, (high, low, grad_in) = refs[:4], refs[4:7]
    *out, grad, left = refs[7:]

    @when_parity(parity)
    def _():
        arrive(tick, start, parity, pieces, shared, grad_in, grad, left)
        store(out, multiply(left, high, low, slice(None)))


def step(tick, start, parity, pieces, shared, high, low, grad, half):
    breadth = grad.shape[1]
    rows = sum(piece.shape[1] for piece in pieces)
    outs = piece_shapes(1, rows, breadth) if parity else piece_shapes(0, half, breadth) * (rows // half)
    operands = [pinned(value) for value in (*pieces, *shared, high, low, grad)]
    return pl.pallas_call(
        functools.partial(step_kernel, tick, start, parity, len(pieces)),
        out_shape=(*outs, pltpu.VMEM(grad.shape, jnp.float32)),
        in_specs=[IN_VMEM] * len(operands),
        out_specs=(IN_VMEM,) * (len(outs) + 1),
        scratch_shapes=[pltpu.VMEM((4 * rows, breadth), jnp.bfloat16)],
        input_output_aliases={len(operands) - 1: len(outs)},
        compiler_params=PARAMS,
        cost_estimate=cost(f"step_{tick}_{start // half}_{parity}"),
        name=f"step_{tick}_{start // half}_{parity}",
    )(*operands)


def gradient_chunks(above, mate, shared, grad, scale):
    breadth = grad.shape[1]
    count = lax.axis_size("freq")
    width = breadth // count

    def body(above, mate, mate_tail, residual, contrast, sites, pulse, grad_in, *refs):
        chunks, total = refs[:count], refs[count]
        arrive_either(HALVES - 1, above, (mate, mate_tail), (residual, contrast, sites, pulse), grad_in, total, None)
        gradient = jnp.sum(total[...], axis=0, keepdims=True) * scale
        me = lax.axis_index("freq")
        for distance in range(count):
            owner = lax.rem(me + distance, count)
            chunk = jnp.zeros((1, width), jnp.float32)
            for place in range(count):
                piece = gradient[:, place * width : (place + 1) * width]
                chunk = jnp.where(owner == place, piece, chunk)
            chunks[distance][...] = chunk

    operands = [pinned(value) for value in (above, *mate, *shared, grad)]
    return pl.pallas_call(
        body,
        out_shape=(pltpu.VMEM((1, width), jnp.float32),) * count,
        in_specs=[IN_VMEM] * len(operands),
        out_specs=(IN_VMEM,) * count,
        scratch_shapes=[pltpu.VMEM(grad.shape, jnp.float32)],
        compiler_params=PARAMS,
        cost_estimate=cost("gradient"),
        name="gradient",
    )(*operands)


def last_kernel(half, above, mate, mate_tail, *refs):
    shared, high, low = refs[:4], refs[4], refs[5]
    if half == 0:
        grad_in, held, grad, left = refs[6:]
        arrive_either(half, above, (mate, mate_tail), shared, grad_in, grad, left)
        held[0], held[1] = multiply(left, high, low, slice(None))
        return
    before, out, left, held, sems = refs[6:]
    rows = held.shape[1]
    copies = [
        pltpu.make_async_copy(piece, out.at[:, pl.ds(place * rows, rows)], sems.at[place])
        for place, piece in enumerate((before, held))
    ]
    copies[0].start()
    arrive_either(half, above, (mate, mate_tail), shared, None, None, left)
    held[0], held[1] = multiply(left, high, low, slice(None))
    copies[1].start()
    for copy in copies:
        copy.wait()


def last(half, above, mate, shared, high, low, grad, held):
    rows, breadth = above.shape[1:]
    left = pltpu.VMEM((4 * rows, breadth), jnp.bfloat16)
    piece = pltpu.VMEM((2, rows, breadth), jnp.float32)
    if half == 0:
        out_shape, out_specs, scratch, aliases = (piece, pltpu.VMEM(grad.shape, jnp.float32)), (IN_VMEM,) * 2, [left], {9: 1}
    else:
        out_shape, out_specs, aliases = (pltpu.HBM((2, rows * HALVES, breadth), jnp.float32),), (IN_HBM,), {}
        scratch = [left, piece, pltpu.SemaphoreType.DMA((HALVES,))]
    operands = [pinned(value) for value in (above, *mate, *shared, high, low, grad if half == 0 else held)]
    return pl.pallas_call(
        functools.partial(last_kernel, half),
        out_shape=out_shape,
        in_specs=[IN_VMEM] * len(operands),
        out_specs=out_specs,
        scratch_shapes=scratch,
        input_output_aliases=aliases,
        compiler_params=PARAMS,
        cost_estimate=cost(f"last_{half}"),
        name=f"last_{half}",
    )(*operands)


def cross_route(levels):
    route = {level: (level + 1) % levels for level in range(levels)}
    chips = levels // 2
    if chips % 2 == 0:
        for chip in range(chips - 1, 1, -2):
            route[levels - 1 if chip == chips - 1 else 2 * chip] = 2 * (chip - 2) + 1
        route[2 if chips > 2 else levels - 1] = 0
    return sorted(route.items())


def local(
    extrapolation_operator,
    impedance_contrast,
    ascending_residual,
    arriving_downward_matrices,
    shot_node_indices,
    emitted_pulse,
):
    levels = lax.axis_size("depth")
    freqs = lax.axis_size("freq")
    shots = arriving_downward_matrices.shape[3]
    mate_route = [(level, level ^ 1) for level in range(levels)]
    down_route = cross_route(levels)
    open_route = [(level, level + 1) for level in range(1, levels - 1, 2)]
    shared = (ascending_residual, impedance_contrast, shot_node_indices, emitted_pulse[0].T)

    def mate(pieces):
        return [lax.ppermute(piece, "depth", mate_route) for piece in pieces]

    def down(piece, closed=True):
        return lax.ppermute(piece, "depth", down_route if closed else open_route)

    rows = shots // HALVES
    start = (extrapolation_operator, impedance_contrast, ascending_residual, arriving_downward_matrices)
    results = first(1, *start, ())
    above = [down(piece) for piece in results[:HALVES]]
    *even, high, low, grad = first(0, *start, results[HALVES:])
    beside = [mate(even[2 * half : 2 * half + 2]) for half in range(HALVES)]
    grads = [grad]

    def odd_step(tick, start, pieces, closed=True):
        odd, grads[0] = step(tick, start, 1, pieces, shared, high, low, grads[0], rows)
        return down(odd, closed)

    def even_step(tick, start, pieces):
        *even, grads[0] = step(tick, start, 0, pieces, shared, high, low, grads[0], rows)
        return mate(even)

    later, latest = [], []
    for half in range(HALVES):
        later.append(odd_step(1, half * rows, beside[half]))
        latest.append(even_step(1, half * rows, [above[half]]))
    above, beside = later, latest
    for tick in range(2, TICKS - 1):
        later = [
            odd_step(tick, half * rows, beside[half], tick < TICKS - 2 or half < HALVES - 1) for half in range(HALVES)
        ]
        beside = [even_step(tick, half * rows, [above[half]]) for half in range(HALVES)]
        above = later

    scale = 1.0 / math.sqrt(shots * TICKS)
    held, grad = last(0, above[0], beside[0], shared, high, low, grads[0], None)
    chunks = gradient_chunks(above[1], beside[1], shared, grad, scale)
    gradient = chunks[0]
    for distance in range(1, freqs):
        route = [(i, (i + distance) % freqs) for i in range(freqs)]
        gradient = gradient + lax.ppermute(chunks[distance], "freq", route)
    (out,) = last(1, above[1], beside[1], shared, high, low, None, held)
    return (out[None, None], gradient)


def solution(mesh):
    placed = (
        P("freq", "depth", None, None, None),
        P("depth", None),
        P("freq", "depth", None, None, None, None),
        P("freq", "depth", None, None, None),
        P(),
        P("freq", None, None),
    )
    return jax.shard_map(
        local,
        mesh=mesh,
        in_specs=placed,
        out_specs=(P("freq", "depth", None, None, None), P("depth", "freq")),
        check_vma=False,
    )
```

```python
import functools
import math

import jax
import jax.numpy as jnp
from jax import lax
from jax.experimental import pallas as pl
from jax.experimental.pallas import tpu as pltpu
from jax.sharding import PartitionSpec as P

TICKS = 5
HALVES = 2
TAIL = 16
VMEM_LIMIT = 24 * 1024 * 1024
WEIGHTS = {
    "first_0": 500000000,
    "first_1": 1000000000,
    "step_1_0_0": 30000000,
    "step_1_0_1": 10000000,
    "step_1_1_0": 1000000000,
    "step_1_1_1": 30000000,
    "step_2_0_0": 10000000,
    "step_2_0_1": 1000000,
    "step_2_1_0": 30000000,
    "step_2_1_1": 30000000,
    "step_3_0_0": 10000000,
    "step_3_0_1": 30000000,
    "step_3_1_0": 200000000,
    "step_3_1_1": 30000000,
    "last_0": 100000000,
    "gradient": 200000000,
}
PARAMS = pltpu.CompilerParams(vmem_limit_bytes=VMEM_LIMIT)
IN_VMEM = pl.BlockSpec(memory_space=pltpu.VMEM)
IN_HBM = pl.BlockSpec(memory_space=pltpu.HBM)


def pinned(value):
    return pltpu.with_memory_space_constraint(value, pltpu.VMEM)


def kept(value):
    return pltpu.with_memory_space_constraint(value, pltpu.HBM)


def cost(kind):
    return pl.CostEstimate(flops=WEIGHTS.get(kind, 1), bytes_accessed=1, transcendentals=0)


def dot(left, right):
    return jnp.dot(left, right, preferred_element_type=jnp.float32)


def is_odd():
    return lax.axis_index("depth") % 2 == 1


def when_parity(parity):
    return pl.when(is_odd() if parity else jnp.logical_not(is_odd()))


def split(value):
    high = value.astype(jnp.bfloat16)
    low = (value - high.astype(jnp.float32)).astype(jnp.bfloat16)
    return high, low


def fold(product):
    return jnp.sum(product.reshape(-1, 8, product.shape[1]), axis=0)


def take(pair, start, waves, contrast, grad_in, grad, left, offset=0):
    count = pair[0].shape[0]
    total = None if grad_in is None else grad_in[...]
    for part in range(2):
        wave = waves[part, pl.ds(start + offset, count)]
        if grad is not None:
            term = fold(pair[part] * wave)
            total = term if total is None else total + term
        if left is not None:
            shots = left.shape[0] // 4
            high, low = split(pair[part] + contrast[...] * wave)
            left[pl.ds(part * shots + offset, count), :] = high
            left[pl.ds((2 + part) * shots + offset, count), :] = low
    if grad is not None:
        grad[...] = total


def multiply(left, high, low, columns):
    shots = left.shape[0] // 4

    def by(part):
        big = dot(left[...], high[part, :, columns])
        small = dot(left[pl.ds(0, 2 * shots), :], low[part, :, columns])
        total = big[: 2 * shots] + (big[2 * shots :] + small)
        return total[:shots], total[shots:]

    real_real, imag_real = by(0)
    real_imag, imag_imag = by(1)
    return real_real - imag_imag, real_imag + imag_real


def injected(tick, start, sites, pulse, shape):
    rows, breadth = shape
    shots = sites.shape[1]
    row = lax.broadcasted_iota(jnp.int32, (rows, shots), 0) + start
    column = lax.broadcasted_iota(jnp.int32, (rows, shots), 1)
    spread = jnp.broadcast_to(sites[pl.ds(tick - 1, 1), :], (rows, shots)).astype(jnp.float32)
    site = jnp.sum(jnp.where(row == column, spread, 0.0), axis=1, keepdims=True)
    lanes = lax.broadcasted_iota(jnp.int32, (rows, breadth), 1).astype(jnp.float32)
    hit = lanes == site
    return [jnp.where(hit, pulse[pl.ds(part, 1), pl.ds(tick - 1, 1)], 0.0) for part in range(2)]


def first_kernel(parity, chained, *refs):
    operator, contrast, residual, panel = refs[:4]
    refs = refs[7:] if chained else refs[4:]
    pieces = HALVES * (2 - parity)
    out = refs[:pieces]
    high, low, grad = refs[pieces : pieces + 3]
    whole, reflect, wave, arrived, left, sems = refs[-6:]
    shots, breadth = arrived.shape[1:]
    depth = breadth // 2

    @when_parity(parity)
    def _():
        copies = [
            pltpu.make_async_copy(contrast, reflect, sems.at[0]),
            pltpu.make_async_copy(residual.at[0, 0, 0], wave, sems.at[1]),
            pltpu.make_async_copy(panel.at[0, 0], arrived, sems.at[2]),
        ]
        pieces = [(part, pl.ds(half * depth, depth)) for half in range(2) for part in range(2)]
        for place, (part, rows) in enumerate(pieces):
            copies.append(
                pltpu.make_async_copy(operator.at[0, 0, part, rows], whole.at[part, rows], sems.at[3 + place])
            )
        for copy in copies:
            copy.start()
        for copy in copies[:3]:
            copy.wait()
        take(arrived, 0, wave, reflect, None, grad, left)
        sums = [None, None]
        for place, (part, rows) in enumerate(pieces):
            copies[3 + place].wait()
            upper, lower = split(whole[part, rows])
            high[part, rows] = upper
            low[part, rows] = lower
            big = dot(left[:, rows], upper)
            small = dot(left[pl.ds(0, 2 * shots), rows], lower)
            total = big[: 2 * shots] + (big[2 * shots :] + small)
            sums[part] = total if sums[part] is None else sums[part] + total
        parts = sums[0][:shots] - sums[1][shots:], sums[1][:shots] + sums[0][shots:]
        store(out, parts)


def store(out, parts):
    start = 0
    for piece in out:
        for part in range(2):
            piece[part] = parts[part][start : start + piece.shape[1]]
        start += piece.shape[1]


def piece_shapes(parity, rows, breadth):
    counts = [rows] if parity else [rows - TAIL, TAIL]
    return tuple(pltpu.VMEM((2, count, breadth), jnp.float32) for count in counts)


def first(parity, operator, contrast, residual, panel, carried):
    shots, breadth = panel.shape[3:]
    half = pltpu.VMEM((2, breadth, breadth), jnp.bfloat16)
    outs = piece_shapes(parity, shots // HALVES, breadth) * HALVES
    return pl.pallas_call(
        functools.partial(first_kernel, parity, bool(carried)),
        out_shape=(*outs, half, half, pltpu.VMEM((8, breadth), jnp.float32)),
        in_specs=[IN_HBM] * 4 + [IN_VMEM] * len(carried),
        out_specs=(IN_VMEM,) * (len(outs) + 3),
        scratch_shapes=[
            pltpu.VMEM((2, breadth, breadth), jnp.float32),
            pltpu.VMEM((1, breadth), jnp.float32),
            pltpu.VMEM((2, shots, breadth), jnp.float32),
            pltpu.VMEM((2, shots, breadth), jnp.float32),
            pltpu.VMEM((4 * shots, breadth), jnp.bfloat16),
            pltpu.SemaphoreType.DMA((7,)),
        ],
        input_output_aliases={4 + i: len(outs) + i for i in range(len(carried))},
        compiler_params=PARAMS,
        cost_estimate=cost(f"first_{parity}"),
        name=f"first_{parity}",
    )(kept(operator), kept(contrast), kept(residual), kept(panel), *[pinned(value) for value in carried])


def arrive(tick, start, parity, pieces, shared, grad_in, grad, left):
    residual, contrast, sites, pulse = shared
    waves = residual.at[0, 0, tick]

    def take_pieces():
        offset = 0
        for piece in pieces:
            take(piece, start, waves, contrast, grad if offset else grad_in, grad, left, offset)
            offset += piece.shape[1]

    if parity:
        take_pieces()
        return
    surface = lax.axis_index("depth") == 0
    shape = sum(piece.shape[1] for piece in pieces), pieces[0].shape[2]

    @pl.when(surface)
    def _():
        take(injected(tick, start, sites, pulse, shape), start, waves, contrast, grad_in, grad, left)

    pl.when(jnp.logical_not(surface))(take_pieces)


def arrive_either(half, above, mate, shared, grad_in, grad, left):
    start = half * above.shape[1]

    @when_parity(1)
    def _():
        arrive(TICKS - 1, start, 1, mate, shared, grad_in, grad, left)

    @when_parity(0)
    def _():
        arrive(TICKS - 1, start, 0, (above,), shared, grad_in, grad, left)


def step_kernel(tick, start, parity, count, *refs):
    pieces, refs = refs[:count], refs[count:]
    shared, (high, low, grad_in) = refs[:4], refs[4:7]
    *out, grad, left = refs[7:]

    @when_parity(parity)
    def _():
        arrive(tick, start, parity, pieces, shared, grad_in, grad, left)
        store(out, multiply(left, high, low, slice(None)))


def step(tick, start, parity, pieces, shared, high, low, grad, half):
    breadth = grad.shape[1]
    rows = sum(piece.shape[1] for piece in pieces)
    outs = piece_shapes(1, rows, breadth) if parity else piece_shapes(0, half, breadth) * (rows // half)
    operands = [pinned(value) for value in (*pieces, *shared, high, low, grad)]
    return pl.pallas_call(
        functools.partial(step_kernel, tick, start, parity, len(pieces)),
        out_shape=(*outs, pltpu.VMEM(grad.shape, jnp.float32)),
        in_specs=[IN_VMEM] * len(operands),
        out_specs=(IN_VMEM,) * (len(outs) + 1),
        scratch_shapes=[pltpu.VMEM((4 * rows, breadth), jnp.bfloat16)],
        input_output_aliases={len(operands) - 1: len(outs)},
        compiler_params=PARAMS,
        cost_estimate=cost(f"step_{tick}_{start // half}_{parity}"),
        name=f"step_{tick}_{start // half}_{parity}",
    )(*operands)


def gradient_chunks(above, mate, shared, grad, scale):
    breadth = grad.shape[1]
    count = lax.axis_size("freq")
    width = breadth // count

    def body(above, mate, mate_tail, residual, contrast, sites, pulse, grad_in, *refs):
        chunks, total = refs[:count], refs[count]
        arrive_either(HALVES - 1, above, (mate, mate_tail), (residual, contrast, sites, pulse), grad_in, total, None)
        gradient = jnp.sum(total[...], axis=0, keepdims=True) * scale
        me = lax.axis_index("freq")
        for distance in range(count):
            owner = lax.rem(me + distance, count)
            chunk = jnp.zeros((1, width), jnp.float32)
            for place in range(count):
                piece = gradient[:, place * width : (place + 1) * width]
                chunk = jnp.where(owner == place, piece, chunk)
            chunks[distance][...] = chunk

    operands = [pinned(value) for value in (above, *mate, *shared, grad)]
    return pl.pallas_call(
        body,
        out_shape=(pltpu.VMEM((1, width), jnp.float32),) * count,
        in_specs=[IN_VMEM] * len(operands),
        out_specs=(IN_VMEM,) * count,
        scratch_shapes=[pltpu.VMEM(grad.shape, jnp.float32)],
        compiler_params=PARAMS,
        cost_estimate=cost("gradient"),
        name="gradient",
    )(*operands)


def last_kernel(half, above, mate, mate_tail, *refs):
    shared, high, low = refs[:4], refs[4], refs[5]
    if half == 0:
        grad_in, held, grad, left = refs[6:]
        arrive_either(half, above, (mate, mate_tail), shared, grad_in, grad, left)
        held[0], held[1] = multiply(left, high, low, slice(None))
        return
    before, out, left, held, sems = refs[6:]
    rows = held.shape[1]
    copies = [
        pltpu.make_async_copy(piece, out.at[:, pl.ds(place * rows, rows)], sems.at[place])
        for place, piece in enumerate((before, held))
    ]
    copies[0].start()
    arrive_either(half, above, (mate, mate_tail), shared, None, None, left)
    held[0], held[1] = multiply(left, high, low, slice(None))
    copies[1].start()
    for copy in copies:
        copy.wait()


def last(half, above, mate, shared, high, low, grad, held):
    rows, breadth = above.shape[1:]
    left = pltpu.VMEM((4 * rows, breadth), jnp.bfloat16)
    piece = pltpu.VMEM((2, rows, breadth), jnp.float32)
    if half == 0:
        out_shape, out_specs, scratch, aliases = (piece, pltpu.VMEM(grad.shape, jnp.float32)), (IN_VMEM,) * 2, [left], {9: 1}
    else:
        out_shape, out_specs, aliases = (pltpu.HBM((2, rows * HALVES, breadth), jnp.float32),), (IN_HBM,), {}
        scratch = [left, piece, pltpu.SemaphoreType.DMA((HALVES,))]
    operands = [pinned(value) for value in (above, *mate, *shared, high, low, grad if half == 0 else held)]
    return pl.pallas_call(
        functools.partial(last_kernel, half),
        out_shape=out_shape,
        in_specs=[IN_VMEM] * len(operands),
        out_specs=out_specs,
        scratch_shapes=scratch,
        input_output_aliases=aliases,
        compiler_params=PARAMS,
        cost_estimate=cost(f"last_{half}"),
        name=f"last_{half}",
    )(*operands)


def cross_route(levels):
    route = {level: (level + 1) % levels for level in range(levels)}
    chips = levels // 2
    if chips % 2 == 0:
        for chip in range(chips - 1, 1, -2):
            route[levels - 1 if chip == chips - 1 else 2 * chip] = 2 * (chip - 2) + 1
        route[2 if chips > 2 else levels - 1] = 0
    return sorted(route.items())


def local(
    extrapolation_operator,
    impedance_contrast,
    ascending_residual,
    arriving_downward_matrices,
    shot_node_indices,
    emitted_pulse,
):
    levels = lax.axis_size("depth")
    freqs = lax.axis_size("freq")
    shots = arriving_downward_matrices.shape[3]
    mate_route = [(level, level ^ 1) for level in range(levels)]
    down_route = cross_route(levels)
    open_route = [(level, level + 1) for level in range(1, levels - 1, 2)]
    shared = (ascending_residual, impedance_contrast, shot_node_indices, emitted_pulse[0].T)

    def mate(pieces):
        return [lax.ppermute(piece, "depth", mate_route) for piece in pieces]

    def down(piece, closed=True):
        return lax.ppermute(piece, "depth", down_route if closed else open_route)

    rows = shots // HALVES
    start = (extrapolation_operator, impedance_contrast, ascending_residual, arriving_downward_matrices)
    results = first(1, *start, ())
    above = [down(piece) for piece in results[:HALVES]]
    *even, high, low, grad = first(0, *start, results[HALVES:])
    beside = [mate(even[2 * half : 2 * half + 2]) for half in range(HALVES)]
    grads = [grad]

    def odd_step(tick, start, pieces, closed=True):
        odd, grads[0] = step(tick, start, 1, pieces, shared, high, low, grads[0], rows)
        return down(odd, closed)

    def even_step(tick, start, pieces):
        *even, grads[0] = step(tick, start, 0, pieces, shared, high, low, grads[0], rows)
        return mate(even)

    later, latest = [], []
    for half in range(HALVES):
        later.append(odd_step(1, half * rows, beside[half]))
        latest.append(even_step(1, half * rows, [above[half]]))
    above, beside = later, latest
    for tick in range(2, TICKS - 1):
        later = [
            odd_step(tick, half * rows, beside[half], tick < TICKS - 2 or half < HALVES - 1) for half in range(HALVES)
        ]
        beside = [even_step(tick, half * rows, [above[half]]) for half in range(HALVES)]
        above = later

    scale = 1.0 / math.sqrt(shots * TICKS)
    held, grad = last(0, above[0], beside[0], shared, high, low, grads[0], None)
    chunks = gradient_chunks(above[1], beside[1], shared, grad, scale)
    gradient = chunks[0]
    for distance in range(1, freqs):
        route = [(i, (i + distance) % freqs) for i in range(freqs)]
        gradient = gradient + lax.ppermute(chunks[distance], "freq", route)
    (out,) = last(1, above[1], beside[1], shared, high, low, None, held)
    return (out[None, None], gradient)


def solution(mesh):
    placed = (
        P("freq", "depth", None, None, None),
        P("depth", None),
        P("freq", "depth", None, None, None, None),
        P("freq", "depth", None, None, None),
        P(),
        P("freq", None, None),
    )
    return jax.shard_map(
        local,
        mesh=mesh,
        in_specs=placed,
        out_specs=(P("freq", "depth", None, None, None), P("depth", "freq")),
        check_vma=False,
    )
```

```python
import functools
import math

import jax
import jax.numpy as jnp
from jax import lax
from jax.experimental import pallas as pl
from jax.experimental.pallas import tpu as pltpu
from jax.sharding import PartitionSpec as P

TICKS = 5
HALVES = 2
SHARES = 4
TAIL = 16
VMEM_LIMIT = 24 * 1024 * 1024
WEIGHTS = {
    "first_0": 500000000,
    "first_1": 1000000000,
    "step_1_0_0": 30000000,
    "step_1_0_1": 10000000,
    "step_1_1_0": 1000000000,
    "step_1_1_1": 30000000,
    "step_2_0_0": 10000000,
    "step_2_0_1": 1000000,
    "step_2_1_0": 30000000,
    "step_2_1_1": 30000000,
    "step_3_0_0": 10000000,
    "step_3_0_1": 30000000,
    "step_3_1_0": 200000000,
    "step_3_1_1": 30000000,
    "last_0": 100000000,
    "gradient": 200000000,
}
PARAMS = pltpu.CompilerParams(vmem_limit_bytes=VMEM_LIMIT)
IN_VMEM = pl.BlockSpec(memory_space=pltpu.VMEM)
IN_HBM = pl.BlockSpec(memory_space=pltpu.HBM)


def pinned(value):
    return pltpu.with_memory_space_constraint(value, pltpu.VMEM)


def kept(value):
    return pltpu.with_memory_space_constraint(value, pltpu.HBM)


def cost(kind):
    return pl.CostEstimate(flops=WEIGHTS.get(kind, 1), bytes_accessed=1, transcendentals=0)


def dot(left, right):
    return jnp.dot(left, right, preferred_element_type=jnp.float32)


def is_odd():
    return lax.axis_index("depth") % 2 == 1


def when_parity(parity):
    return pl.when(is_odd() if parity else jnp.logical_not(is_odd()))


def split(value):
    high = value.astype(jnp.bfloat16)
    low = (value - high.astype(jnp.float32)).astype(jnp.bfloat16)
    return high, low


def fold(product):
    return jnp.sum(product.reshape(-1, 8, product.shape[1]), axis=0)


def take(pair, start, waves, contrast, grad_in, grad, left, offset=0):
    count = pair[0].shape[0]
    total = None if grad_in is None else grad_in[...]
    for part in range(2):
        wave = waves[part, pl.ds(start + offset, count)]
        if grad is not None:
            term = fold(pair[part] * wave)
            total = term if total is None else total + term
        if left is not None:
            shots = left.shape[0] // 4
            high, low = split(pair[part] + contrast[...] * wave)
            left[pl.ds(part * shots + offset, count), :] = high
            left[pl.ds((2 + part) * shots + offset, count), :] = low
    if grad is not None:
        grad[...] = total


def multiply(left, high, low, columns):
    shots = left.shape[0] // 4

    def by(part):
        big = dot(left[...], high[part, :, columns])
        small = dot(left[pl.ds(0, 2 * shots), :], low[part, :, columns])
        total = big[: 2 * shots] + (big[2 * shots :] + small)
        return total[:shots], total[shots:]

    real_real, imag_real = by(0)
    real_imag, imag_imag = by(1)
    return real_real - imag_imag, real_imag + imag_real


def injected(tick, start, sites, pulse, shape):
    rows, breadth = shape
    shots = sites.shape[1]
    row = lax.broadcasted_iota(jnp.int32, (rows, shots), 0) + start
    column = lax.broadcasted_iota(jnp.int32, (rows, shots), 1)
    spread = jnp.broadcast_to(sites[pl.ds(tick - 1, 1), :], (rows, shots)).astype(jnp.float32)
    site = jnp.sum(jnp.where(row == column, spread, 0.0), axis=1, keepdims=True)
    lanes = lax.broadcasted_iota(jnp.int32, (rows, breadth), 1).astype(jnp.float32)
    hit = lanes == site
    return [jnp.where(hit, pulse[pl.ds(part, 1), pl.ds(tick - 1, 1)], 0.0) for part in range(2)]


def first_kernel(parity, chained, *refs):
    operator, contrast, residual, panel = refs[:4]
    refs = refs[7:] if chained else refs[4:]
    pieces = HALVES * (2 - parity)
    out = refs[:pieces]
    high, low, grad = refs[pieces : pieces + 3]
    whole, reflect, wave, arrived, left, sems = refs[-6:]
    shots, breadth = arrived.shape[1:]
    depth = breadth // 2

    @when_parity(parity)
    def _():
        copies = [pltpu.make_async_copy(contrast, reflect, sems.at[0])]
        for part in range(2):
            copies.append(pltpu.make_async_copy(residual.at[0, 0, 0, part], wave.at[part], sems.at[1 + part]))
            copies.append(pltpu.make_async_copy(panel.at[0, 0, part], arrived.at[part], sems.at[3 + part]))
        early = len(copies)
        pieces = [(part, half * depth) for half in range(2) for part in range(2)]
        for part, row in pieces:
            for shift in range(0, depth, depth // SHARES):
                rows = pl.ds(row + shift, depth // SHARES)
                source, target = operator.at[0, 0, part, rows], whole.at[part, rows]
                copies.append(pltpu.make_async_copy(source, target, sems.at[len(copies)]))
        for copy in copies:
            copy.start()
        for copy in copies[:early]:
            copy.wait()
        take(arrived, 0, wave, reflect, None, grad, left)
        sums = [None, None]
        for place, (part, row) in enumerate(pieces):
            rows = pl.ds(row, depth)
            for copy in copies[early + place * SHARES : early + (place + 1) * SHARES]:
                copy.wait()
            upper, lower = split(whole[part, rows])
            high[part, rows] = upper
            low[part, rows] = lower
            big = dot(left[:, rows], upper)
            small = dot(left[pl.ds(0, 2 * shots), rows], lower)
            total = big[: 2 * shots] + (big[2 * shots :] + small)
            sums[part] = total if sums[part] is None else sums[part] + total
        parts = sums[0][:shots] - sums[1][shots:], sums[1][:shots] + sums[0][shots:]
        store(out, parts)


def store(out, parts):
    start = 0
    for piece in out:
        for part in range(2):
            piece[part] = parts[part][start : start + piece.shape[1]]
        start += piece.shape[1]


def piece_shapes(parity, rows, breadth):
    counts = [rows] if parity else [rows - TAIL, TAIL]
    return tuple(pltpu.VMEM((2, count, breadth), jnp.float32) for count in counts)


def first(parity, operator, contrast, residual, panel, carried):
    shots, breadth = panel.shape[3:]
    half = pltpu.VMEM((2, breadth, breadth), jnp.bfloat16)
    outs = piece_shapes(parity, shots // HALVES, breadth) * HALVES
    return pl.pallas_call(
        functools.partial(first_kernel, parity, bool(carried)),
        out_shape=(*outs, half, half, pltpu.VMEM((8, breadth), jnp.float32)),
        in_specs=[IN_HBM] * 4 + [IN_VMEM] * len(carried),
        out_specs=(IN_VMEM,) * (len(outs) + 3),
        scratch_shapes=[
            pltpu.VMEM((2, breadth, breadth), jnp.float32),
            pltpu.VMEM((1, breadth), jnp.float32),
            pltpu.VMEM((2, shots, breadth), jnp.float32),
            pltpu.VMEM((2, shots, breadth), jnp.float32),
            pltpu.VMEM((4 * shots, breadth), jnp.bfloat16),
            pltpu.SemaphoreType.DMA((5 + 4 * SHARES,)),
        ],
        input_output_aliases={4 + i: len(outs) + i for i in range(len(carried))},
        compiler_params=PARAMS,
        cost_estimate=cost(f"first_{parity}"),
        name=f"first_{parity}",
    )(kept(operator), kept(contrast), kept(residual), kept(panel), *[pinned(value) for value in carried])


def arrive(tick, start, parity, pieces, shared, grad_in, grad, left):
    residual, contrast, sites, pulse = shared
    waves = residual.at[0, 0, tick]

    def take_pieces():
        offset = 0
        for piece in pieces:
            take(piece, start, waves, contrast, grad if offset else grad_in, grad, left, offset)
            offset += piece.shape[1]

    if parity:
        take_pieces()
        return
    surface = lax.axis_index("depth") == 0
    shape = sum(piece.shape[1] for piece in pieces), pieces[0].shape[2]

    @pl.when(surface)
    def _():
        take(injected(tick, start, sites, pulse, shape), start, waves, contrast, grad_in, grad, left)

    pl.when(jnp.logical_not(surface))(take_pieces)


def arrive_either(half, above, mate, shared, grad_in, grad, left):
    start = half * above.shape[1]

    @when_parity(1)
    def _():
        arrive(TICKS - 1, start, 1, mate, shared, grad_in, grad, left)

    @when_parity(0)
    def _():
        arrive(TICKS - 1, start, 0, (above,), shared, grad_in, grad, left)


def step_kernel(tick, start, parity, count, *refs):
    pieces, refs = refs[:count], refs[count:]
    shared, (high, low, grad_in) = refs[:4], refs[4:7]
    *out, grad, left = refs[7:]

    @when_parity(parity)
    def _():
        arrive(tick, start, parity, pieces, shared, grad_in, grad, left)
        store(out, multiply(left, high, low, slice(None)))


def step(tick, start, parity, pieces, shared, high, low, grad, half):
    breadth = grad.shape[1]
    rows = sum(piece.shape[1] for piece in pieces)
    outs = piece_shapes(1, rows, breadth) if parity else piece_shapes(0, half, breadth) * (rows // half)
    operands = [pinned(value) for value in (*pieces, *shared, high, low, grad)]
    return pl.pallas_call(
        functools.partial(step_kernel, tick, start, parity, len(pieces)),
        out_shape=(*outs, pltpu.VMEM(grad.shape, jnp.float32)),
        in_specs=[IN_VMEM] * len(operands),
        out_specs=(IN_VMEM,) * (len(outs) + 1),
        scratch_shapes=[pltpu.VMEM((4 * rows, breadth), jnp.bfloat16)],
        input_output_aliases={len(operands) - 1: len(outs)},
        compiler_params=PARAMS,
        cost_estimate=cost(f"step_{tick}_{start // half}_{parity}"),
        name=f"step_{tick}_{start // half}_{parity}",
    )(*operands)


def gradient_chunks(above, mate, shared, grad, scale):
    breadth = grad.shape[1]
    count = lax.axis_size("freq")
    width = breadth // count

    def body(above, mate, mate_tail, residual, contrast, sites, pulse, grad_in, *refs):
        chunks, total = refs[:count], refs[count]
        arrive_either(HALVES - 1, above, (mate, mate_tail), (residual, contrast, sites, pulse), grad_in, total, None)
        gradient = jnp.sum(total[...], axis=0, keepdims=True) * scale
        me = lax.axis_index("freq")
        for distance in range(count):
            owner = lax.rem(me + distance, count)
            chunk = jnp.zeros((1, width), jnp.float32)
            for place in range(count):
                piece = gradient[:, place * width : (place + 1) * width]
                chunk = jnp.where(owner == place, piece, chunk)
            chunks[distance][...] = chunk

    operands = [pinned(value) for value in (above, *mate, *shared, grad)]
    return pl.pallas_call(
        body,
        out_shape=(pltpu.VMEM((1, width), jnp.float32),) * count,
        in_specs=[IN_VMEM] * len(operands),
        out_specs=(IN_VMEM,) * count,
        scratch_shapes=[pltpu.VMEM(grad.shape, jnp.float32)],
        compiler_params=PARAMS,
        cost_estimate=cost("gradient"),
        name="gradient",
    )(*operands)


def last_kernel(half, above, mate, mate_tail, *refs):
    shared, high, low = refs[:4], refs[4], refs[5]
    if half == 0:
        grad_in, held, grad, left = refs[6:]
        arrive_either(half, above, (mate, mate_tail), shared, grad_in, grad, left)
        held[0], held[1] = multiply(left, high, low, slice(None))
        return
    before, out, left, held, sems = refs[6:]
    rows = held.shape[1]
    copies = [
        pltpu.make_async_copy(piece, out.at[:, pl.ds(place * rows, rows)], sems.at[place])
        for place, piece in enumerate((before, held))
    ]
    copies[0].start()
    arrive_either(half, above, (mate, mate_tail), shared, None, None, left)
    held[0], held[1] = multiply(left, high, low, slice(None))
    copies[1].start()
    for copy in copies:
        copy.wait()


def last(half, above, mate, shared, high, low, grad, held):
    rows, breadth = above.shape[1:]
    left = pltpu.VMEM((4 * rows, breadth), jnp.bfloat16)
    piece = pltpu.VMEM((2, rows, breadth), jnp.float32)
    if half == 0:
        out_shape, out_specs, scratch, aliases = (piece, pltpu.VMEM(grad.shape, jnp.float32)), (IN_VMEM,) * 2, [left], {9: 1}
    else:
        out_shape, out_specs, aliases = (pltpu.HBM((2, rows * HALVES, breadth), jnp.float32),), (IN_HBM,), {}
        scratch = [left, piece, pltpu.SemaphoreType.DMA((HALVES,))]
    operands = [pinned(value) for value in (above, *mate, *shared, high, low, grad if half == 0 else held)]
    return pl.pallas_call(
        functools.partial(last_kernel, half),
        out_shape=out_shape,
        in_specs=[IN_VMEM] * len(operands),
        out_specs=out_specs,
        scratch_shapes=scratch,
        input_output_aliases=aliases,
        compiler_params=PARAMS,
        cost_estimate=cost(f"last_{half}"),
        name=f"last_{half}",
    )(*operands)


def cross_route(levels):
    route = {level: (level + 1) % levels for level in range(levels)}
    chips = levels // 2
    if chips % 2 == 0:
        for chip in range(chips - 1, 1, -2):
            route[levels - 1 if chip == chips - 1 else 2 * chip] = 2 * (chip - 2) + 1
        route[2 if chips > 2 else levels - 1] = 0
    return sorted(route.items())


def local(
    extrapolation_operator,
    impedance_contrast,
    ascending_residual,
    arriving_downward_matrices,
    shot_node_indices,
    emitted_pulse,
):
    levels = lax.axis_size("depth")
    freqs = lax.axis_size("freq")
    shots = arriving_downward_matrices.shape[3]
    mate_route = [(level, level ^ 1) for level in range(levels)]
    down_route = cross_route(levels)
    open_route = [(level, level + 1) for level in range(1, levels - 1, 2)]
    shared = (ascending_residual, impedance_contrast, shot_node_indices, emitted_pulse[0].T)

    def mate(pieces):
        return [lax.ppermute(piece, "depth", mate_route) for piece in pieces]

    def down(piece, closed=True):
        return lax.ppermute(piece, "depth", down_route if closed else open_route)

    rows = shots // HALVES
    start = (extrapolation_operator, impedance_contrast, ascending_residual, arriving_downward_matrices)
    results = first(1, *start, ())
    above = [down(piece) for piece in results[:HALVES]]
    *even, high, low, grad = first(0, *start, results[HALVES:])
    beside = [mate(even[2 * half : 2 * half + 2]) for half in range(HALVES)]
    grads = [grad]

    def odd_step(tick, start, pieces, closed=True):
        odd, grads[0] = step(tick, start, 1, pieces, shared, high, low, grads[0], rows)
        return down(odd, closed)

    def even_step(tick, start, pieces):
        *even, grads[0] = step(tick, start, 0, pieces, shared, high, low, grads[0], rows)
        return mate(even)

    later, latest = [], []
    for half in range(HALVES):
        later.append(odd_step(1, half * rows, beside[half]))
        latest.append(even_step(1, half * rows, [above[half]]))
    above, beside = later, latest
    for tick in range(2, TICKS - 1):
        later = [
            odd_step(tick, half * rows, beside[half], tick < TICKS - 2 or half < HALVES - 1) for half in range(HALVES)
        ]
        beside = [even_step(tick, half * rows, [above[half]]) for half in range(HALVES)]
        above = later

    scale = 1.0 / math.sqrt(shots * TICKS)
    held, grad = last(0, above[0], beside[0], shared, high, low, grads[0], None)
    chunks = gradient_chunks(above[1], beside[1], shared, grad, scale)
    gradient = chunks[0]
    for distance in range(1, freqs):
        route = [(i, (i + distance) % freqs) for i in range(freqs)]
        gradient = gradient + lax.ppermute(chunks[distance], "freq", route)
    (out,) = last(1, above[1], beside[1], shared, high, low, None, held)
    return (out[None, None], gradient)


def solution(mesh):
    placed = (
        P("freq", "depth", None, None, None),
        P("depth", None),
        P("freq", "depth", None, None, None, None),
        P("freq", "depth", None, None, None),
        P(),
        P("freq", None, None),
    )
    return jax.shard_map(
        local,
        mesh=mesh,
        in_specs=placed,
        out_specs=(P("freq", "depth", None, None, None), P("depth", "freq")),
        check_vma=False,
    )
```

```python
import functools
import math

import jax
import jax.numpy as jnp
from jax import lax
from jax.experimental import pallas as pl
from jax.experimental.pallas import tpu as pltpu
from jax.sharding import PartitionSpec as P

TICKS = 5
HALVES = 2
TAIL = 16
VMEM_LIMIT = 24 * 1024 * 1024
WEIGHTS = {
    "first_0": 500000000,
    "first_1": 1000000000,
    "step_1_0_0": 30000000,
    "step_1_0_1": 10000000,
    "step_1_1_0": 1000000000,
    "step_1_1_1": 30000000,
    "step_2_0_0": 10000000,
    "step_2_0_1": 1000000,
    "step_2_1_0": 30000000,
    "step_2_1_1": 30000000,
    "step_3_0_0": 10000000,
    "step_3_0_1": 30000000,
    "step_3_1_0": 200000000,
    "step_3_1_1": 30000000,
    "last_0": 100000000,
    "gradient": 200000000,
}
PARAMS = pltpu.CompilerParams(vmem_limit_bytes=VMEM_LIMIT)
IN_VMEM = pl.BlockSpec(memory_space=pltpu.VMEM)
IN_HBM = pl.BlockSpec(memory_space=pltpu.HBM)


def pinned(value):
    return pltpu.with_memory_space_constraint(value, pltpu.VMEM)


def kept(value):
    return pltpu.with_memory_space_constraint(value, pltpu.HBM)


def cost(kind):
    return pl.CostEstimate(flops=WEIGHTS.get(kind, 1), bytes_accessed=1, transcendentals=0)


def dot(left, right):
    return jnp.dot(left, right, preferred_element_type=jnp.float32)


def is_odd():
    return lax.axis_index("depth") % 2 == 1


def when_parity(parity):
    return pl.when(is_odd() if parity else jnp.logical_not(is_odd()))


def split(value):
    high = value.astype(jnp.bfloat16)
    low = (value - high.astype(jnp.float32)).astype(jnp.bfloat16)
    return high, low


def fold(product):
    return jnp.sum(product.reshape(-1, 8, product.shape[1]), axis=0)


def take(pair, start, waves, contrast, grad_in, grad, left, offset=0):
    count = pair[0].shape[0]
    total = None if grad_in is None else grad_in[...]
    for part in range(2):
        wave = waves[part, pl.ds(start + offset, count)]
        if grad is not None:
            term = fold(pair[part] * wave)
            total = term if total is None else total + term
        if left is not None:
            shots = left.shape[0] // 4
            high, low = split(pair[part] + contrast[...] * wave)
            left[pl.ds(part * shots + offset, count), :] = high
            left[pl.ds((2 + part) * shots + offset, count), :] = low
    if grad is not None:
        grad[...] = total


def multiply(left, high, low, columns):
    shots = left.shape[0] // 4

    def by(part):
        big = dot(left[...], high[part, :, columns])
        small = dot(left[pl.ds(0, 2 * shots), :], low[part, :, columns])
        total = big[: 2 * shots] + (big[2 * shots :] + small)
        return total[:shots], total[shots:]

    real_real, imag_real = by(0)
    real_imag, imag_imag = by(1)
    return real_real - imag_imag, real_imag + imag_real


def injected(tick, start, sites, pulse, shape):
    rows, breadth = shape
    shots = sites.shape[1]
    row = lax.broadcasted_iota(jnp.int32, (rows, shots), 0) + start
    column = lax.broadcasted_iota(jnp.int32, (rows, shots), 1)
    spread = jnp.broadcast_to(sites[pl.ds(tick - 1, 1), :], (rows, shots)).astype(jnp.float32)
    site = jnp.sum(jnp.where(row == column, spread, 0.0), axis=1, keepdims=True)
    lanes = lax.broadcasted_iota(jnp.int32, (rows, breadth), 1).astype(jnp.float32)
    hit = lanes == site
    return [jnp.where(hit, pulse[pl.ds(part, 1), pl.ds(tick - 1, 1)], 0.0) for part in range(2)]


def first_kernel(parity, chained, *refs):
    operator, contrast, residual, panel = refs[:4]
    refs = refs[7:] if chained else refs[4:]
    pieces = HALVES * (2 - parity)
    out = refs[:pieces]
    high, low, grad = refs[pieces : pieces + 3]
    whole, reflect, wave, arrived, left, sems = refs[-6:]
    shots, breadth = arrived.shape[1:]
    depth = breadth // 2

    @when_parity(parity)
    def _():
        copies = [
            pltpu.make_async_copy(contrast, reflect, sems.at[0]),
            pltpu.make_async_copy(residual.at[0, 0, 0], wave, sems.at[1]),
            pltpu.make_async_copy(panel.at[0, 0], arrived, sems.at[2]),
        ]
        pieces = [(part, pl.ds(half * depth, depth)) for half in range(2) for part in range(2)]
        for place, (part, rows) in enumerate(pieces):
            copies.append(
                pltpu.make_async_copy(operator.at[0, 0, part, rows], whole.at[part, rows], sems.at[3 + place])
            )
        for copy in copies:
            copy.start()
        for copy in copies[:3]:
            copy.wait()
        take(arrived, 0, wave, reflect, None, grad, left)
        sums = [None, None]
        for place, (part, rows) in enumerate(pieces):
            copies[3 + place].wait()
            upper, lower = split(whole[part, rows])
            high[part, rows] = upper
            low[part, rows] = lower
            big = dot(left[:, rows], upper)
            small = dot(left[pl.ds(0, 2 * shots), rows], lower)
            total = big[: 2 * shots] + (big[2 * shots :] + small)
            sums[part] = total if sums[part] is None else sums[part] + total
        parts = sums[0][:shots] - sums[1][shots:], sums[1][:shots] + sums[0][shots:]
        store(out, parts)


def store(out, parts):
    start = 0
    for piece in out:
        for part in range(2):
            piece[part] = parts[part][start : start + piece.shape[1]]
        start += piece.shape[1]


def piece_shapes(parity, rows, breadth):
    counts = [rows] if parity else [rows - TAIL, TAIL]
    return tuple(pltpu.VMEM((2, count, breadth), jnp.float32) for count in counts)


def first(parity, operator, contrast, residual, panel, carried):
    shots, breadth = panel.shape[3:]
    half = pltpu.VMEM((2, breadth, breadth), jnp.bfloat16)
    outs = piece_shapes(parity, shots // HALVES, breadth) * HALVES
    return pl.pallas_call(
        functools.partial(first_kernel, parity, bool(carried)),
        out_shape=(*outs, half, half, pltpu.VMEM((8, breadth), jnp.float32)),
        in_specs=[IN_HBM] * 4 + [IN_VMEM] * len(carried),
        out_specs=(IN_VMEM,) * (len(outs) + 3),
        scratch_shapes=[
            pltpu.VMEM((2, breadth, breadth), jnp.float32),
            pltpu.VMEM((1, breadth), jnp.float32),
            pltpu.VMEM((2, shots, breadth), jnp.float32),
            pltpu.VMEM((2, shots, breadth), jnp.float32),
            pltpu.VMEM((4 * shots, breadth), jnp.bfloat16),
            pltpu.SemaphoreType.DMA((7,)),
        ],
        input_output_aliases={4 + i: len(outs) + i for i in range(len(carried))},
        compiler_params=PARAMS,
        cost_estimate=cost(f"first_{parity}"),
        name=f"first_{parity}",
    )(kept(operator), kept(contrast), kept(residual), kept(panel), *[pinned(value) for value in carried])


def arrive(tick, start, parity, pieces, shared, grad_in, grad, left):
    residual, contrast, sites, pulse = shared
    waves = residual.at[0, 0, tick]

    def take_pieces():
        offset = 0
        for piece in pieces:
            take(piece, start, waves, contrast, grad if offset else grad_in, grad, left, offset)
            offset += piece.shape[1]

    if parity:
        take_pieces()
        return
    surface = lax.axis_index("depth") == 0
    shape = sum(piece.shape[1] for piece in pieces), pieces[0].shape[2]

    @pl.when(surface)
    def _():
        take(injected(tick, start, sites, pulse, shape), start, waves, contrast, grad_in, grad, left)

    pl.when(jnp.logical_not(surface))(take_pieces)


def arrive_either(half, above, mate, shared, grad_in, grad, left):
    start = half * above.shape[1]

    @when_parity(1)
    def _():
        arrive(TICKS - 1, start, 1, mate, shared, grad_in, grad, left)

    @when_parity(0)
    def _():
        arrive(TICKS - 1, start, 0, (above,), shared, grad_in, grad, left)


def step_kernel(tick, start, parity, count, *refs):
    pieces, refs = refs[:count], refs[count:]
    shared, (high, low, grad_in) = refs[:4], refs[4:7]
    *out, grad, left = refs[7:]

    @when_parity(parity)
    def _():
        arrive(tick, start, parity, pieces, shared, grad_in, grad, left)
        store(out, multiply(left, high, low, slice(None)))


def step(tick, start, parity, pieces, shared, high, low, grad, half):
    breadth = grad.shape[1]
    rows = sum(piece.shape[1] for piece in pieces)
    outs = piece_shapes(1, rows, breadth) if parity else piece_shapes(0, half, breadth) * (rows // half)
    operands = [pinned(value) for value in (*pieces, *shared, high, low, grad)]
    return pl.pallas_call(
        functools.partial(step_kernel, tick, start, parity, len(pieces)),
        out_shape=(*outs, pltpu.VMEM(grad.shape, jnp.float32)),
        in_specs=[IN_VMEM] * len(operands),
        out_specs=(IN_VMEM,) * (len(outs) + 1),
        scratch_shapes=[pltpu.VMEM((4 * rows, breadth), jnp.bfloat16)],
        input_output_aliases={len(operands) - 1: len(outs)},
        compiler_params=PARAMS,
        cost_estimate=cost(f"step_{tick}_{start // half}_{parity}"),
        name=f"step_{tick}_{start // half}_{parity}",
    )(*operands)


def gradient_chunks(above, mate, shared, grad, scale):
    breadth = grad.shape[1]
    count = lax.axis_size("freq")
    width = breadth // count

    def body(above, mate, mate_tail, residual, contrast, sites, pulse, grad_in, *refs):
        chunks, total = refs[:count], refs[count]
        arrive_either(HALVES - 1, above, (mate, mate_tail), (residual, contrast, sites, pulse), grad_in, total, None)
        gradient = jnp.sum(total[...], axis=0, keepdims=True) * scale
        me = lax.axis_index("freq")
        for distance in range(count):
            owner = lax.rem(me + distance, count)
            chunk = jnp.zeros((1, width), jnp.float32)
            for place in range(count):
                piece = gradient[:, place * width : (place + 1) * width]
                chunk = jnp.where(owner == place, piece, chunk)
            chunks[distance][...] = chunk

    operands = [pinned(value) for value in (above, *mate, *shared, grad)]
    return pl.pallas_call(
        body,
        out_shape=(pltpu.VMEM((1, width), jnp.float32),) * count,
        in_specs=[IN_VMEM] * len(operands),
        out_specs=(IN_VMEM,) * count,
        scratch_shapes=[pltpu.VMEM(grad.shape, jnp.float32)],
        compiler_params=PARAMS,
        cost_estimate=cost("gradient"),
        name="gradient",
    )(*operands)


def last_kernel(half, above, mate, mate_tail, *refs):
    shared, high, low = refs[:4], refs[4], refs[5]
    if half == 0:
        grad_in, held, grad, left = refs[6:]
        arrive_either(half, above, (mate, mate_tail), shared, grad_in, grad, left)
        held[0], held[1] = multiply(left, high, low, slice(None))
        return
    before, out, left, held, sems = refs[6:]
    rows = held.shape[1]
    copies = [
        pltpu.make_async_copy(piece, out.at[:, pl.ds(place * rows, rows)], sems.at[place])
        for place, piece in enumerate((before, held))
    ]
    copies[0].start()
    arrive_either(half, above, (mate, mate_tail), shared, None, None, left)
    held[0], held[1] = multiply(left, high, low, slice(None))
    copies[1].start()
    for copy in copies:
        copy.wait()


def last(half, above, mate, shared, high, low, grad, held):
    rows, breadth = above.shape[1:]
    left = pltpu.VMEM((4 * rows, breadth), jnp.bfloat16)
    piece = pltpu.VMEM((2, rows, breadth), jnp.float32)
    if half == 0:
        out_shape, out_specs, scratch, aliases = (piece, pltpu.VMEM(grad.shape, jnp.float32)), (IN_VMEM,) * 2, [left], {9: 1}
    else:
        out_shape, out_specs, aliases = (pltpu.HBM((2, rows * HALVES, breadth), jnp.float32),), (IN_HBM,), {}
        scratch = [left, piece, pltpu.SemaphoreType.DMA((HALVES,))]
    operands = [pinned(value) for value in (above, *mate, *shared, high, low, grad if half == 0 else held)]
    return pl.pallas_call(
        functools.partial(last_kernel, half),
        out_shape=out_shape,
        in_specs=[IN_VMEM] * len(operands),
        out_specs=out_specs,
        scratch_shapes=scratch,
        input_output_aliases=aliases,
        compiler_params=PARAMS,
        cost_estimate=cost(f"last_{half}"),
        name=f"last_{half}",
    )(*operands)


def cross_route(levels):
    route = {level: (level + 1) % levels for level in range(levels)}
    chips = levels // 2
    if chips % 2 == 0:
        for chip in range(chips - 1, 1, -2):
            route[levels - 1 if chip == chips - 1 else 2 * chip] = 2 * (chip - 2) + 1
        route[2 if chips > 2 else levels - 1] = 0
    return sorted(route.items())


def surface_alone(route):
    old = dict(route)[0]
    return [(source, 0 if source == 0 else old if target == 0 else target) for source, target in route]


def local(
    extrapolation_operator,
    impedance_contrast,
    ascending_residual,
    arriving_downward_matrices,
    shot_node_indices,
    emitted_pulse,
):
    levels = lax.axis_size("depth")
    freqs = lax.axis_size("freq")
    shots = arriving_downward_matrices.shape[3]
    mate_route = [(level, level ^ 1) for level in range(levels)]
    down_route = cross_route(levels)
    final_route = surface_alone(down_route)
    shared = (ascending_residual, impedance_contrast, shot_node_indices, emitted_pulse[0].T)

    def mate(pieces):
        return [lax.ppermute(piece, "depth", mate_route) for piece in pieces]

    def down(piece, final=False):
        return lax.ppermute(piece, "depth", final_route if final else down_route)

    rows = shots // HALVES
    start = (extrapolation_operator, impedance_contrast, ascending_residual, arriving_downward_matrices)
    results = first(1, *start, ())
    above = [down(piece) for piece in results[:HALVES]]
    *even, high, low, grad = first(0, *start, results[HALVES:])
    beside = [mate(even[2 * half : 2 * half + 2]) for half in range(HALVES)]
    grads = [grad]

    def odd_step(tick, start, pieces, final=False):
        odd, grads[0] = step(tick, start, 1, pieces, shared, high, low, grads[0], rows)
        return down(odd, final)

    def even_step(tick, start, pieces):
        *even, grads[0] = step(tick, start, 0, pieces, shared, high, low, grads[0], rows)
        return mate(even)

    later, latest = [], []
    for half in range(HALVES):
        later.append(odd_step(1, half * rows, beside[half]))
        latest.append(even_step(1, half * rows, [above[half]]))
    above, beside = later, latest
    for tick in range(2, TICKS - 1):
        later = [
            odd_step(tick, half * rows, beside[half], tick == TICKS - 2 and half == HALVES - 1) for half in range(HALVES)
        ]
        beside = [even_step(tick, half * rows, [above[half]]) for half in range(HALVES)]
        above = later

    scale = 1.0 / math.sqrt(shots * TICKS)
    held, grad = last(0, above[0], beside[0], shared, high, low, grads[0], None)
    chunks = gradient_chunks(above[1], beside[1], shared, grad, scale)
    gradient = chunks[0]
    for distance in range(1, freqs):
        route = [(i, (i + distance) % freqs) for i in range(freqs)]
        gradient = gradient + lax.ppermute(chunks[distance], "freq", route)
    (out,) = last(1, above[1], beside[1], shared, high, low, None, held)
    return (out[None, None], gradient)


def solution(mesh):
    placed = (
        P("freq", "depth", None, None, None),
        P("depth", None),
        P("freq", "depth", None, None, None, None),
        P("freq", "depth", None, None, None),
        P(),
        P("freq", None, None),
    )
    return jax.shard_map(
        local,
        mesh=mesh,
        in_specs=placed,
        out_specs=(P("freq", "depth", None, None, None), P("depth", "freq")),
        check_vma=False,
    )
```

```python
import functools
import math

import jax
import jax.numpy as jnp
from jax import lax
from jax.experimental import pallas as pl
from jax.experimental.pallas import tpu as pltpu
from jax.sharding import PartitionSpec as P

TICKS = 5
HALVES = 2
TAIL = 16
VMEM_LIMIT = 24 * 1024 * 1024
WEIGHTS = {
    "first_0": 500000000,
    "first_1": 1000000000,
    "step_1_0_0": 30000000,
    "step_1_0_1": 10000000,
    "step_1_1_0": 1000000000,
    "step_1_1_1": 30000000,
    "step_2_0_0": 10000000,
    "step_2_0_1": 1000000,
    "step_2_1_0": 30000000,
    "step_2_1_1": 30000000,
    "step_3_0_0": 10000000,
    "step_3_0_1": 30000000,
    "step_3_1_0": 200000000,
    "step_3_1_1": 30000000,
    "last_0": 100000000,
    "gradient": 200000000,
}
PARAMS = pltpu.CompilerParams(vmem_limit_bytes=VMEM_LIMIT)
IN_VMEM = pl.BlockSpec(memory_space=pltpu.VMEM)
IN_HBM = pl.BlockSpec(memory_space=pltpu.HBM)


def pinned(value):
    return pltpu.with_memory_space_constraint(value, pltpu.VMEM)


def kept(value):
    return pltpu.with_memory_space_constraint(value, pltpu.HBM)


def cost(kind):
    return pl.CostEstimate(flops=WEIGHTS.get(kind, 1), bytes_accessed=1, transcendentals=0)


def dot(left, right):
    return jnp.dot(left, right, preferred_element_type=jnp.float32)


def is_odd():
    return lax.axis_index("depth") % 2 == 1


def when_parity(parity):
    return pl.when(is_odd() if parity else jnp.logical_not(is_odd()))


def split(value):
    high = value.astype(jnp.bfloat16)
    low = (value - high.astype(jnp.float32)).astype(jnp.bfloat16)
    return high, low


def fold(product):
    return jnp.sum(product.reshape(-1, 8, product.shape[1]), axis=0)


def take(pair, start, waves, contrast, grad_in, grad, left, offset=0):
    count = pair[0].shape[0]
    total = None if grad_in is None else grad_in[...]
    for part in range(2):
        wave = waves[part, pl.ds(start + offset, count)]
        if grad is not None:
            term = fold(pair[part] * wave)
            total = term if total is None else total + term
        if left is not None:
            shots = left.shape[0] // 4
            high, low = split(pair[part] + contrast[...] * wave)
            left[pl.ds(part * shots + offset, count), :] = high
            left[pl.ds((2 + part) * shots + offset, count), :] = low
    if grad is not None:
        grad[...] = total


def multiply(left, high, low, columns):
    shots = left.shape[0] // 4

    def by(part):
        big = dot(left[...], high[part, :, columns])
        small = dot(left[pl.ds(0, 2 * shots), :], low[part, :, columns])
        total = big[: 2 * shots] + (big[2 * shots :] + small)
        return total[:shots], total[shots:]

    real_real, imag_real = by(0)
    real_imag, imag_imag = by(1)
    return real_real - imag_imag, real_imag + imag_real


def injected(tick, start, sites, pulse, shape):
    rows, breadth = shape
    shots = sites.shape[1]
    row = lax.broadcasted_iota(jnp.int32, (rows, shots), 0) + start
    column = lax.broadcasted_iota(jnp.int32, (rows, shots), 1)
    spread = jnp.broadcast_to(sites[pl.ds(tick - 1, 1), :], (rows, shots)).astype(jnp.float32)
    site = jnp.sum(jnp.where(row == column, spread, 0.0), axis=1, keepdims=True)
    lanes = lax.broadcasted_iota(jnp.int32, (rows, breadth), 1).astype(jnp.float32)
    hit = lanes == site
    return [jnp.where(hit, pulse[pl.ds(part, 1), pl.ds(tick - 1, 1)], 0.0) for part in range(2)]


def first_kernel(parity, chained, *refs):
    operator, contrast, residual, panel = refs[:4]
    refs = refs[7:] if chained else refs[4:]
    pieces = HALVES * (2 - parity)
    out = refs[:pieces]
    high, low, grad = refs[pieces : pieces + 3]
    whole, reflect, wave, arrived, left, sems = refs[-6:]
    shots, breadth = arrived.shape[1:]
    depth = breadth // 2

    @when_parity(parity)
    def _():
        copies = [
            pltpu.make_async_copy(contrast, reflect, sems.at[0]),
            pltpu.make_async_copy(residual.at[0, 0, 0], wave, sems.at[1]),
            pltpu.make_async_copy(panel.at[0, 0], arrived, sems.at[2]),
        ]
        pieces = [(part, pl.ds(half * depth, depth)) for half in range(2) for part in range(2)]
        for place, (part, rows) in enumerate(pieces):
            copies.append(
                pltpu.make_async_copy(operator.at[0, 0, part, rows], whole.at[part, rows], sems.at[3 + place])
            )
        for copy in copies:
            copy.start()
        for copy in copies[:3]:
            copy.wait()
        take(arrived, 0, wave, reflect, None, grad, left)
        sums = [None, None]
        for place, (part, rows) in enumerate(pieces):
            copies[3 + place].wait()
            upper, lower = split(whole[part, rows])
            high[part, rows] = upper
            low[part, rows] = lower
            big = dot(left[:, rows], upper)
            small = dot(left[pl.ds(0, 2 * shots), rows], lower)
            total = big[: 2 * shots] + (big[2 * shots :] + small)
            sums[part] = total if sums[part] is None else sums[part] + total
        parts = sums[0][:shots] - sums[1][shots:], sums[1][:shots] + sums[0][shots:]
        store(out, parts)


def store(out, parts):
    start = 0
    for piece in out:
        for part in range(2):
            piece[part] = parts[part][start : start + piece.shape[1]]
        start += piece.shape[1]


def piece_shapes(parity, rows, breadth):
    counts = [rows] if parity else [rows - TAIL, TAIL]
    return tuple(pltpu.VMEM((2, count, breadth), jnp.float32) for count in counts)


def first(parity, operator, contrast, residual, panel, carried):
    shots, breadth = panel.shape[3:]
    half = pltpu.VMEM((2, breadth, breadth), jnp.bfloat16)
    outs = piece_shapes(parity, shots // HALVES, breadth) * HALVES
    return pl.pallas_call(
        functools.partial(first_kernel, parity, bool(carried)),
        out_shape=(*outs, half, half, pltpu.VMEM((8, breadth), jnp.float32)),
        in_specs=[IN_HBM] * 4 + [IN_VMEM] * len(carried),
        out_specs=(IN_VMEM,) * (len(outs) + 3),
        scratch_shapes=[
            pltpu.VMEM((2, breadth, breadth), jnp.float32),
            pltpu.VMEM((1, breadth), jnp.float32),
            pltpu.VMEM((2, shots, breadth), jnp.float32),
            pltpu.VMEM((2, shots, breadth), jnp.float32),
            pltpu.VMEM((4 * shots, breadth), jnp.bfloat16),
            pltpu.SemaphoreType.DMA((7,)),
        ],
        input_output_aliases={4 + i: len(outs) + i for i in range(len(carried))},
        compiler_params=PARAMS,
        cost_estimate=cost(f"first_{parity}"),
        name=f"first_{parity}",
    )(kept(operator), kept(contrast), kept(residual), kept(panel), *[pinned(value) for value in carried])


def arrive(tick, start, parity, pieces, shared, grad_in, grad, left):
    residual, contrast, sites, pulse = shared
    waves = residual.at[0, 0, tick]

    def take_pieces():
        offset = 0
        for piece in pieces:
            take(piece, start, waves, contrast, grad if offset else grad_in, grad, left, offset)
            offset += piece.shape[1]

    if parity:
        take_pieces()
        return
    surface = lax.axis_index("depth") == 0
    shape = sum(piece.shape[1] for piece in pieces), pieces[0].shape[2]

    @pl.when(surface)
    def _():
        take(injected(tick, start, sites, pulse, shape), start, waves, contrast, grad_in, grad, left)

    pl.when(jnp.logical_not(surface))(take_pieces)


def arrive_either(half, above, mate, shared, grad_in, grad, left):
    start = half * above.shape[1]

    @when_parity(1)
    def _():
        arrive(TICKS - 1, start, 1, mate, shared, grad_in, grad, left)

    @when_parity(0)
    def _():
        arrive(TICKS - 1, start, 0, (above,), shared, grad_in, grad, left)


def step_kernel(tick, start, parity, count, *refs):
    pieces, refs = refs[:count], refs[count:]
    shared, (high, low, grad_in) = refs[:4], refs[4:7]
    *out, grad, left = refs[7:]

    @when_parity(parity)
    def _():
        arrive(tick, start, parity, pieces, shared, grad_in, grad, left)
        store(out, multiply(left, high, low, slice(None)))


def step(tick, start, parity, pieces, shared, high, low, grad, half):
    breadth = grad.shape[1]
    rows = sum(piece.shape[1] for piece in pieces)
    outs = piece_shapes(1, rows, breadth) if parity else piece_shapes(0, half, breadth) * (rows // half)
    operands = [pinned(value) for value in (*pieces, *shared, high, low, grad)]
    return pl.pallas_call(
        functools.partial(step_kernel, tick, start, parity, len(pieces)),
        out_shape=(*outs, pltpu.VMEM(grad.shape, jnp.float32)),
        in_specs=[IN_VMEM] * len(operands),
        out_specs=(IN_VMEM,) * (len(outs) + 1),
        scratch_shapes=[pltpu.VMEM((4 * rows, breadth), jnp.bfloat16)],
        input_output_aliases={len(operands) - 1: len(outs)},
        compiler_params=PARAMS,
        cost_estimate=cost(f"step_{tick}_{start // half}_{parity}"),
        name=f"step_{tick}_{start // half}_{parity}",
    )(*operands)


def gradient_chunks(above, mate, shared, grad, scale):
    breadth = grad.shape[1]
    count = lax.axis_size("freq")
    width = breadth // count

    def body(above, mate, mate_tail, residual, contrast, sites, pulse, grad_in, *refs):
        chunks, total = refs[:count], refs[count]
        arrive_either(HALVES - 1, above, (mate, mate_tail), (residual, contrast, sites, pulse), grad_in, total, None)
        gradient = jnp.sum(total[...], axis=0, keepdims=True) * scale
        me = lax.axis_index("freq")
        for distance in range(count):
            owner = lax.rem(me + distance, count)
            chunk = jnp.zeros((1, width), jnp.float32)
            for place in range(count):
                piece = gradient[:, place * width : (place + 1) * width]
                chunk = jnp.where(owner == place, piece, chunk)
            chunks[distance][...] = chunk

    operands = [pinned(value) for value in (above, *mate, *shared, grad)]
    return pl.pallas_call(
        body,
        out_shape=(pltpu.VMEM((1, width), jnp.float32),) * count,
        in_specs=[IN_VMEM] * len(operands),
        out_specs=(IN_VMEM,) * count,
        scratch_shapes=[pltpu.VMEM(grad.shape, jnp.float32)],
        compiler_params=PARAMS,
        cost_estimate=cost("gradient"),
        name="gradient",
    )(*operands)


def last_kernel(half, above, mate, mate_tail, *refs):
    shared, high, low = refs[:4], refs[4], refs[5]
    if half == 0:
        grad_in, held, grad, left = refs[6:]
        arrive_either(half, above, (mate, mate_tail), shared, grad_in, grad, left)
        held[0], held[1] = multiply(left, high, low, slice(None))
        return
    before, out, left, held, sems = refs[6:]
    rows = held.shape[1]
    copies = [
        pltpu.make_async_copy(piece, out.at[:, pl.ds(place * rows, rows)], sems.at[place])
        for place, piece in enumerate((before, held))
    ]
    copies[0].start()
    arrive_either(half, above, (mate, mate_tail), shared, None, None, left)
    held[0], held[1] = multiply(left, high, low, slice(None))
    copies[1].start()
    for copy in copies:
        copy.wait()


def last(half, above, mate, shared, high, low, grad, held):
    rows, breadth = above.shape[1:]
    left = pltpu.VMEM((4 * rows, breadth), jnp.bfloat16)
    piece = pltpu.VMEM((2, rows, breadth), jnp.float32)
    if half == 0:
        out_shape, out_specs, scratch, aliases = (piece, pltpu.VMEM(grad.shape, jnp.float32)), (IN_VMEM,) * 2, [left], {9: 1}
    else:
        out_shape, out_specs, aliases = (pltpu.HBM((2, rows * HALVES, breadth), jnp.float32),), (IN_HBM,), {}
        scratch = [left, piece, pltpu.SemaphoreType.DMA((HALVES,))]
    operands = [pinned(value) for value in (above, *mate, *shared, high, low, grad if half == 0 else held)]
    return pl.pallas_call(
        functools.partial(last_kernel, half),
        out_shape=out_shape,
        in_specs=[IN_VMEM] * len(operands),
        out_specs=out_specs,
        scratch_shapes=scratch,
        input_output_aliases=aliases,
        compiler_params=PARAMS,
        cost_estimate=cost(f"last_{half}"),
        name=f"last_{half}",
    )(*operands)


def cross_route(levels, upper=True):
    route = {level: (level + 1) % levels for level in range(levels)}
    chips = levels // 2
    if chips % 2 or chips < 4:
        return sorted(route.items())
    if upper:
        for chip in range(chips - 1, 1, -2):
            route[levels - 1 if chip == chips - 1 else 2 * chip] = 2 * (chip - 2) + 1
        route[2] = 0
    else:
        route[levels - 1] = levels - 3
        for chip in range(chips - 2, 2, -2):
            route[2 * chip] = 2 * (chip - 2) + 1
        route[4] = 0
    return sorted(route.items())


def local(
    extrapolation_operator,
    impedance_contrast,
    ascending_residual,
    arriving_downward_matrices,
    shot_node_indices,
    emitted_pulse,
):
    levels = lax.axis_size("depth")
    freqs = lax.axis_size("freq")
    shots = arriving_downward_matrices.shape[3]
    mate_route = [(level, level ^ 1) for level in range(levels)]
    down_route = cross_route(levels)
    other_route = cross_route(levels, False)
    shared = (ascending_residual, impedance_contrast, shot_node_indices, emitted_pulse[0].T)

    def mate(pieces):
        return [lax.ppermute(piece, "depth", mate_route) for piece in pieces]

    def down(piece, other=False):
        return lax.ppermute(piece, "depth", other_route if other else down_route)

    rows = shots // HALVES
    start = (extrapolation_operator, impedance_contrast, ascending_residual, arriving_downward_matrices)
    results = first(1, *start, ())
    above = [down(piece) for piece in results[:HALVES]]
    *even, high, low, grad = first(0, *start, results[HALVES:])
    beside = [mate(even[2 * half : 2 * half + 2]) for half in range(HALVES)]
    grads = [grad]

    def odd_step(tick, start, pieces, other=False):
        odd, grads[0] = step(tick, start, 1, pieces, shared, high, low, grads[0], rows)
        return down(odd, other)

    def even_step(tick, start, pieces):
        *even, grads[0] = step(tick, start, 0, pieces, shared, high, low, grads[0], rows)
        return mate(even)

    later, latest = [], []
    for half in range(HALVES):
        later.append(odd_step(1, half * rows, beside[half]))
        latest.append(even_step(1, half * rows, [above[half]]))
    above, beside = later, latest
    for tick in range(2, TICKS - 1):
        later = [
            odd_step(tick, half * rows, beside[half], tick == TICKS - 2 and half == 0) for half in range(HALVES)
        ]
        beside = [even_step(tick, half * rows, [above[half]]) for half in range(HALVES)]
        above = later

    scale = 1.0 / math.sqrt(shots * TICKS)
    held, grad = last(0, above[0], beside[0], shared, high, low, grads[0], None)
    chunks = gradient_chunks(above[1], beside[1], shared, grad, scale)
    gradient = chunks[0]
    for distance in range(1, freqs):
        route = [(i, (i + distance) % freqs) for i in range(freqs)]
        gradient = gradient + lax.ppermute(chunks[distance], "freq", route)
    (out,) = last(1, above[1], beside[1], shared, high, low, None, held)
    return (out[None, None], gradient)


def solution(mesh):
    placed = (
        P("freq", "depth", None, None, None),
        P("depth", None),
        P("freq", "depth", None, None, None, None),
        P("freq", "depth", None, None, None),
        P(),
        P("freq", None, None),
    )
    return jax.shard_map(
        local,
        mesh=mesh,
        in_specs=placed,
        out_specs=(P("freq", "depth", None, None, None), P("depth", "freq")),
        check_vma=False,
    )
```

```python
import functools
import math

import jax
import jax.numpy as jnp
from jax import lax
from jax.experimental import pallas as pl
from jax.experimental.pallas import tpu as pltpu
from jax.sharding import PartitionSpec as P

TICKS = 5
HALVES = 2
TAIL = 16
VMEM_LIMIT = 24 * 1024 * 1024
WEIGHTS = {
    "first_0": 500000000,
    "first_1": 1000000000,
    "step_1_0_0": 30000000,
    "step_1_0_1": 10000000,
    "step_1_1_0": 1000000000,
    "step_1_1_1": 30000000,
    "step_2_0_0": 10000000,
    "step_2_0_1": 1000000,
    "step_2_1_0": 30000000,
    "step_2_1_1": 30000000,
    "step_3_0_0": 10000000,
    "step_3_0_1": 30000000,
    "step_3_1_0": 200000000,
    "step_3_1_1": 30000000,
    "last_0": 100000000,
    "gradient": 200000000,
}
PARAMS = pltpu.CompilerParams(vmem_limit_bytes=VMEM_LIMIT)
IN_VMEM = pl.BlockSpec(memory_space=pltpu.VMEM)
IN_HBM = pl.BlockSpec(memory_space=pltpu.HBM)


def pinned(value):
    return pltpu.with_memory_space_constraint(value, pltpu.VMEM)


def kept(value):
    return pltpu.with_memory_space_constraint(value, pltpu.HBM)


def cost(kind):
    return pl.CostEstimate(flops=WEIGHTS.get(kind, 1), bytes_accessed=1, transcendentals=0)


def dot(left, right):
    return jnp.dot(left, right, preferred_element_type=jnp.float32)


def is_odd():
    return lax.axis_index("depth") % 2 == 1


def when_parity(parity):
    return pl.when(is_odd() if parity else jnp.logical_not(is_odd()))


def split(value):
    high = value.astype(jnp.bfloat16)
    low = (value - high.astype(jnp.float32)).astype(jnp.bfloat16)
    return high, low


def fold(product):
    return jnp.sum(product.reshape(-1, 8, product.shape[1]), axis=0)


def take(pair, start, waves, contrast, grad_in, grad, left, offset=0):
    count = pair[0].shape[0]
    total = None if grad_in is None else grad_in[...]
    for part in range(2):
        wave = waves[part, pl.ds(start + offset, count)]
        if grad is not None:
            term = fold(pair[part] * wave)
            total = term if total is None else total + term
        if left is not None:
            shots = left.shape[0] // 4
            high, low = split(pair[part] + contrast[...] * wave)
            left[pl.ds(part * shots + offset, count), :] = high
            left[pl.ds((2 + part) * shots + offset, count), :] = low
    if grad is not None:
        grad[...] = total


def multiply(left, high, low, columns):
    shots = left.shape[0] // 4

    def by(part):
        big = dot(left[...], high[part, :, columns])
        small = dot(left[pl.ds(0, 2 * shots), :], low[part, :, columns])
        total = big[: 2 * shots] + (big[2 * shots :] + small)
        return total[:shots], total[shots:]

    real_real, imag_real = by(0)
    real_imag, imag_imag = by(1)
    return real_real - imag_imag, real_imag + imag_real


def injected(tick, start, sites, pulse, shape):
    rows, breadth = shape
    shots = sites.shape[1]
    row = lax.broadcasted_iota(jnp.int32, (rows, shots), 0) + start
    column = lax.broadcasted_iota(jnp.int32, (rows, shots), 1)
    spread = jnp.broadcast_to(sites[pl.ds(tick - 1, 1), :], (rows, shots)).astype(jnp.float32)
    site = jnp.sum(jnp.where(row == column, spread, 0.0), axis=1, keepdims=True)
    lanes = lax.broadcasted_iota(jnp.int32, (rows, breadth), 1).astype(jnp.float32)
    hit = lanes == site
    return [jnp.where(hit, pulse[pl.ds(part, 1), pl.ds(tick - 1, 1)], 0.0) for part in range(2)]


def first_kernel(parity, chained, *refs):
    operator, contrast, residual, panel = refs[:4]
    refs = refs[7:] if chained else refs[4:]
    pieces = HALVES * (2 - parity)
    out = refs[:pieces]
    high, low, grad = refs[pieces : pieces + 3]
    whole, reflect, wave, arrived, left, sems = refs[-6:]
    shots, breadth = arrived.shape[1:]
    depth = breadth // 2

    @when_parity(parity)
    def _():
        copies = [
            pltpu.make_async_copy(contrast, reflect, sems.at[0]),
            pltpu.make_async_copy(residual.at[0, 0, 0], wave, sems.at[1]),
            pltpu.make_async_copy(panel.at[0, 0], arrived, sems.at[2]),
        ]
        pieces = [(part, pl.ds(half * depth, depth)) for half in range(2) for part in range(2)]
        for place, (part, rows) in enumerate(pieces):
            copies.append(
                pltpu.make_async_copy(operator.at[0, 0, part, rows], whole.at[part, rows], sems.at[3 + place])
            )
        for copy in copies:
            copy.start()
        for copy in copies[:3]:
            copy.wait()
        take(arrived, 0, wave, reflect, None, grad, left)
        sums = [None, None]
        for place, (part, rows) in enumerate(pieces):
            copies[3 + place].wait()
            upper, lower = split(whole[part, rows])
            high[part, rows] = upper
            low[part, rows] = lower
            big = dot(left[:, rows], upper)
            small = dot(left[pl.ds(0, 2 * shots), rows], lower)
            total = big[: 2 * shots] + (big[2 * shots :] + small)
            sums[part] = total if sums[part] is None else sums[part] + total
        parts = sums[0][:shots] - sums[1][shots:], sums[1][:shots] + sums[0][shots:]
        store(out, parts)


def store(out, parts):
    start = 0
    for piece in out:
        for part in range(2):
            piece[part] = parts[part][start : start + piece.shape[1]]
        start += piece.shape[1]


def piece_shapes(parity, rows, breadth):
    counts = [rows] if parity else [rows - TAIL, TAIL]
    return tuple(pltpu.VMEM((2, count, breadth), jnp.float32) for count in counts)


def first(parity, operator, contrast, residual, panel, carried):
    shots, breadth = panel.shape[3:]
    half = pltpu.VMEM((2, breadth, breadth), jnp.bfloat16)
    outs = piece_shapes(parity, shots // HALVES, breadth) * HALVES
    return pl.pallas_call(
        functools.partial(first_kernel, parity, bool(carried)),
        out_shape=(*outs, half, half, pltpu.VMEM((8, breadth), jnp.float32)),
        in_specs=[IN_HBM] * 4 + [IN_VMEM] * len(carried),
        out_specs=(IN_VMEM,) * (len(outs) + 3),
        scratch_shapes=[
            pltpu.VMEM((2, breadth, breadth), jnp.float32),
            pltpu.VMEM((1, breadth), jnp.float32),
            pltpu.VMEM((2, shots, breadth), jnp.float32),
            pltpu.VMEM((2, shots, breadth), jnp.float32),
            pltpu.VMEM((4 * shots, breadth), jnp.bfloat16),
            pltpu.SemaphoreType.DMA((7,)),
        ],
        input_output_aliases={4 + i: len(outs) + i for i in range(len(carried))},
        compiler_params=PARAMS,
        cost_estimate=cost(f"first_{parity}"),
        name=f"first_{parity}",
    )(kept(operator), kept(contrast), kept(residual), kept(panel), *[pinned(value) for value in carried])


def arrive(tick, start, parity, pieces, shared, grad_in, grad, left):
    residual, contrast, sites, pulse = shared
    waves = residual.at[0, 0, tick]

    def take_pieces():
        offset = 0
        for piece in pieces:
            take(piece, start, waves, contrast, grad if offset else grad_in, grad, left, offset)
            offset += piece.shape[1]

    if parity:
        take_pieces()
        return
    surface = lax.axis_index("depth") == 0
    shape = sum(piece.shape[1] for piece in pieces), pieces[0].shape[2]

    @pl.when(surface)
    def _():
        take(injected(tick, start, sites, pulse, shape), start, waves, contrast, grad_in, grad, left)

    pl.when(jnp.logical_not(surface))(take_pieces)


def arrive_either(half, above, mate, shared, grad_in, grad, left):
    start = half * above.shape[1]

    @when_parity(1)
    def _():
        arrive(TICKS - 1, start, 1, mate, shared, grad_in, grad, left)

    @when_parity(0)
    def _():
        arrive(TICKS - 1, start, 0, (above,), shared, grad_in, grad, left)


def step_kernel(tick, start, parity, count, *refs):
    pieces, refs = refs[:count], refs[count:]
    shared, (high, low, grad_in) = refs[:4], refs[4:7]
    *out, grad, left = refs[7:]

    @when_parity(parity)
    def _():
        arrive(tick, start, parity, pieces, shared, grad_in, grad, left)
        store(out, multiply(left, high, low, slice(None)))


def step(tick, start, parity, pieces, shared, high, low, grad, half):
    breadth = grad.shape[1]
    rows = sum(piece.shape[1] for piece in pieces)
    outs = piece_shapes(1, rows, breadth) if parity else piece_shapes(0, half, breadth) * (rows // half)
    operands = [pinned(value) for value in (*pieces, *shared, high, low, grad)]
    return pl.pallas_call(
        functools.partial(step_kernel, tick, start, parity, len(pieces)),
        out_shape=(*outs, pltpu.VMEM(grad.shape, jnp.float32)),
        in_specs=[IN_VMEM] * len(operands),
        out_specs=(IN_VMEM,) * (len(outs) + 1),
        scratch_shapes=[pltpu.VMEM((4 * rows, breadth), jnp.bfloat16)],
        input_output_aliases={len(operands) - 1: len(outs)},
        compiler_params=PARAMS,
        cost_estimate=cost(f"step_{tick}_{start // half}_{parity}"),
        name=f"step_{tick}_{start // half}_{parity}",
    )(*operands)


def gradient_chunks(above, mate, shared, grad, scale):
    breadth = grad.shape[1]
    count = lax.axis_size("freq")
    width = breadth // count

    def body(above, mate, mate_tail, residual, contrast, sites, pulse, grad_in, *refs):
        chunks, total = refs[:count], refs[count]
        arrive_either(HALVES - 1, above, (mate, mate_tail), (residual, contrast, sites, pulse), grad_in, total, None)
        gradient = jnp.sum(total[...], axis=0, keepdims=True) * scale
        me = lax.axis_index("freq")
        for distance in range(count):
            owner = lax.rem(me + distance, count)
            chunk = jnp.zeros((1, width), jnp.float32)
            for place in range(count):
                piece = gradient[:, place * width : (place + 1) * width]
                chunk = jnp.where(owner == place, piece, chunk)
            chunks[distance][...] = chunk

    operands = [pinned(value) for value in (above, *mate, *shared, grad)]
    return pl.pallas_call(
        body,
        out_shape=(pltpu.VMEM((1, width), jnp.float32),) * count,
        in_specs=[IN_VMEM] * len(operands),
        out_specs=(IN_VMEM,) * count,
        scratch_shapes=[pltpu.VMEM(grad.shape, jnp.float32)],
        compiler_params=PARAMS,
        cost_estimate=cost("gradient"),
        name="gradient",
    )(*operands)


def last_kernel(half, above, mate, mate_tail, *refs):
    shared, high, low = refs[:4], refs[4], refs[5]
    if half == 0:
        grad_in, held, grad, left = refs[6:]
        arrive_either(half, above, (mate, mate_tail), shared, grad_in, grad, left)
        held[0], held[1] = multiply(left, high, low, slice(None))
        return
    before, out, left, held, sems = refs[6:]
    rows = held.shape[1]
    copies = [
        pltpu.make_async_copy(piece, out.at[:, pl.ds(place * rows, rows)], sems.at[place])
        for place, piece in enumerate((before, held))
    ]
    copies[0].start()
    arrive_either(half, above, (mate, mate_tail), shared, None, None, left)
    held[0], held[1] = multiply(left, high, low, slice(None))
    copies[1].start()
    for copy in copies:
        copy.wait()


def last(half, above, mate, shared, high, low, grad, held):
    rows, breadth = above.shape[1:]
    left = pltpu.VMEM((4 * rows, breadth), jnp.bfloat16)
    piece = pltpu.VMEM((2, rows, breadth), jnp.float32)
    if half == 0:
        out_shape, out_specs, scratch, aliases = (piece, pltpu.VMEM(grad.shape, jnp.float32)), (IN_VMEM,) * 2, [left], {9: 1}
    else:
        out_shape, out_specs, aliases = (pltpu.HBM((2, rows * HALVES, breadth), jnp.float32),), (IN_HBM,), {}
        scratch = [left, piece, pltpu.SemaphoreType.DMA((HALVES,))]
    operands = [pinned(value) for value in (above, *mate, *shared, high, low, grad if half == 0 else held)]
    return pl.pallas_call(
        functools.partial(last_kernel, half),
        out_shape=out_shape,
        in_specs=[IN_VMEM] * len(operands),
        out_specs=out_specs,
        scratch_shapes=scratch,
        input_output_aliases=aliases,
        compiler_params=PARAMS,
        cost_estimate=cost(f"last_{half}"),
        name=f"last_{half}",
    )(*operands)


def cross_route(levels, upper=True):
    route = {level: (level + 1) % levels for level in range(levels)}
    chips = levels // 2
    if chips % 2 or chips < 4:
        return sorted(route.items())
    for chip in range(chips - 1, 1, -2):
        route[levels - 1 if chip == chips - 1 else 2 * chip] = 2 * (chip - 2) + 1
    route[2] = 0
    if not upper:
        route[0], route[2], route[4] = route[4], route[0], 0
    return sorted(route.items())


def local(
    extrapolation_operator,
    impedance_contrast,
    ascending_residual,
    arriving_downward_matrices,
    shot_node_indices,
    emitted_pulse,
):
    levels = lax.axis_size("depth")
    freqs = lax.axis_size("freq")
    shots = arriving_downward_matrices.shape[3]
    mate_route = [(level, level ^ 1) for level in range(levels)]
    down_route = cross_route(levels)
    other_route = cross_route(levels, False)
    shared = (ascending_residual, impedance_contrast, shot_node_indices, emitted_pulse[0].T)

    def mate(pieces):
        return [lax.ppermute(piece, "depth", mate_route) for piece in pieces]

    def down(piece, other=False):
        return lax.ppermute(piece, "depth", other_route if other else down_route)

    rows = shots // HALVES
    start = (extrapolation_operator, impedance_contrast, ascending_residual, arriving_downward_matrices)
    results = first(1, *start, ())
    above = [down(piece) for piece in results[:HALVES]]
    *even, high, low, grad = first(0, *start, results[HALVES:])
    beside = [mate(even[2 * half : 2 * half + 2]) for half in range(HALVES)]
    grads = [grad]

    def odd_step(tick, start, pieces, other=False):
        odd, grads[0] = step(tick, start, 1, pieces, shared, high, low, grads[0], rows)
        return down(odd, other)

    def even_step(tick, start, pieces):
        *even, grads[0] = step(tick, start, 0, pieces, shared, high, low, grads[0], rows)
        return mate(even)

    later, latest = [], []
    for half in range(HALVES):
        later.append(odd_step(1, half * rows, beside[half]))
        latest.append(even_step(1, half * rows, [above[half]]))
    above, beside = later, latest
    for tick in range(2, TICKS - 1):
        later = [
            odd_step(tick, half * rows, beside[half], tick == TICKS - 2 and half == HALVES - 1) for half in range(HALVES)
        ]
        beside = [even_step(tick, half * rows, [above[half]]) for half in range(HALVES)]
        above = later

    scale = 1.0 / math.sqrt(shots * TICKS)
    held, grad = last(0, above[0], beside[0], shared, high, low, grads[0], None)
    chunks = gradient_chunks(above[1], beside[1], shared, grad, scale)
    gradient = chunks[0]
    for distance in range(1, freqs):
        route = [(i, (i + distance) % freqs) for i in range(freqs)]
        gradient = gradient + lax.ppermute(chunks[distance], "freq", route)
    (out,) = last(1, above[1], beside[1], shared, high, low, None, held)
    return (out[None, None], gradient)


def solution(mesh):
    placed = (
        P("freq", "depth", None, None, None),
        P("depth", None),
        P("freq", "depth", None, None, None, None),
        P("freq", "depth", None, None, None),
        P(),
        P("freq", None, None),
    )
    return jax.shard_map(
        local,
        mesh=mesh,
        in_specs=placed,
        out_specs=(P("freq", "depth", None, None, None), P("depth", "freq")),
        check_vma=False,
    )
```
